32 devices in a mesh: section: 2 (over core), seq: 4 (over z), dp: 4 (over y, x).
Axes of the slice: x: 2, y: 2, z: 4, core: 2. Of those that a mesh axis runs over, the one named last changes fastest.
Arguments:
- hidden_in: bfloat16 [8, 1024, 1536], P('dp', 'seq'), may hold values from -6 to 6
- doc_starts: int32 [8, 4], P('dp'), may hold values from 0 to 1023, as said below
- cotangent: bfloat16 [8, 1024, 1536], P('dp', 'seq'), may hold values from -6 to 6
- norm_gain: bfloat16 [2, 1536], P('section', 'seq'), may hold values from 0.5 to 1.5
- in_weight: bfloat16 [2, 1536, 6448], P('section', 'seq'), may hold values from -0.15625 to 0.15625
- conv_weight: bfloat16 [2, 4, 3328], P('section', None, 'seq'), may hold values from -3 to 3
- conv_bias: bfloat16 [2, 3328], P('section', 'seq'), may hold values from -3 to 3
- step_bias: bfloat16 [2, 48], P('section', 'seq'), may hold values from -6 to -2
- decay_log: bfloat16 [2, 48], P('section', 'seq'), may hold values from -5 to 2
- skip_gain: bfloat16 [2, 48], P('section', 'seq'), may hold values from 0.099609375 to 1.8984375
- gate_gain: bfloat16 [2, 3072], P('section', 'seq'), may hold values from 0.5 to 1.5
- out_weight: bfloat16 [2, 3072, 1536], P('section', 'seq'), may hold values from -0.109375 to 0.109375
Outputs:
- layer_out: bfloat16 [2, 8, 1024, 1536], P('section', 'dp', 'seq')
- input_grads: float32 [2, 8, 1024, 1536], P('section', 'dp', 'seq')
- grad_norm_gain: float32 [2, 1536], P('section', 'seq')
- grad_in_weight: float32 [2, 1536, 6448], P('section', 'seq')
- grad_conv_weight: float32 [2, 4, 3328], P('section', None, 'seq')
- grad_conv_bias: float32 [2, 3328], P('section', 'seq')
- grad_step_bias: float32 [2, 48], P('section', 'seq')
- grad_decay_log: float32 [2, 48], P('section', 'seq')
- grad_skip_gain: float32 [2, 48], P('section', 'seq')
- grad_gate_gain: float32 [2, 3072], P('section', 'seq')
- grad_out_weight: float32 [2, 3072, 1536], P('section', 'seq')
The draws below stay inside these ranges and needn't reach their ends.
Inputs may be any that keep to these rules, and one draw needn't show every extreme that they name: `doc_starts`: entries are positions within a stream. Among the 2 streams of each index of dp, one drawn from the seed has all entries 0 (a single document); every other stream has entry 0 equal to 0.
All inputs are finite; a program needn't handle non-finite values.
Results may differ from the reference program's by a relative error of at most 0.04.
Values may be sent and summed in bfloat16 or wider, within the bound.
A program may use at most 320 MiB of HBM per device.

```python
import jax
import jax.numpy as jnp
from jax import lax

D = 1536
HEADS = 48
CONV = 4
SPAN = 256
MB = 2
DOCS = 4
INNER = 3072
PROJ_WIDTH = 6448
CONV_CHANNELS = 3328
LENGTH = 1024
BATCH = 8


def draw_doc_starts(key, part):
    key = jax.random.fold_in(key, 7)
    pick_key, start_key = jax.random.split(key)
    chosen = jax.random.randint(pick_key, (BATCH // MB,), 0, MB)
    stream_rows = jnp.arange(BATCH)
    single = stream_rows % MB == chosen[stream_rows // MB]
    starts = jax.random.randint(start_key, (BATCH, DOCS), 1, LENGTH)
    starts = starts.at[:, 0].set(0)
    return jnp.where(single[:, None], 0, starts).astype(jnp.int32)


def level_of(rng, shape, cuts, smallest, top_value):
    def one(axis_at, shards_of):
        heights = jax.random.uniform(jax.random.fold_in(jax.random.fold_in(rng, 6), axis_at), (shards_of,), jnp.float32, smallest / len(cuts), top_value / len(cuts))
        return jnp.repeat(jnp.exp(heights), shape[axis_at] // shards_of).reshape((-1,) + (1,) * (len(shape) - axis_at - 1))

    loudness = one(*cuts[0])
    for cut in cuts[1:]:
        loudness = loudness * one(*cut)
    return loudness


def bell_draw(stream_key, dims, width, bound, pieces=(), kind=jnp.bfloat16):
    gain = level_of(stream_key, dims, pieces, -0.22, 0.18) if pieces else 1.0
    values = jax.random.normal(stream_key, dims, jnp.float32) * width * gain
    return jnp.minimum(jnp.maximum(values, -bound), bound).astype(kind)


def setup_inputs(seed: int = 0) -> dict:
    key_of = jax.random.split(jax.random.key(seed), 13)
    hidden_in = bell_draw(key_of[0], (BATCH, LENGTH, D), 1.0, 6.0, ((0, 4), (1, 4)))
    doc_starts = draw_doc_starts(jax.random.fold_in(key_of[12], 71), 0)
    cotangent = bell_draw(key_of[2], (BATCH, LENGTH, D), 1.0, 6.0, ((0, 4), (1, 4)))
    norm_gain = jnp.clip(1.0 + 0.1 * jax.random.normal(key_of[3], (2, D), jnp.float32), 0.5, 1.5).astype(jnp.bfloat16)
    in_weight = bell_draw(key_of[4], (2, D, PROJ_WIDTH), D ** -0.5, 0.15625, ((0, 2), (1, 4)))
    conv_weight = bell_draw(key_of[5], (2, CONV, CONV_CHANNELS), CONV ** -0.5, 3.0, ((0, 2), (2, 4)))
    conv_bias = bell_draw(key_of[6], (2, CONV_CHANNELS), 0.5, 3.0, ((0, 2), (1, 4)))
    step_bias = jnp.clip(-6.0 + 4.0 * jax.random.uniform(key_of[7], (2, HEADS), jnp.float32) ** level_of(key_of[7], (2, HEADS), ((0, 2), (1, 4)), -0.2, 0.2), -6.0, -2.0).astype(jnp.bfloat16)
    decay_log = jnp.clip(-5.0 + 7.0 * jax.random.uniform(key_of[8], (2, HEADS), jnp.float32) ** level_of(key_of[8], (2, HEADS), ((0, 2), (1, 4)), -0.2, 0.2), -5.0, 2.0).astype(jnp.bfloat16)
    skip_gain = jnp.clip(1.0 + 0.18 * jax.random.normal(key_of[9], (2, HEADS), jnp.float32), 0.099609375, 1.8984375).astype(jnp.bfloat16)
    gate_gain = jnp.clip(1.0 + 0.1 * jax.random.normal(key_of[10], (2, INNER), jnp.float32), 0.5, 1.5).astype(jnp.bfloat16)
    out_weight = bell_draw(key_of[11], (2, INNER, D), INNER ** -0.5, 0.109375, ((0, 2), (1, 4)))
    return dict(hidden_in=hidden_in, doc_starts=doc_starts, cotangent=cotangent, norm_gain=norm_gain, in_weight=in_weight, conv_weight=conv_weight, conv_bias=conv_bias, step_bias=step_bias, decay_log=decay_log, skip_gain=skip_gain, gate_gain=gate_gain, out_weight=out_weight)


EPSILON = 1e-05
HIGHEST = lax.Precision.HIGHEST

@jax.custom_vjp
def low(v):
    return lax.optimization_barrier(v.astype(jnp.bfloat16)).astype(jnp.float32)

@jax.custom_vjp
def low_back(v):
    return v

def low_keep(v):
    return (low(v), None)

def low_pass(kept, grad):
    return (grad,)

def back_keep(v):
    return (v, None)

def back_low(kept, grad):
    return (low(grad),)
low.defvjp(low_keep, low_pass)
low_back.defvjp(back_keep, back_low)

def norm_rows(rows_in, gain_vec):
    return rows_in * lax.rsqrt(lax.optimization_barrier(jnp.mean(rows_in * rows_in, axis=-1, keepdims=True)) + EPSILON) * gain_vec

def gate_norm(mixed_rows, gate_in, gain_vec):
    return norm_rows(mixed_rows * jax.nn.silu(gate_in), gain_vec)

def causal_conv(signal, kernel, offset, segment_ids):
    tap_count = kernel.shape[0]
    summed = signal * kernel[tap_count - 1] + offset
    for lag_size in range(1, tap_count):
        shifted = jnp.pad(signal, ((lag_size, 0), (0, 0)))[:-lag_size]
        shifted_ids = jnp.pad(segment_ids, (lag_size, 0), constant_values=-1)[:-lag_size]
        same_doc = (shifted_ids == segment_ids).astype(signal.dtype)
        summed = summed + shifted * same_doc[:, None] * kernel[tap_count - 1 - lag_size]
    return summed

def ssd_scan(values, deltas, log_rates, b_rows, c_rows, segment_ids):
    length, n_heads, head_width = values.shape
    blocks = length // SPAN
    float_kind = values.dtype
    indices = jnp.arange(SPAN)
    causal = indices[:, None] >= indices[None, :]
    inputs = (values.reshape(blocks, SPAN, n_heads, head_width), deltas.reshape(blocks, SPAN, n_heads), log_rates.reshape(blocks, SPAN, n_heads), b_rows.reshape(blocks, SPAN, -1), c_rows.reshape(blocks, SPAN, -1), segment_ids.astype(jnp.int32).reshape(blocks, SPAN))

    def advance(state_pair, block_in):
        memory, last_id = state_pair
        block_vals, block_deltas, block_rates, block_b, block_c, block_ids = block_in
        cumulative = jnp.cumsum(block_rates, axis=0)
        same_doc = causal & (block_ids[:, None] == block_ids[None, :])
        doc_mask = same_doc.astype(float_kind)[:, :, None]
        decay_mat = jnp.exp(jnp.where(same_doc[:, :, None], cumulative[:, None, :] - cumulative[None, :, :], 0.0)) * doc_mask
        scores = jnp.dot(block_c, block_b.T, precision=HIGHEST)
        mix_weights = scores[:, :, None] * decay_mat * block_deltas[None, :, :]
        local_out = jnp.einsum('ijh,jhp->ihp', mix_weights, block_vals, precision=HIGHEST)
        carried = (block_ids == last_id).astype(float_kind)
        from_memory = jnp.einsum('in,hpn->ihp', block_c, memory, precision=HIGHEST) * (carried[:, None] * jnp.exp(cumulative))[:, :, None]
        to_end = (block_ids == block_ids[-1]).astype(float_kind)[:, None] * jnp.exp(cumulative[-1][None, :] - cumulative) * block_deltas
        fresh_state = jnp.einsum('jh,jhp,jn->hpn', to_end, block_vals, block_b, precision=HIGHEST)
        memory = memory * (carried[-1] * jnp.exp(cumulative[-1]))[:, None, None] + fresh_state
        return ((memory, block_ids[-1].astype(jnp.int32)), local_out + from_memory)
    initial = (jnp.zeros((n_heads, head_width, b_rows.shape[1]), float_kind), jnp.array(-1, dtype=jnp.int32))
    _, outputs = lax.scan(jax.checkpoint(advance), initial, inputs)
    return outputs.reshape(length, n_heads, head_width)

def mix_heads(proj_x, proj_dt, proj_bc, kernel, offset, dt_offset, rate_log, skip_part, segment_ids):
    channels = proj_x.shape[1]
    n_heads = proj_dt.shape[1]
    n_state = proj_bc.shape[1] // 2
    length = proj_x.shape[0]
    activated = jax.nn.silu(causal_conv(jnp.concatenate([proj_x, proj_bc], axis=1), kernel, offset, segment_ids))
    values = activated[:, :channels].reshape(length, n_heads, channels // n_heads)
    b_rows = activated[:, channels:channels + n_state]
    c_rows = activated[:, channels + n_state:]
    deltas = jax.nn.softplus(proj_dt + dt_offset)
    log_rates = -jnp.exp(rate_log) * deltas
    scanned = ssd_scan(values, deltas, log_rates, b_rows, c_rows, segment_ids) + skip_part[None, :, None] * values
    return scanned.reshape(length, channels)

def mamba_layer(stream_in, weights, segment_ids):
    norm_gain, in_weight, conv_weight, conv_bias, step_bias, decay_log, skip_gain, gate_gain, out_weight = weights
    inner_width = out_weight.shape[0]
    n_heads = step_bias.shape[0]
    normed = low(norm_rows(stream_in, norm_gain))
    projected = low_back(low(jnp.dot(normed, in_weight, precision=HIGHEST)))
    total_width = projected.shape[1]
    gate_in = projected[:, :inner_width]
    proj_x = projected[:, inner_width:2 * inner_width]
    proj_bc = projected[:, 2 * inner_width:total_width - n_heads]
    proj_dt = projected[:, total_width - n_heads:]
    mixed_rows = low_back(low(mix_heads(proj_x, proj_dt, proj_bc, conv_weight, conv_bias, step_bias, decay_log, skip_gain, segment_ids)))
    gated_rows = low(gate_norm(mixed_rows, gate_in, gate_gain))
    return stream_in + low_back(jnp.dot(gated_rows, out_weight, precision=HIGHEST))

def reference(hidden_in, doc_starts, cotangent, norm_gain, in_weight, conv_weight, conv_bias, step_bias, decay_log, skip_gain, gate_gain, out_weight):
    stacked = (norm_gain, in_weight, conv_weight, conv_bias, step_bias, decay_log, skip_gain, gate_gain, out_weight)
    first_layer = tuple((weight_arr[0].astype(jnp.float32) for weight_arr in stacked))
    second_layer = tuple((weight_arr[1].astype(jnp.float32) for weight_arr in stacked))
    positions = jnp.arange(LENGTH, dtype=jnp.int32)

    def one_stream(totals, item_in):
        stream, starts, outer_grad = item_in
        segment_ids = lax.optimization_barrier(jnp.sum((starts.astype(jnp.int32)[:, None] <= positions[None, :]).astype(jnp.int32), axis=0, dtype=jnp.int32))

        def run_layer(stream_in, weights):
            return mamba_layer(stream_in, weights, segment_ids)
        hidden_first, pull_first = jax.vjp(run_layer, stream.astype(jnp.float32), first_layer)
        hidden_low = hidden_first.astype(jnp.bfloat16)
        hidden_second, pull_second = jax.vjp(run_layer, hidden_low.astype(jnp.float32), second_layer)
        grad_mid, grads_second = pull_second(outer_grad.astype(jnp.float32))
        grad_first, grads_first = pull_first(low(grad_mid))
        totals = (jax.tree.map(jnp.add, totals[0], grads_first), jax.tree.map(jnp.add, totals[1], grads_second))
        return (totals, (hidden_low, hidden_second.astype(jnp.bfloat16), grad_first, grad_mid))
    zero_grads = jax.tree.map(jnp.zeros_like, first_layer)
    totals, (first_out, second_out, first_grad, mid_grad) = lax.scan(one_stream, (zero_grads, zero_grads), (hidden_in, doc_starts, cotangent))
    grads = [jnp.stack([first_part, second_part]) for first_part, second_part in zip(totals[0], totals[1])]
    return (jnp.stack([first_out, second_out]), jnp.stack([first_grad, mid_grad]), grads[0], grads[1], grads[2], grads[3], grads[4], grads[5], grads[6], grads[7], grads[8])
```

```python
import functools

import jax
import jax.numpy as jnp
from jax import lax
from jax.experimental import pallas as pl
from jax.experimental.pallas import tpu as pltpu
from jax.sharding import PartitionSpec as P

SPAN = 256
HEAD = 64
STATE = 128
TAPS = 4
EPSILON = 1e-05
HIGHEST = lax.Precision.HIGHEST
F32 = jnp.float32
BF16 = jnp.bfloat16
FAR = -1e30


def mm(a, b):
    return jnp.dot(a, b, preferred_element_type=F32)


def mm_nt(a, b):
    return lax.dot_general(a, b, (((1,), (1,)), ((), ())), preferred_element_type=F32)


def mm_tn(a, b):
    return lax.dot_general(a, b, (((0,), (0,)), ((), ())), preferred_element_type=F32)


def exact(a, b):
    return lax.dot_general(
        a, b, (((1,), (0,)), ((), ())), precision=HIGHEST, preferred_element_type=F32
    )


def doc_of(starts_ref, position):
    total = jnp.zeros(position.shape, jnp.int32)
    for entry in range(starts_ref.shape[0]):
        total = total + (starts_ref[entry] <= position).astype(jnp.int32)
    return total


def tiles_of(width):
    return [(low, min(low + 128, width)) for low in range(0, width, 128)]


def spread_pair(columns, tile, width):
    rows = columns.shape[0]
    first = jnp.broadcast_to(columns[:, 2 * tile : 2 * tile + 1], (rows, width))
    if width <= HEAD:
        return first
    second = jnp.broadcast_to(columns[:, 2 * tile + 1 : 2 * tile + 2], (rows, width))
    lane = lax.broadcasted_iota(jnp.int32, (rows, width), 1)
    return jnp.where(lane < HEAD, first, second)


def block_facts(starts_ref, block, length):
    base = block * SPAN
    column = base + lax.broadcasted_iota(jnp.int32, (SPAN, 128), 0)
    doc_col = doc_of(starts_ref, column)
    before = []
    for lag in range(1, TAPS):
        same = (doc_of(starts_ref, column - lag) == doc_col) & (column >= lag)
        before.append(same.astype(F32))
    row = base + lax.broadcasted_iota(jnp.int32, (8, SPAN), 1)
    doc_row = doc_of(starts_ref, row)
    same_square = doc_col[:, 0:1] == doc_row[0:1, :]
    edge_before = jnp.full((8, 128), base - 1, jnp.int32)
    last_doc_before = doc_of(starts_ref, edge_before)[0:1, :]
    last_doc = doc_of(starts_ref, jnp.full((8, 128), base + SPAN - 1, jnp.int32))[0:1, :]
    carried = ((doc_col == last_doc_before) & (base > 0)).astype(F32)
    to_last = (doc_col == last_doc).astype(F32)
    return doc_col, column, before, same_square, carried, to_last


def taps_sum(ext_ref, low, high, before, kernel, bias):
    summed = ext_ref[pl.ds(8, SPAN), low:high] * kernel[TAPS - 1 : TAPS, low:high] + bias[0:1, low:high]
    for lag in range(1, TAPS):
        summed = summed + (
            ext_ref[pl.ds(8 - lag, SPAN), low:high]
            * before[lag - 1][:, : high - low]
            * kernel[TAPS - 1 - lag : TAPS - lag, low:high]
        )
    return summed


def sigmoid(value):
    return 1.0 / (1.0 + jnp.exp(-value))


def softplus(value):
    small = jnp.exp(-jnp.abs(value))
    series = small * (1.0 - small * (0.5 - small * (1.0 / 3.0)))
    return jnp.maximum(value, 0.0) + jnp.where(small < 0.01, series, jnp.log(1.0 + small))


def lower_ones():
    row = lax.broadcasted_iota(jnp.int32, (SPAN, SPAN), 0)
    col = lax.broadcasted_iota(jnp.int32, (SPAN, SPAN), 1)
    return row, col


def forward_kernel(
    with_back,
    length,
    starts_ref,
    normed_ref,
    wg_ref,
    wx_ref,
    wbc_ref,
    wdt_ref,
    kx_ref,
    kbc_ref,
    heads_ref,
    gain_ref,
    wo_ref,
    *rest,
):
    if with_back:
        dh_ref, rest = rest[0], rest[1:]
    (
        gate_ref,
        x_ref,
        bc_ref,
        dt_ref,
        scan_ref,
        state_ref,
        part_ref,
        stat_ref,
        ext_x,
        ext_bc,
        memory,
        gu_ref,
        y_ref,
    ) = rest
    block = pl.program_id(0)
    inner = wx_ref.shape[1]

    @pl.when(block == 0)
    def _():
        ext_x[...] = jnp.zeros_like(ext_x)
        ext_bc[...] = jnp.zeros_like(ext_bc)
        memory[...] = jnp.zeros_like(memory)

    @pl.when(block > 0)
    def _():
        ext_x[0:8, :] = ext_x[SPAN : SPAN + 8, :]
        ext_bc[0:8, :] = ext_bc[SPAN : SPAN + 8, :]

    normed = normed_ref[...]
    bc_low = mm(normed, wbc_ref[...]).astype(BF16)
    bc_ref[...] = bc_low
    ext_bc[8 : SPAN + 8, :] = bc_low.astype(F32)
    dt_low = mm(normed, wdt_ref[...]).astype(BF16).astype(F32)
    dt_ref[...] = dt_low
    x_low = mm(normed, wx_ref[...]).astype(BF16)
    x_ref[...] = x_low
    ext_x[8 : SPAN + 8, :] = x_low.astype(F32)
    gate_low = mm(normed, wg_ref[...]).astype(BF16)
    gate_ref[...] = gate_low

    _, _, before, same_square, carried, to_last = block_facts(starts_ref, block, length)
    row, col = lower_ones()
    lower = (row >= col).astype(F32)
    keep = jnp.where(same_square & (row >= col), 0.0, FAR)

    delta = softplus(dt_low + heads_ref[0:1, :])
    rate = -jnp.exp(heads_ref[1:2, :]) * delta
    total = exact(lower, rate)
    total_rows = jnp.transpose(total)
    grown = carried * jnp.exp(total)
    last_total = total[SPAN - 1 : SPAN, :]
    ending = to_last * jnp.exp(last_total - total)
    carry_last = grown[SPAN - 1 : SPAN, :]

    kbc = kbc_ref[...]
    b_conv = taps_sum(ext_bc, 0, STATE, before, kbc, kbc[TAPS : TAPS + 1])
    c_conv = taps_sum(ext_bc, STATE, 2 * STATE, before, kbc, kbc[TAPS : TAPS + 1])
    b_low = (b_conv * sigmoid(b_conv)).astype(BF16)
    c_low = (c_conv * sigmoid(c_conv)).astype(BF16)
    scores = mm_nt(c_low, b_low)
    b_flip = jnp.transpose(b_low.astype(F32)).astype(BF16)

    state_ref[0] = memory[...].astype(BF16)
    kx = kx_ref[...]
    squares = jnp.zeros((SPAN, 128), F32)
    for tile, (low, high) in enumerate(tiles_of(inner)):
        width = high - low
        lane = lax.broadcasted_iota(jnp.int32, (SPAN, width), 1)
        conv = taps_sum(ext_x, low, high, before, kx, kx[TAPS : TAPS + 1])
        values = conv * sigmoid(conv)
        weighted = spread_pair(delta, tile, width) * values
        w_low = weighted.astype(BF16)
        mixed = None
        for half in range(width // HEAD):
            head = 2 * tile + half
            decay = jnp.exp(total[:, head : head + 1] - total_rows[head : head + 1, :] + keep)
            part = mm((scores * decay).astype(BF16), w_low)
            mixed = part if mixed is None else jnp.where(lane < HEAD, mixed, part)
        mem = memory[:, low:high]
        mixed = mixed + mm(c_low, mem.astype(BF16)) * spread_pair(grown, tile, width)
        scan_ref[:, low:high] = mixed
        fresh = mm(b_flip, (weighted * spread_pair(ending, tile, width)).astype(BF16))
        memory[:, low:high] = mem * spread_pair(carry_last, tile, width) + fresh
        mixed = (
            (mixed + spread_pair(heads_ref[2:3, :], tile, width) * values).astype(BF16).astype(F32)
        )
        gate = gate_ref[:, low:high].astype(F32)
        g = mixed * (gate * sigmoid(gate))
        if width == 128:
            squares = squares + g * g
        else:
            squares = squares + jnp.concatenate([g * g, jnp.zeros((SPAN, 128 - width), F32)], axis=1)
        gu_ref[:, low:high] = (g * gain_ref[0:1, low:high]).astype(BF16)

    stats = jnp.sum(squares, axis=1, keepdims=True)
    gu = gu_ref[...]
    part_ref[...] = mm(gu, wo_ref[...]).astype(BF16)
    if with_back:
        dgated = mm_nt(dh_ref[...], wo_ref[...])
        along = jnp.sum(dgated * gu.astype(F32), axis=1, keepdims=True)
        lane = lax.broadcasted_iota(jnp.int32, (SPAN, 128), 1)
        both = jnp.where(lane == 0, stats, jnp.where(lane == 1, along, 0.0))
    else:
        both = jnp.broadcast_to(stats, (SPAN, 128))
    stat_ref[...] = jnp.transpose(both)[0:8, :]


def backward_kernel(
    length,
    starts_ref,
    dh_ref,
    stat_ref,
    wg_ref,
    wx_ref,
    wbc_ref,
    wdt_ref,
    kx_ref,
    kbc_ref,
    heads_ref,
    gain_ref,
    wo_ref,
    gate_ref,
    x_ref,
    xh_ref,
    bc_ref,
    bch_ref,
    dt_ref,
    scan_ref,
    state_ref,
    dgate_ref,
    dx_ref,
    dbc_ref,
    ddt_ref,
    gated_ref,
    dnormed_ref,
    gx_ref,
    gbc_ref,
    gheads_ref,
    ext_x,
    ext_bc,
    ext_dx,
    ext_dbc,
    dmemory,
    dscore,
):
    blocks = pl.num_programs(0)
    block = blocks - 1 - pl.program_id(0)
    inner = wx_ref.shape[1]

    @pl.when(pl.program_id(0) == 0)
    def _():
        ext_dx[...] = jnp.zeros_like(ext_dx)
        ext_dbc[...] = jnp.zeros_like(ext_dbc)
        dmemory[...] = jnp.zeros_like(dmemory)
        gx_ref[...] = jnp.zeros_like(gx_ref)
        gbc_ref[...] = jnp.zeros_like(gbc_ref)
        gheads_ref[...] = jnp.zeros_like(gheads_ref)

    @pl.when(pl.program_id(0) > 0)
    def _():
        ext_dx[SPAN : SPAN + 8, :] = ext_dx[0:8, :]
        ext_dbc[SPAN : SPAN + 8, :] = ext_dbc[0:8, :]

    ext_x[0:8, :] = xh_ref[8:16, :].astype(F32)
    ext_x[8 : SPAN + 8, :] = x_ref[...].astype(F32)
    ext_bc[0:8, :] = bch_ref[8:16, :].astype(F32)
    ext_bc[8 : SPAN + 8, :] = bc_ref[...].astype(F32)

    doc_col, column, before, same_square, carried, to_last = block_facts(starts_ref, block, length)
    after = []
    for lag in range(1, TAPS):
        same = (doc_of(starts_ref, column + lag) == doc_col) & (column + lag < length)
        after.append(same.astype(F32))
    row, col = lower_ones()
    lower = (row >= col).astype(F32)
    upper = (row <= col).astype(F32)
    keep = jnp.where(same_square & (row <= col), 0.0, FAR)

    dt = dt_ref[...] + heads_ref[0:1, :]
    delta = softplus(dt)
    slope = -jnp.exp(heads_ref[1:2, :])
    rate = slope * delta
    total = exact(lower, rate)
    total_rows = jnp.transpose(total)
    grown = carried * jnp.exp(total)
    last_total = total[SPAN - 1 : SPAN, :]
    ending = to_last * jnp.exp(last_total - total)
    carry_last = grown[SPAN - 1 : SPAN, :]

    kbc = kbc_ref[...]
    b_conv = taps_sum(ext_bc, 0, STATE, before, kbc, kbc[TAPS : TAPS + 1])
    c_conv = taps_sum(ext_bc, STATE, 2 * STATE, before, kbc, kbc[TAPS : TAPS + 1])
    b_sig = sigmoid(b_conv)
    c_sig = sigmoid(c_conv)
    b_low = (b_conv * b_sig).astype(BF16)
    c_low = (c_conv * c_sig).astype(BF16)
    scores = mm_nt(b_low, c_low)
    c_flip = jnp.transpose(c_low.astype(F32)).astype(BF16)

    stat_cols = jnp.transpose(jnp.broadcast_to(stat_ref[0:1, :], (128, SPAN)))
    mean_cols = jnp.transpose(jnp.broadcast_to(stat_ref[1:2, :], (128, SPAN)))
    dgated = mm_nt(dh_ref[...], wo_ref[...])
    dscore[...] = jnp.zeros_like(dscore)
    kx = kx_ref[...]
    db = jnp.zeros((SPAN, STATE), F32)
    dc = jnp.zeros((SPAN, STATE), F32)
    dtotal = jnp.zeros((SPAN, 128), F32)
    ddelta = jnp.zeros((SPAN, 128), F32)
    dlast = jnp.zeros((8, 128), F32)
    for tile, (low, high) in enumerate(tiles_of(inner)):
        width = high - low
        lane = lax.broadcasted_iota(jnp.int32, (SPAN, width), 1)
        picker = (
            lax.broadcasted_iota(jnp.int32, (width, 128), 1)
            == 2 * tile + lax.broadcasted_iota(jnp.int32, (width, 128), 0) // HEAD
        ).astype(F32)
        skip = spread_pair(heads_ref[2:3, :], tile, width)
        conv = taps_sum(ext_x, low, high, before, kx, kx[TAPS : TAPS + 1])
        sig = sigmoid(conv)
        values = conv * sig
        delta_t = spread_pair(delta, tile, width)
        weighted = delta_t * values
        w_low = weighted.astype(BF16)
        scanned = scan_ref[:, low:high]
        mixed = (scanned + skip * values).astype(BF16).astype(F32)
        gate = gate_ref[:, low:high].astype(F32)
        gate_sig = sigmoid(gate)
        silu = gate * gate_sig
        g = mixed * silu
        scale = stat_cols[:, :width]
        n = g * scale
        gain = gain_ref[0:1, low:high]
        dgated_t = dgated[:, low:high]
        gated_ref[:, low:high] = (n * gain).astype(BF16)
        dg = scale * (dgated_t * gain - n * mean_cols[:, :width])
        dgate_ref[:, low:high] = (
            dg * mixed * (gate_sig * (1.0 + gate * (1.0 - gate_sig)))
        ).astype(BF16)
        dy_low = (dg * silu).astype(BF16)
        dy = dy_low.astype(F32)
        grad_w = None
        for half in range(width // HEAD):
            head = 2 * tile + half
            decay = jnp.exp(total_rows[head : head + 1, :] - total[:, head : head + 1] + keep)
            mine = (lane // HEAD) == half
            pairs = mm_nt(jnp.where(mine, w_low, jnp.zeros_like(w_low)), dy_low)
            dscore[...] += decay * pairs
            part = mm((scores * decay).astype(BF16), dy_low)
            grad_w = part if grad_w is None else jnp.where(lane < HEAD, grad_w, part)
        dmem = dmemory[:, low:high]
        dmem_low = dmem.astype(BF16)
        mem_low = state_ref[0, :, low:high]
        ending_t = spread_pair(ending, tile, width)
        from_state = mm(b_low, dmem_low) * ending_t
        grad_w = grad_w + from_state
        db = db + mm_nt((weighted * ending_t).astype(BF16), dmem_low)
        dy_grown = (dy * spread_pair(grown, tile, width)).astype(BF16)
        dc = dc + mm_nt(dy_grown, mem_low)
        carry_t = spread_pair(carry_last, tile, width)
        w_round = w_low.astype(F32)
        at_last = jnp.sum(w_round * from_state, axis=0, keepdims=True) + jnp.sum(
            dmem * mem_low.astype(F32) * carry_t, axis=0, keepdims=True
        )
        dlast = dlast + exact(jnp.broadcast_to(at_last, (8, width)), picker)
        dmemory[:, low:high] = dmem * carry_t + mm(c_flip, dy_grown)
        dtotal = dtotal + exact(dy * scanned - w_round * grad_w, picker)
        ddelta = ddelta + exact(values * grad_w, picker)
        dconv = (delta_t * grad_w + skip * dy) * (sig * (1.0 + conv * (1.0 - sig)))
        ext_dx[0:SPAN, low:high] = dconv
        sums = [jnp.sum(dconv * ext_x[pl.ds(8, SPAN), low:high], axis=0, keepdims=True)]
        for lag in range(1, TAPS):
            sums.append(
                jnp.sum(
                    dconv * before[lag - 1][:, :width] * ext_x[pl.ds(8 - lag, SPAN), low:high],
                    axis=0,
                    keepdims=True,
                )
            )
        sums = sums[::-1] + [
            jnp.sum(dconv, axis=0, keepdims=True),
            jnp.sum(dy * values, axis=0, keepdims=True),
            jnp.sum(dgated_t * n, axis=0, keepdims=True),
            jnp.zeros((1, width), F32),
        ]
        gx_ref[:, low:high] += jnp.concatenate(sums, axis=0)
        back = ext_dx[0:SPAN, low:high] * kx[TAPS - 1 : TAPS, low:high]
        for lag in range(1, TAPS):
            back = back + (
                ext_dx[pl.ds(lag, SPAN), low:high]
                * after[lag - 1][:, :width]
                * kx[TAPS - 1 - lag : TAPS - lag, low:high]
            )
        dx_ref[:, low:high] = back.astype(BF16)

    score_grad = dscore[...]
    db = db + mm(score_grad.astype(BF16), c_low)
    dc = dc + mm(jnp.transpose(score_grad).astype(BF16), b_low)
    for part, (conv, sig, grad) in enumerate(((b_conv, b_sig, db), (c_conv, c_sig, dc))):
        low, high = part * STATE, (part + 1) * STATE
        dconv = grad * (sig * (1.0 + conv * (1.0 - sig)))
        ext_dbc[0:SPAN, low:high] = dconv
        sums = [jnp.sum(dconv * ext_bc[pl.ds(8, SPAN), low:high], axis=0, keepdims=True)]
        for lag in range(1, TAPS):
            sums.append(
                jnp.sum(
                    dconv * before[lag - 1] * ext_bc[pl.ds(8 - lag, SPAN), low:high],
                    axis=0,
                    keepdims=True,
                )
            )
        sums = sums[::-1] + [jnp.sum(dconv, axis=0, keepdims=True), jnp.zeros((3, STATE), F32)]
        gbc_ref[:, low:high] += jnp.concatenate(sums, axis=0)
        back = dconv * kbc[TAPS - 1 : TAPS, low:high]
        for lag in range(1, TAPS):
            back = back + (
                ext_dbc[pl.ds(lag, SPAN), low:high]
                * after[lag - 1]
                * kbc[TAPS - 1 - lag : TAPS - lag, low:high]
            )
        dbc_ref[:, low:high] = back.astype(BF16)

    drate = exact(upper, dtotal) + dlast[0:1, :]
    ddt = (ddelta + slope * drate) * sigmoid(dt)
    ddt_low = ddt.astype(BF16)
    ddt_ref[...] = ddt_low
    gheads_ref[...] += jnp.concatenate(
        [
            jnp.sum(ddt, axis=0, keepdims=True),
            jnp.sum(drate * rate, axis=0, keepdims=True),
            jnp.zeros((6, 128), F32),
        ],
        axis=0,
    )
    dnormed_ref[...] = (
        mm_nt(dgate_ref[...], wg_ref[...])
        + mm_nt(dx_ref[...], wx_ref[...])
        + mm_nt(dbc_ref[...], wbc_ref[...])
        + mm_nt(ddt_low, wdt_ref[...])
    ).astype(BF16)


def whole(array):
    return pl.BlockSpec(array.shape, lambda i: (0,) * array.ndim, pipeline_mode=pl.Buffered(1))


def cost(length, width, inner, passes):
    flops = 2 * length * width * (3 * inner + 384) * passes
    return pl.CostEstimate(flops=flops, bytes_accessed=length * width * 16, transcendentals=0)


VMEM_LIMIT = 48 * 2**20


def run_forward(starts, normed, weights, dh=None):
    wg, wx, wbc, wdt, kx, kbc, heads, gain, wo = weights
    length, width = normed.shape
    inner = wx.shape[1]
    blocks = length // SPAN
    rows = lambda cols: pl.BlockSpec((SPAN, cols), lambda i: (i, 0))
    operands = [starts, normed, wg, wx, wbc, wdt, kx, kbc, heads, gain, wo]
    in_specs = [pl.BlockSpec(memory_space=pltpu.SMEM), rows(width)] + [
        whole(array) for array in operands[2:]
    ]
    if dh is not None:
        operands.append(dh)
        in_specs.append(rows(width))
    out_shape = [
        jax.ShapeDtypeStruct((length, inner), BF16),
        jax.ShapeDtypeStruct((length, inner), BF16),
        jax.ShapeDtypeStruct((length, 2 * STATE), BF16),
        jax.ShapeDtypeStruct((length, 128), F32),
        jax.ShapeDtypeStruct((length, inner), F32),
        jax.ShapeDtypeStruct((blocks, STATE, inner), BF16),
        jax.ShapeDtypeStruct((length, width), BF16),
        jax.ShapeDtypeStruct((8, length), F32),
    ]
    out_specs = [
        rows(inner),
        rows(inner),
        rows(2 * STATE),
        rows(128),
        rows(inner),
        pl.BlockSpec((1, STATE, inner), lambda i: (i, 0, 0)),
        rows(width),
        pl.BlockSpec((8, SPAN), lambda i: (0, i)),
    ]
    return pl.pallas_call(
        functools.partial(forward_kernel, dh is not None, length),
        grid=(blocks,),
        in_specs=in_specs,
        out_specs=out_specs,
        out_shape=out_shape,
        scratch_shapes=[
            pltpu.VMEM((SPAN + 8, inner), F32),
            pltpu.VMEM((SPAN + 8, 2 * STATE), F32),
            pltpu.VMEM((STATE, inner), F32),
            pltpu.VMEM((SPAN, inner), BF16),
            pltpu.VMEM((SPAN, inner), F32),
        ],
        compiler_params=pltpu.CompilerParams(
            dimension_semantics=("arbitrary",), vmem_limit_bytes=VMEM_LIMIT
        ),
        cost_estimate=cost(length, width, inner, 1),
        name="layer_forward",
    )(*operands)


def run_backward(starts, dh, stats, weights, saved):
    wg, wx, wbc, wdt, kx, kbc, heads, gain, wo = weights
    gate, x, bc, dt, scanned, states = saved
    length, width = dh.shape
    inner = wx.shape[1]
    blocks = length // SPAN
    rows = lambda cols: pl.BlockSpec((SPAN, cols), lambda i: (blocks - 1 - i, 0))
    halo = lambda cols: pl.BlockSpec(
        (16, cols), lambda i: (jnp.maximum((blocks - 1 - i) * (SPAN // 16) - 1, 0), 0)
    )
    fixed = lambda shape: pl.BlockSpec(shape, lambda i: (0,) * len(shape))
    operands = [starts, dh, stats, wg, wx, wbc, wdt, kx, kbc, heads, gain, wo]
    in_specs = [
        pl.BlockSpec(memory_space=pltpu.SMEM),
        rows(width),
        pl.BlockSpec((8, SPAN), lambda i: (0, blocks - 1 - i)),
    ] + [whole(array) for array in operands[3:]]
    operands += [gate, x, x, bc, bc, dt, scanned, states]
    in_specs += [
        rows(inner),
        rows(inner),
        halo(inner),
        rows(2 * STATE),
        halo(2 * STATE),
        rows(128),
        rows(inner),
        pl.BlockSpec((1, STATE, inner), lambda i: (blocks - 1 - i, 0, 0)),
    ]
    out_shape = [
        jax.ShapeDtypeStruct((length, inner), BF16),
        jax.ShapeDtypeStruct((length, inner), BF16),
        jax.ShapeDtypeStruct((length, 2 * STATE), BF16),
        jax.ShapeDtypeStruct((length, 128), BF16),
        jax.ShapeDtypeStruct((length, inner), BF16),
        jax.ShapeDtypeStruct((length, width), BF16),
        jax.ShapeDtypeStruct((8, inner), F32),
        jax.ShapeDtypeStruct((8, 2 * STATE), F32),
        jax.ShapeDtypeStruct((8, 128), F32),
    ]
    out_specs = [
        rows(inner),
        rows(inner),
        rows(2 * STATE),
        rows(128),
        rows(inner),
        rows(width),
        fixed((8, inner)),
        fixed((8, 2 * STATE)),
        fixed((8, 128)),
    ]
    return pl.pallas_call(
        functools.partial(backward_kernel, length),
        grid=(blocks,),
        in_specs=in_specs,
        out_specs=out_specs,
        out_shape=out_shape,
        scratch_shapes=[
            pltpu.VMEM((SPAN + 8, inner), F32),
            pltpu.VMEM((SPAN + 8, 2 * STATE), F32),
            pltpu.VMEM((SPAN + 8, inner), F32),
            pltpu.VMEM((SPAN + 8, 2 * STATE), F32),
            pltpu.VMEM((STATE, inner), F32),
            pltpu.VMEM((SPAN, SPAN), F32),
        ],
        compiler_params=pltpu.CompilerParams(
            dimension_semantics=("arbitrary",), vmem_limit_bytes=VMEM_LIMIT
        ),
        cost_estimate=cost(length, width, inner, 2),
        name="layer_backward",
    )(*operands)


def norm_rows(rows_in, gain_vec):
    return (
        rows_in
        * lax.rsqrt(jnp.mean(rows_in * rows_in, axis=-1, keepdims=True) + EPSILON)
        * gain_vec
    )


def norm_back(rows_in, gain_vec, grad):
    inverse = lax.rsqrt(jnp.mean(rows_in * rows_in, axis=-1, keepdims=True) + EPSILON)
    unit = rows_in * inverse
    scaled = grad * gain_vec
    back = inverse * (scaled - unit * jnp.mean(scaled * unit, axis=-1, keepdims=True))
    return back, jnp.sum(grad * unit, axis=0)


def other_core(array):
    return lax.ppermute(array, "section", [(0, 1), (1, 0)])


def both_layers(array):
    core = lax.axis_index("section")
    theirs = other_core(array)
    return (
        jnp.where(core == 0, array, theirs),
        jnp.where(core == 0, theirs, array),
    )


def layer_weights(in_weight, conv_weight, conv_bias, step_bias, decay_log, skip_gain, gate_gain, out_weight, norm_gain):
    count = lax.axis_size("seq")
    rank = lax.axis_index("seq")
    inner = out_weight.shape[1]
    heads = step_bias.shape[1]
    whole_inner = inner * count
    depth = in_weight.shape[1]
    rows = in_weight[0]
    gate = rows[:, :whole_inner].reshape(depth, count, inner)
    x = rows[:, whole_inner : 2 * whole_inner].reshape(depth, count, inner)
    bc = rows[:, 2 * whole_inner : 2 * whole_inner + 2 * STATE]
    dt = rows[:, 2 * whole_inner + 2 * STATE :].reshape(depth, count, heads)
    bundle = jnp.concatenate(
        [
            gate,
            x,
            jnp.broadcast_to(bc[:, None, :], (depth, count, 2 * STATE)),
            jnp.pad(dt, ((0, 0), (0, 0), (0, 128 - heads))),
        ],
        axis=2,
    ).transpose(1, 0, 2)
    mine = lax.all_to_all(bundle, "seq", split_axis=0, concat_axis=0, tiled=True)
    mine = mine.reshape(count * depth, -1)
    in_both = both_layers(mine)
    out_both = both_layers(out_weight[0])
    small = jnp.concatenate(
        [
            conv_weight[0].reshape(-1),
            conv_bias[0],
            norm_gain[0],
        ]
    )
    gathered = lax.all_gather(small, "seq", axis=0)
    part = conv_bias.shape[1]
    kernel = gathered[:, : TAPS * part].reshape(count, TAPS, part).transpose(1, 0, 2).reshape(TAPS, -1)
    bias = gathered[:, TAPS * part : (TAPS + 1) * part].reshape(-1)
    gain = gathered[:, (TAPS + 1) * part :].reshape(-1)
    taps = jnp.concatenate([kernel, bias[None], jnp.zeros((3, bias.shape[0]), BF16)], axis=0)
    own = jnp.concatenate([step_bias, decay_log, skip_gain], axis=0)
    own = jnp.pad(own, ((0, 5), (0, 128 - heads)))
    packed = [
        lax.dynamic_slice_in_dim(taps, rank * inner, inner, 1).astype(F32),
        taps[:, whole_inner:].astype(F32),
        own.astype(F32),
        jnp.broadcast_to(gate_gain, (8, inner)).astype(F32),
        jnp.broadcast_to(gain[None], (8, gain.shape[0])).astype(F32),
    ]
    shared = [both_layers(array) for array in packed]
    layers = []
    for layer in range(2):
        w = in_both[layer]
        kx, kbc, head_rows, gain_rows, norm_gain_rows = (pair[layer] for pair in shared)
        layers.append(
            (
                (
                    w[:, :inner],
                    w[:, inner : 2 * inner],
                    w[:, 2 * inner : 2 * inner + 2 * STATE],
                    w[:, 2 * inner + 2 * STATE :],
                    kx,
                    kbc,
                    head_rows,
                    gain_rows,
                    out_both[layer],
                ),
                norm_gain_rows[0],
            )
        )
    return layers


def local(
    hidden_in,
    doc_starts,
    cotangent,
    norm_gain,
    in_weight,
    conv_weight,
    conv_bias,
    step_bias,
    decay_log,
    skip_gain,
    gate_gain,
    out_weight,
):
    core = lax.axis_index("section")
    rank = lax.axis_index("seq")
    count = lax.axis_size("seq")
    inner = out_weight.shape[1]
    heads = step_bias.shape[1]
    whole_inner = inner * count
    layers = layer_weights(
        in_weight, conv_weight, conv_bias, step_bias, decay_log, skip_gain, gate_gain, out_weight, norm_gain
    )
    stream = lax.dynamic_index_in_dim(hidden_in, core, 0, keepdims=False).astype(F32)
    outer = lax.dynamic_index_in_dim(cotangent, core, 0, keepdims=False)
    starts = lax.dynamic_index_in_dim(doc_starts, core, 0, keepdims=False)
    tokens = stream.shape[0]

    gather = lambda array: lax.all_gather(array, "seq", axis=0, tiled=True)
    scatter = lambda array: lax.psum_scatter(array, "seq", scatter_dimension=0, tiled=True)
    own_tokens = lambda row: lax.dynamic_slice_in_dim(row, rank * tokens, tokens, 0)

    dh_whole = gather(outer)
    normed_0 = gather(norm_rows(stream, layers[0][1]).astype(BF16))
    fwd_0 = run_forward(starts, normed_0, layers[0][0])
    square_0 = lax.psum(fwd_0[7][0], "seq")
    scale_0 = lax.rsqrt(square_0 / whole_inner + EPSILON)
    product_0 = scatter(fwd_0[6]).astype(F32) * own_tokens(scale_0)[:, None]
    hidden_1 = (stream + product_0).astype(BF16)
    stream_1 = hidden_1.astype(F32)
    normed_1 = gather(norm_rows(stream_1, layers[1][1]).astype(BF16))
    fwd_1 = run_forward(starts, normed_1, layers[1][0], dh_whole)
    sums_1 = lax.psum(fwd_1[7][:2], "seq")
    scale_1 = lax.rsqrt(sums_1[0] / whole_inner + EPSILON)
    stats_1 = jnp.concatenate(
        [scale_1[None], (sums_1[1] * scale_1 / whole_inner)[None], jnp.zeros((6, scale_1.shape[0]), F32)]
    )
    hidden_2 = (
        stream_1 + scatter(fwd_1[6]).astype(F32) * own_tokens(scale_1)[:, None]
    ).astype(BF16)

    def weight_grads(normed, dh, back):
        return (
            jnp.concatenate([mm_tn(normed, part) for part in back[:4]], axis=1).astype(BF16),
            mm_tn(back[4], dh).astype(BF16),
        )

    back_1 = run_backward(starts, dh_whole, stats_1, layers[1][0], fwd_1[:6])
    dnormed_1 = scatter(back_1[5]).astype(F32)
    through_1, gain_grad_1 = norm_back(stream_1, layers[1][1], dnormed_1)
    input_grad_1 = outer.astype(F32) + through_1
    dh_low = input_grad_1.astype(BF16)
    mean_0 = jnp.sum(dh_low.astype(F32) * product_0, axis=1) / whole_inner
    dh_0 = gather(dh_low)
    means_0 = gather(mean_0)
    stats_0 = jnp.concatenate([scale_0[None], means_0[None], jnp.zeros((6, scale_0.shape[0]), F32)])
    back_0 = run_backward(starts, dh_0, stats_0, layers[0][0], fwd_0[:6])
    dnormed_0 = scatter(back_0[5]).astype(F32)
    through_0, gain_grad_0 = norm_back(stream, layers[0][1], dnormed_0)
    input_grad_0 = dh_low.astype(F32) + through_0

    grads_1 = weight_grads(normed_1, dh_whole, back_1)
    grads_0 = weight_grads(normed_0, dh_0, back_0)

    def to_core(pair):
        theirs = other_core(jnp.where(core == 0, pair[1], pair[0]))
        return jnp.where(core == 0, pair[0], pair[1]).astype(F32) + theirs.astype(F32)

    in_grad = to_core((grads_0[0], grads_1[0])).astype(BF16)
    out_grad = to_core((grads_0[1], grads_1[1])).astype(BF16)
    depth = in_weight.shape[1]
    in_grad = lax.all_to_all(
        in_grad.reshape(count, depth, -1), "seq", split_axis=0, concat_axis=0, tiled=True
    )
    in_grad = lax.psum(in_grad, "dp")
    out_grad = lax.psum(out_grad, "dp")
    in_grad = in_grad.astype(F32)
    grad_in_weight = jnp.concatenate(
        [
            in_grad[:, :, :inner].transpose(1, 0, 2).reshape(depth, whole_inner),
            in_grad[:, :, inner : 2 * inner].transpose(1, 0, 2).reshape(depth, whole_inner),
            jnp.sum(in_grad[:, :, 2 * inner : 2 * inner + 2 * STATE], axis=0),
            in_grad[:, :, 2 * inner + 2 * STATE : 2 * inner + 2 * STATE + heads]
            .transpose(1, 0, 2)
            .reshape(depth, heads * count),
        ],
        axis=1,
    )

    def small(back, gain_grad):
        gx, gbc, gheads = back[6:9]
        channels = jnp.concatenate(
            [
                lax.dynamic_update_slice_in_dim(
                    jnp.zeros((TAPS + 1, whole_inner), F32), gx[: TAPS + 1], rank * inner, 1
                ),
                gbc[: TAPS + 1],
            ],
            axis=1,
        )
        own = jnp.concatenate(
            [
                gheads[0, :heads],
                gheads[1, :heads],
                jnp.sum(gx[TAPS + 1].reshape(heads, HEAD), axis=1),
                gx[TAPS + 2],
            ]
        )
        return channels, gain_grad, own

    channels, norm_grad, own = (
        to_core(pair)
        for pair in zip(small(back_0, gain_grad_0), small(back_1, gain_grad_1))
    )
    channels, norm_grad = lax.psum((channels, norm_grad), ("dp", "seq"))
    own = lax.psum(own, "dp")
    part = conv_bias.shape[1]
    channels = lax.dynamic_slice_in_dim(channels, rank * part, part, 1)
    norm_grad = lax.dynamic_slice_in_dim(norm_grad, rank * norm_gain.shape[1], norm_gain.shape[1], 0)

    def by_layer(first, second):
        mine = jnp.where(core == 0, first, second)
        theirs = other_core(jnp.where(core == 0, second, first))
        return jnp.stack([jnp.where(core == 0, mine, theirs), jnp.where(core == 0, theirs, mine)])

    return (
        by_layer(hidden_1, hidden_2)[None],
        by_layer(input_grad_0, input_grad_1)[None],
        norm_grad[None],
        grad_in_weight[None],
        channels[None, :TAPS],
        channels[TAPS:],
        own[None, :heads],
        own[None, heads : 2 * heads],
        own[None, 2 * heads : 3 * heads],
        own[None, 3 * heads :],
        out_grad.astype(F32)[None],
    )


def solution(mesh):
    return jax.shard_map(
        local,
        mesh=mesh,
        in_specs=(
            P("dp", "seq", None),
            P("dp", None),
            P("dp", "seq", None),
            P("section", "seq"),
            P("section", "seq", None),
            P("section", None, "seq"),
            P("section", "seq"),
            P("section", "seq"),
            P("section", "seq"),
            P("section", "seq"),
            P("section", "seq"),
            P("section", "seq", None),
        ),
        out_specs=(
            P("section", "dp", "seq", None),
            P("section", "dp", "seq", None),
            P("section", "seq"),
            P("section", "seq", None),
            P("section", None, "seq"),
            P("section", "seq"),
            P("section", "seq"),
            P("section", "seq"),
            P("section", "seq"),
            P("section", "seq"),
            P("section", "seq", None),
        ),
        check_vma=False,
    )
```

```python
import functools

import jax
import jax.numpy as jnp
from jax import lax
from jax.experimental import pallas as pl
from jax.experimental.pallas import tpu as pltpu
from jax.sharding import PartitionSpec as P

SPAN = 256
HEAD = 64
STATE = 128
TAPS = 4
EPSILON = 1e-05
HIGHEST = lax.Precision.HIGHEST
F32 = jnp.float32
BF16 = jnp.bfloat16
FAR = -1e30


def mm(a, b):
    return jnp.dot(a, b, preferred_element_type=F32)


def mm_nt(a, b):
    return lax.dot_general(a, b, (((1,), (1,)), ((), ())), preferred_element_type=F32)


def mm_tn(a, b):
    return lax.dot_general(a, b, (((0,), (0,)), ((), ())), preferred_element_type=F32)


def exact(a, b):
    return lax.dot_general(
        a, b, (((1,), (0,)), ((), ())), precision=HIGHEST, preferred_element_type=F32
    )


def doc_of(starts_ref, position):
    total = jnp.zeros(position.shape, jnp.int32)
    for entry in range(starts_ref.shape[0]):
        total = total + (starts_ref[entry] <= position).astype(jnp.int32)
    return total


def tiles_of(width):
    return [(low, min(low + 128, width)) for low in range(0, width, 128)]


def spread_pair(columns, tile, width):
    rows = columns.shape[0]
    first = jnp.broadcast_to(columns[:, 2 * tile : 2 * tile + 1], (rows, width))
    if width <= HEAD:
        return first
    second = jnp.broadcast_to(columns[:, 2 * tile + 1 : 2 * tile + 2], (rows, width))
    lane = lax.broadcasted_iota(jnp.int32, (rows, width), 1)
    return jnp.where(lane < HEAD, first, second)


def block_facts(starts_ref, block, length):
    base = block * SPAN
    column = base + lax.broadcasted_iota(jnp.int32, (SPAN, 128), 0)
    doc_col = doc_of(starts_ref, column)
    before = []
    for lag in range(1, TAPS):
        same = (doc_of(starts_ref, column - lag) == doc_col) & (column >= lag)
        before.append(same.astype(F32))
    row = base + lax.broadcasted_iota(jnp.int32, (8, SPAN), 1)
    doc_row = doc_of(starts_ref, row)
    same_square = doc_col[:, 0:1] == doc_row[0:1, :]
    edge_before = jnp.full((8, 128), base - 1, jnp.int32)
    last_doc_before = doc_of(starts_ref, edge_before)[0:1, :]
    last_doc = doc_of(starts_ref, jnp.full((8, 128), base + SPAN - 1, jnp.int32))[0:1, :]
    carried = ((doc_col == last_doc_before) & (base > 0)).astype(F32)
    to_last = (doc_col == last_doc).astype(F32)
    return doc_col, column, before, same_square, carried, to_last


def taps_sum(ext_ref, low, high, before, kernel, bias):
    summed = ext_ref[pl.ds(8, SPAN), low:high] * kernel[TAPS - 1 : TAPS, low:high] + bias[0:1, low:high]
    for lag in range(1, TAPS):
        summed = summed + (
            ext_ref[pl.ds(8 - lag, SPAN), low:high]
            * before[lag - 1][:, : high - low]
            * kernel[TAPS - 1 - lag : TAPS - lag, low:high]
        )
    return summed


def sigmoid(value):
    return 1.0 / (1.0 + jnp.exp(-value))


def softplus(value):
    small = jnp.exp(-jnp.abs(value))
    series = small * (1.0 - small * (0.5 - small * (1.0 / 3.0)))
    return jnp.maximum(value, 0.0) + jnp.where(small < 0.01, series, jnp.log(1.0 + small))


def lower_ones():
    row = lax.broadcasted_iota(jnp.int32, (SPAN, SPAN), 0)
    col = lax.broadcasted_iota(jnp.int32, (SPAN, SPAN), 1)
    return row, col


def split_weights(inner, refs):
    if refs[0].shape[1] > inner:
        parts = [(0, inner), (inner, 2 * inner), (2 * inner, 2 * inner + 3 * STATE)]
        return [refs[0].at[:, low:high] for low, high in parts] + [refs[1:]]
    return [refs[0], refs[1], refs[2], refs[3:]]


def own_heads(columns, heads, sign):
    shift = lax.rem(128 + sign * heads * lax.axis_index("seq"), 128)
    return pltpu.roll(columns, shift, 1)


def forward_kernel(
    with_back,
    length,
    starts_ref,
    normed_ref,
    kx_ref,
    kbc_ref,
    heads_ref,
    gain_ref,
    wo_ref,
    *rest,
):
    inner = kx_ref.shape[1]
    wg_ref, wx_ref, wbc_ref, rest = split_weights(inner, rest)
    if with_back:
        dh_ref, rest = rest[0], rest[1:]
    (
        gate_ref,
        x_ref,
        bc_ref,
        dt_ref,
        scan_ref,
        state_ref,
        part_ref,
        stat_ref,
        ext_x,
        ext_bc,
        memory,
        gu_ref,
    ) = rest
    block = pl.program_id(0)

    @pl.when(block == 0)
    def _():
        ext_x[...] = jnp.zeros_like(ext_x)
        ext_bc[...] = jnp.zeros_like(ext_bc)
        memory[...] = jnp.zeros_like(memory)

    @pl.when(block > 0)
    def _():
        ext_x[0:8, :] = ext_x[SPAN : SPAN + 8, :]
        ext_bc[0:8, :] = ext_bc[SPAN : SPAN + 8, :]

    normed = normed_ref[...]
    bcdt = mm(normed, wbc_ref[...]).astype(BF16)
    bc_ref[...] = bcdt[:, : 2 * STATE]
    ext_bc[8 : SPAN + 8, :] = bcdt[:, : 2 * STATE].astype(F32)
    dt_low = own_heads(bcdt[:, 2 * STATE :].astype(F32), inner // HEAD, -1)
    dt_ref[...] = dt_low
    x_low = mm(normed, wx_ref[...]).astype(BF16)
    x_ref[...] = x_low
    ext_x[8 : SPAN + 8, :] = x_low.astype(F32)
    gate_low = mm(normed, wg_ref[...]).astype(BF16)
    gate_ref[...] = gate_low

    _, _, before, same_square, carried, to_last = block_facts(starts_ref, block, length)
    row, col = lower_ones()
    lower = (row >= col).astype(F32)
    keep = jnp.where(same_square & (row >= col), 0.0, FAR)

    delta = softplus(dt_low + heads_ref[0:1, :])
    rate = -jnp.exp(heads_ref[1:2, :]) * delta
    total = exact(lower, rate)
    total_rows = jnp.transpose(total)
    grown = carried * jnp.exp(total)
    last_total = total[SPAN - 1 : SPAN, :]
    ending = to_last * jnp.exp(last_total - total)
    carry_last = grown[SPAN - 1 : SPAN, :]

    kbc = kbc_ref[...]
    b_conv = taps_sum(ext_bc, 0, STATE, before, kbc, kbc[TAPS : TAPS + 1])
    c_conv = taps_sum(ext_bc, STATE, 2 * STATE, before, kbc, kbc[TAPS : TAPS + 1])
    b_low = (b_conv * sigmoid(b_conv)).astype(BF16)
    c_low = (c_conv * sigmoid(c_conv)).astype(BF16)
    scores = mm_nt(c_low, b_low)
    b_flip = jnp.transpose(b_low.astype(F32)).astype(BF16)

    state_ref[0] = memory[...].astype(BF16)
    kx = kx_ref[...]
    squares = jnp.zeros((SPAN, 128), F32)
    for tile, (low, high) in enumerate(tiles_of(inner)):
        width = high - low
        lane = lax.broadcasted_iota(jnp.int32, (SPAN, width), 1)
        conv = taps_sum(ext_x, low, high, before, kx, kx[TAPS : TAPS + 1])
        values = conv * sigmoid(conv)
        weighted = spread_pair(delta, tile, width) * values
        w_low = weighted.astype(BF16)
        mixed = None
        for half in range(width // HEAD):
            head = 2 * tile + half
            decay = jnp.exp(total[:, head : head + 1] - total_rows[head : head + 1, :] + keep)
            part = mm((scores * decay).astype(BF16), w_low)
            mixed = part if mixed is None else jnp.where(lane < HEAD, mixed, part)
        mem = memory[:, low:high]
        mixed = mixed + mm(c_low, mem.astype(BF16)) * spread_pair(grown, tile, width)
        scan_ref[:, low:high] = mixed
        fresh = mm(b_flip, (weighted * spread_pair(ending, tile, width)).astype(BF16))
        memory[:, low:high] = mem * spread_pair(carry_last, tile, width) + fresh
        mixed = (
            (mixed + spread_pair(heads_ref[2:3, :], tile, width) * values).astype(BF16).astype(F32)
        )
        gate = gate_ref[:, low:high].astype(F32)
        g = mixed * (gate * sigmoid(gate))
        if width == 128:
            squares = squares + g * g
        else:
            squares = squares + jnp.concatenate([g * g, jnp.zeros((SPAN, 128 - width), F32)], axis=1)
        gu_ref[:, low:high] = (g * gain_ref[0:1, low:high]).astype(BF16)

    stats = jnp.sum(squares, axis=1, keepdims=True)
    gu = gu_ref[...]
    part_ref[...] = mm(gu, wo_ref[...]).astype(part_ref.dtype)
    if with_back:
        dgated = mm_nt(dh_ref[...], wo_ref[...])
        along = jnp.sum(dgated * gu.astype(F32), axis=1, keepdims=True)
        lane = lax.broadcasted_iota(jnp.int32, (SPAN, 128), 1)
        both = jnp.where(lane == 0, stats, jnp.where(lane == 1, along, 0.0))
    else:
        both = jnp.broadcast_to(stats, (SPAN, 128))
    stat_ref[...] = jnp.transpose(both)[0:8, :]


def carry_on(sources, slots, sems):
    turn, turns = pl.program_id(0), pl.num_programs(0)
    copies = lax.axis_size("dp")
    member = lax.axis_index("dp")
    square = Square(member, sources, slots, sems)
    holds = lax.axis_index("section") == 1

    @pl.when(turn == 0)
    def _():
        greet_all({"dp": copies}, {"dp": member})

    for when, stage in ((0, square.begin), (turns // 2, square.middle), (turns - 1, square.end)):

        @pl.when((turn == when) & holds)
        def _():
            stage(0)
            stage(1)


def backward_kernel(
    carries,
    length,
    starts_ref,
    dh_ref,
    scale_ref,
    mean_ref,
    kx_ref,
    kbc_ref,
    heads_ref,
    gain_ref,
    wo_ref,
    gate_ref,
    x_ref,
    xh_ref,
    bc_ref,
    bch_ref,
    dt_ref,
    scan_ref,
    state_ref,
    *rest,
):
    inner = kx_ref.shape[1]
    wg_ref, wx_ref, wbc_ref, rest = split_weights(inner, rest)
    if carries:
        sources, rest = rest[:2], rest[2:]
    dgate_ref, dx_ref, dbc_ref, rest = split_weights(inner, rest)
    gated_ref, dnormed_ref, gx_ref, gbc_ref, gheads_ref, *rest = rest
    if carries:
        slots, sems, rest = rest[:2], rest[-3:], rest[2:-3]
        carry_on(sources, slots, sems)
    (
        ext_x,
        ext_bc,
        ext_dx,
        ext_dbc,
        dmemory,
        dscore,
    ) = rest
    blocks = pl.num_programs(0)
    block = blocks - 1 - pl.program_id(0)

    @pl.when(pl.program_id(0) == 0)
    def _():
        ext_dx[...] = jnp.zeros_like(ext_dx)
        ext_dbc[...] = jnp.zeros_like(ext_dbc)
        dmemory[...] = jnp.zeros_like(dmemory)
        gx_ref[...] = jnp.zeros_like(gx_ref)
        gbc_ref[...] = jnp.zeros_like(gbc_ref)
        gheads_ref[...] = jnp.zeros_like(gheads_ref)

    @pl.when(pl.program_id(0) > 0)
    def _():
        ext_dx[SPAN : SPAN + 8, :] = ext_dx[0:8, :]
        ext_dbc[SPAN : SPAN + 8, :] = ext_dbc[0:8, :]

    ext_x[0:8, :] = xh_ref[8:16, :].astype(F32)
    ext_x[8 : SPAN + 8, :] = x_ref[...].astype(F32)
    ext_bc[0:8, :] = bch_ref[8:16, :].astype(F32)
    ext_bc[8 : SPAN + 8, :] = bc_ref[...].astype(F32)

    doc_col, column, before, same_square, carried, to_last = block_facts(starts_ref, block, length)
    after = []
    for lag in range(1, TAPS):
        same = (doc_of(starts_ref, column + lag) == doc_col) & (column + lag < length)
        after.append(same.astype(F32))
    row, col = lower_ones()
    lower = (row >= col).astype(F32)
    upper = (row <= col).astype(F32)
    keep = jnp.where(same_square & (row <= col), 0.0, FAR)

    dt = dt_ref[...] + heads_ref[0:1, :]
    delta = softplus(dt)
    slope = -jnp.exp(heads_ref[1:2, :])
    rate = slope * delta
    total = exact(lower, rate)
    total_rows = jnp.transpose(total)
    grown = carried * jnp.exp(total)
    last_total = total[SPAN - 1 : SPAN, :]
    ending = to_last * jnp.exp(last_total - total)
    carry_last = grown[SPAN - 1 : SPAN, :]

    kbc = kbc_ref[...]
    b_conv = taps_sum(ext_bc, 0, STATE, before, kbc, kbc[TAPS : TAPS + 1])
    c_conv = taps_sum(ext_bc, STATE, 2 * STATE, before, kbc, kbc[TAPS : TAPS + 1])
    b_sig = sigmoid(b_conv)
    c_sig = sigmoid(c_conv)
    b_low = (b_conv * b_sig).astype(BF16)
    c_low = (c_conv * c_sig).astype(BF16)
    scores = mm_nt(b_low, c_low)
    c_flip = jnp.transpose(c_low.astype(F32)).astype(BF16)

    stat_cols = row_to_columns(scale_ref[0, 0:1, :])
    mean_cols = row_to_columns(mean_ref[0, 0:1, :])
    dgated = mm_nt(dh_ref[...], wo_ref[...])
    dscore[...] = jnp.zeros_like(dscore)
    kx = kx_ref[...]
    db = jnp.zeros((SPAN, STATE), F32)
    dc = jnp.zeros((SPAN, STATE), F32)
    dtotal = jnp.zeros((SPAN, 128), F32)
    ddelta = jnp.zeros((SPAN, 128), F32)
    dlast = jnp.zeros((8, 128), F32)
    for tile, (low, high) in enumerate(tiles_of(inner)):
        width = high - low
        lane = lax.broadcasted_iota(jnp.int32, (SPAN, width), 1)
        picker = (
            lax.broadcasted_iota(jnp.int32, (width, 128), 1)
            == 2 * tile + lax.broadcasted_iota(jnp.int32, (width, 128), 0) // HEAD
        ).astype(F32)
        skip = spread_pair(heads_ref[2:3, :], tile, width)
        conv = taps_sum(ext_x, low, high, before, kx, kx[TAPS : TAPS + 1])
        sig = sigmoid(conv)
        values = conv * sig
        delta_t = spread_pair(delta, tile, width)
        weighted = delta_t * values
        w_low = weighted.astype(BF16)
        scanned = scan_ref[:, low:high]
        mixed = (scanned + skip * values).astype(BF16).astype(F32)
        gate = gate_ref[:, low:high].astype(F32)
        gate_sig = sigmoid(gate)
        silu = gate * gate_sig
        g = mixed * silu
        scale = stat_cols[:, :width]
        n = g * scale
        gain = gain_ref[0:1, low:high]
        dgated_t = dgated[:, low:high]
        gated_ref[:, low:high] = (n * gain).astype(BF16)
        dg = scale * (dgated_t * gain - n * mean_cols[:, :width])
        dgate_ref[:, low:high] = (
            dg * mixed * (gate_sig * (1.0 + gate * (1.0 - gate_sig)))
        ).astype(BF16)
        dy_low = (dg * silu).astype(BF16)
        dy = dy_low.astype(F32)
        grad_w = None
        for half in range(width // HEAD):
            head = 2 * tile + half
            decay = jnp.exp(total_rows[head : head + 1, :] - total[:, head : head + 1] + keep)
            mine = (lane // HEAD) == half
            pairs = mm_nt(jnp.where(mine, w_low, jnp.zeros_like(w_low)), dy_low)
            dscore[...] += decay * pairs
            part = mm((scores * decay).astype(BF16), dy_low)
            grad_w = part if grad_w is None else jnp.where(lane < HEAD, grad_w, part)
        dmem = dmemory[:, low:high]
        dmem_low = dmem.astype(BF16)
        mem_low = state_ref[0, :, low:high]
        ending_t = spread_pair(ending, tile, width)
        from_state = mm(b_low, dmem_low) * ending_t
        grad_w = grad_w + from_state
        db = db + mm_nt((weighted * ending_t).astype(BF16), dmem_low)
        dy_grown = (dy * spread_pair(grown, tile, width)).astype(BF16)
        dc = dc + mm_nt(dy_grown, mem_low)
        carry_t = spread_pair(carry_last, tile, width)
        w_round = w_low.astype(F32)
        at_last = jnp.sum(w_round * from_state, axis=0, keepdims=True) + jnp.sum(
            dmem * mem_low.astype(F32) * carry_t, axis=0, keepdims=True
        )
        dlast = dlast + exact(jnp.broadcast_to(at_last, (8, width)), picker)
        dmemory[:, low:high] = dmem * carry_t + mm(c_flip, dy_grown)
        dtotal = dtotal + exact(dy * scanned - w_round * grad_w, picker)
        ddelta = ddelta + exact(values * grad_w, picker)
        dconv = (delta_t * grad_w + skip * dy) * (sig * (1.0 + conv * (1.0 - sig)))
        ext_dx[0:SPAN, low:high] = dconv
        sums = [jnp.sum(dconv * ext_x[pl.ds(8, SPAN), low:high], axis=0, keepdims=True)]
        for lag in range(1, TAPS):
            sums.append(
                jnp.sum(
                    dconv * before[lag - 1][:, :width] * ext_x[pl.ds(8 - lag, SPAN), low:high],
                    axis=0,
                    keepdims=True,
                )
            )
        sums = sums[::-1] + [
            jnp.sum(dconv, axis=0, keepdims=True),
            jnp.sum(dy * values, axis=0, keepdims=True),
            jnp.sum(dgated_t * n, axis=0, keepdims=True),
            jnp.zeros((1, width), F32),
        ]
        gx_ref[:, low:high] += jnp.concatenate(sums, axis=0)
        back = ext_dx[0:SPAN, low:high] * kx[TAPS - 1 : TAPS, low:high]
        for lag in range(1, TAPS):
            back = back + (
                ext_dx[pl.ds(lag, SPAN), low:high]
                * after[lag - 1][:, :width]
                * kx[TAPS - 1 - lag : TAPS - lag, low:high]
            )
        dx_ref[:, low:high] = back.astype(BF16)

    score_grad = dscore[...]
    db = db + mm(score_grad.astype(BF16), c_low)
    dc = dc + mm(jnp.transpose(score_grad).astype(BF16), b_low)
    for part, (conv, sig, grad) in enumerate(((b_conv, b_sig, db), (c_conv, c_sig, dc))):
        low, high = part * STATE, (part + 1) * STATE
        dconv = grad * (sig * (1.0 + conv * (1.0 - sig)))
        ext_dbc[0:SPAN, low:high] = dconv
        sums = [jnp.sum(dconv * ext_bc[pl.ds(8, SPAN), low:high], axis=0, keepdims=True)]
        for lag in range(1, TAPS):
            sums.append(
                jnp.sum(
                    dconv * before[lag - 1] * ext_bc[pl.ds(8 - lag, SPAN), low:high],
                    axis=0,
                    keepdims=True,
                )
            )
        sums = sums[::-1] + [jnp.sum(dconv, axis=0, keepdims=True), jnp.zeros((3, STATE), F32)]
        gbc_ref[:, low:high] += jnp.concatenate(sums, axis=0)
        back = dconv * kbc[TAPS - 1 : TAPS, low:high]
        for lag in range(1, TAPS):
            back = back + (
                ext_dbc[pl.ds(lag, SPAN), low:high]
                * after[lag - 1]
                * kbc[TAPS - 1 - lag : TAPS - lag, low:high]
            )
        dbc_ref[:, low:high] = back.astype(BF16)

    drate = exact(upper, dtotal) + dlast[0:1, :]
    ddt = (ddelta + slope * drate) * sigmoid(dt)
    lane = lax.broadcasted_iota(jnp.int32, (SPAN, 128), 1)
    own_ddt = jnp.where(lane < inner // HEAD, ddt, 0.0)
    dbc_ref[:, 2 * STATE :] = own_heads(own_ddt, inner // HEAD, 1).astype(BF16)
    gheads_ref[...] += jnp.concatenate(
        [
            jnp.sum(ddt, axis=0, keepdims=True),
            jnp.sum(drate * rate, axis=0, keepdims=True),
            jnp.zeros((6, 128), F32),
        ],
        axis=0,
    )
    dnormed_ref[...] = (
        mm_nt(dgate_ref[...], wg_ref[...])
        + mm_nt(dx_ref[...], wx_ref[...])
        + mm_nt(dbc_ref[...], wbc_ref[...])
    ).astype(dnormed_ref.dtype)


def whole(array):
    return pl.BlockSpec(array.shape, lambda i: (0,) * array.ndim, pipeline_mode=pl.Buffered(1))


def of_layer(array, layer):
    return pl.BlockSpec(
        (None,) + array.shape[1:],
        lambda i: (layer,) + (0,) * (array.ndim - 1),
        pipeline_mode=pl.Buffered(1),
    )


def cost(length, width, inner, passes):
    flops = 2 * length * width * (3 * inner + 384) * passes
    return pl.CostEstimate(flops=flops, bytes_accessed=length * width * 16, transcendentals=0)


VMEM_LIMIT = 48 * 2**20


def part_kind(length, width):
    return F32 if length * width * 4 <= 8 * 2**20 else BF16


def run_forward(starts, normed, weights, dh=None):
    columns, kx, kbc, heads, gain, wo = weights
    length, width = normed.shape
    inner = kx.shape[1]
    blocks = length // SPAN
    rows = lambda cols: pl.BlockSpec((SPAN, cols), lambda i: (i, 0))
    small = [kx, kbc, heads, gain]
    given = [wo] + list(columns)
    operands = [starts, normed] + small + [array for array, _ in given]
    in_specs = [pl.BlockSpec(memory_space=pltpu.SMEM), rows(width)]
    in_specs += [whole(array) for array in small] + [spec for _, spec in given]
    if dh is not None:
        operands.append(dh)
        in_specs.append(rows(width))
    out_shape = [
        jax.ShapeDtypeStruct((length, inner), BF16),
        jax.ShapeDtypeStruct((length, inner), BF16),
        jax.ShapeDtypeStruct((length, 2 * STATE), BF16),
        jax.ShapeDtypeStruct((length, 128), F32),
        jax.ShapeDtypeStruct((length, inner), F32),
        jax.ShapeDtypeStruct((blocks, STATE, inner), BF16),
        jax.ShapeDtypeStruct((length, width), part_kind(length, width)),
        jax.ShapeDtypeStruct((8, length), F32),
    ]
    out_specs = [
        rows(inner),
        rows(inner),
        rows(2 * STATE),
        rows(128),
        rows(inner),
        pl.BlockSpec((1, STATE, inner), lambda i: (i, 0, 0)),
        rows(width),
        pl.BlockSpec((8, SPAN), lambda i: (0, i)),
    ]
    return pl.pallas_call(
        functools.partial(forward_kernel, dh is not None, length),
        grid=(blocks,),
        in_specs=in_specs,
        out_specs=out_specs,
        out_shape=out_shape,
        scratch_shapes=[
            pltpu.VMEM((SPAN + 8, inner), F32),
            pltpu.VMEM((SPAN + 8, 2 * STATE), F32),
            pltpu.VMEM((STATE, inner), F32),
            pltpu.VMEM((SPAN, inner), BF16),
        ],
        compiler_params=pltpu.CompilerParams(
            dimension_semantics=("arbitrary",), vmem_limit_bytes=VMEM_LIMIT
        ),
        cost_estimate=cost(length, width, inner, 1),
        name="layer_forward",
    )(*operands)


def run_backward(starts, dh, scales, means, weights, saved, carried=()):
    columns, kx, kbc, heads, gain, wo = weights
    gate, x, bc, dt, scanned, states = saved
    length, width = dh.shape
    inner = kx.shape[1]
    blocks = length // SPAN
    rows = lambda cols: pl.BlockSpec((SPAN, cols), lambda i: (blocks - 1 - i, 0))
    halo = lambda cols: pl.BlockSpec(
        (16, cols), lambda i: (jnp.maximum((blocks - 1 - i) * (SPAN // 16) - 1, 0), 0)
    )
    fixed = lambda shape: pl.BlockSpec(shape, lambda i: (0,) * len(shape))
    stat = pl.BlockSpec((1, 8, SPAN), lambda i: (blocks - 1 - i, 0, 0))
    small = [kx, kbc, heads, gain]
    operands = [starts, dh, scales, means] + small + [wo[0]]
    in_specs = [pl.BlockSpec(memory_space=pltpu.SMEM), rows(width), stat, stat]
    in_specs += [whole(array) for array in small] + [wo[1]]
    operands += [gate, x, x, bc, bc, dt, scanned, states]
    in_specs += [
        rows(inner),
        rows(inner),
        halo(inner),
        rows(2 * STATE),
        halo(2 * STATE),
        rows(128),
        rows(inner),
        pl.BlockSpec((1, STATE, inner), lambda i: (blocks - 1 - i, 0, 0)),
    ]
    operands += [array for array, _ in columns]
    in_specs += [spec for _, spec in columns]
    operands += list(carried)
    in_specs += [whole(array) for array in carried]
    widths = [2 * inner + 3 * STATE] if len(columns) == 1 else [inner, inner, 3 * STATE]
    out_shape = [jax.ShapeDtypeStruct((length, cols), BF16) for cols in widths] + [
        jax.ShapeDtypeStruct((length, inner), BF16),
        jax.ShapeDtypeStruct((length, width), part_kind(length, width)),
        jax.ShapeDtypeStruct((8, inner), F32),
        jax.ShapeDtypeStruct((8, 2 * STATE), F32),
        jax.ShapeDtypeStruct((8, 128), F32),
    ]
    out_specs = [rows(cols) for cols in widths] + [
        rows(inner),
        rows(width),
        fixed((8, inner)),
        fixed((8, 2 * STATE)),
        fixed((8, 128)),
    ]
    sems, settings = [], {}
    if carried:
        copies = lax.axis_size("dp")
        out_shape += [jax.ShapeDtypeStruct((copies,) + c.shape, c.dtype) for c in carried]
        out_specs += [IN_HBM, IN_HBM]
        sems, settings = square_sems(), {"collective_id": 6, "has_side_effects": True}
    return pl.pallas_call(
        functools.partial(backward_kernel, bool(carried), length),
        grid=(blocks,),
        in_specs=in_specs,
        out_specs=out_specs,
        out_shape=out_shape,
        scratch_shapes=[
            pltpu.VMEM((SPAN + 8, inner), F32),
            pltpu.VMEM((SPAN + 8, 2 * STATE), F32),
            pltpu.VMEM((SPAN + 8, inner), F32),
            pltpu.VMEM((SPAN + 8, 2 * STATE), F32),
            pltpu.VMEM((STATE, inner), F32),
            pltpu.VMEM((SPAN, SPAN), F32),
        ]
        + sems,
        compiler_params=pltpu.CompilerParams(
            dimension_semantics=("arbitrary",), vmem_limit_bytes=VMEM_LIMIT, **settings
        ),
        cost_estimate=cost(length, width, inner, 2),
        name="layer_backward",
    )(*operands)


def norm_rows(rows_in, gain_vec):
    return (
        rows_in
        * lax.rsqrt(jnp.mean(rows_in * rows_in, axis=-1, keepdims=True) + EPSILON)
        * gain_vec
    )


def norm_back(rows_in, gain_vec, grad):
    inverse = lax.rsqrt(jnp.mean(rows_in * rows_in, axis=-1, keepdims=True) + EPSILON)
    unit = rows_in * inverse
    scaled = grad * gain_vec
    back = inverse * (scaled - unit * jnp.mean(scaled * unit, axis=-1, keepdims=True))
    return back, jnp.sum(grad * unit, axis=0, keepdims=True)


MESH = pl.DeviceIdType.MESH
PIECE = 16
HOP = 1


def along(axis, index):
    return {axis: index}


def greet(axis, count, rank):
    barrier = pltpu.get_barrier_semaphore()
    for step in range(1, count):
        pl.semaphore_signal(
            barrier, inc=1, device_id=along(axis, lax.rem(rank + step, count)), device_id_type=MESH
        )
    pl.semaphore_wait(barrier, count - 1)


def send_to(axis, index, source, target, send_sem, recv_sem):
    return pltpu.make_async_remote_copy(
        src_ref=source,
        dst_ref=target,
        send_sem=send_sem,
        recv_sem=recv_sem,
        device_id=along(axis, index),
        device_id_type=MESH,
    )


def share_with_all(count, rank, source, slots, send_sems, recv_sems):
    for step in range(1, count):
        to = lax.rem(rank + step, count)
        send_to("seq", to, source, slots.at[rank], send_sems.at[step], recv_sems.at[rank]).start()


def share_wait_recv(count, rank, source, slots, send_sems, recv_sems):
    for step in range(1, count):
        origin = lax.rem(rank + step, count)
        send_to(
            "seq", origin, source, slots.at[origin], send_sems.at[step], recv_sems.at[origin]
        ).wait_recv()


def share_wait_send(count, rank, source, slots, send_sems, recv_sems):
    for step in range(1, count):
        to = lax.rem(rank + step, count)
        send_to("seq", to, source, slots.at[rank], send_sems.at[step], recv_sems.at[rank]).wait_send()


class Line:
    def __init__(self, count, rank, part, inbox, spread, sems):
        self.count, self.rank = count, rank
        self.part, self.inbox, self.spread = part, inbox, spread
        self.sum_send, self.sum_recv, self.out_right, self.out_left, self.out_recv = sems

    def sum_copy(self, slot, target_slot, to, piece):
        rows = pl.ds(piece * PIECE, PIECE)
        return send_to(
            "seq",
            to,
            self.inbox.at[slot, rows],
            self.inbox.at[target_slot, rows],
            self.sum_send.at[slot, piece],
            self.sum_recv.at[target_slot, piece],
        )

    def arrived(self, slot, piece):
        self.sum_copy(slot, slot, self.rank, piece).wait_recv()

    def own_part(self, block, piece):
        start = pl.multiple_of(block * SPAN + piece * PIECE, PIECE)
        return self.part[pl.ds(start, PIECE), :].astype(F32)

    def pass_sum(self, piece, away, sign):
        count, rank = self.count, self.rank
        rows = pl.ds(pl.multiple_of(piece * PIECE, PIECE), PIECE)
        block = rank + sign * away
        first = rank == 0 if sign > 0 else rank == count - 1

        @pl.when(first)
        def _():
            self.inbox[block, rows, :] = self.own_part(block, piece).astype(BF16)

        @pl.when(jnp.logical_not(first))
        def _():
            self.arrived(block, piece)
            total = self.own_part(block, piece) + self.inbox[block, rows, :].astype(F32)
            self.inbox[block, rows, :] = total.astype(BF16)

        target = count if sign < 0 and away == 1 else block
        self.sum_copy(block, target, rank + sign, piece).start()

    def pass_sums(self, turn, pieces):
        count, rank = self.count, self.rank
        for away in range(count - 1, 0, -1):
            for sign in (1, -1):
                block = rank + sign * away
                inside = block < count if sign > 0 else block >= 0
                piece = turn - HOP * (rank if sign > 0 else count - 1 - rank)

                @pl.when(inside & (piece >= 0) & (piece < pieces))
                def _():
                    self.pass_sum(piece, away, sign)

    def own_lag(self, block):
        return HOP * jnp.maximum(block, self.count - 1 - block)

    def own_total(self, piece):
        count, rank = self.count, self.rank
        rows = pl.ds(pl.multiple_of(piece * PIECE, PIECE), PIECE)

        @pl.when(rank > 0)
        def _():
            self.arrived(rank, piece)

        @pl.when(rank < count - 1)
        def _():
            self.arrived(count, piece)

        from_left = jnp.where(rank > 0, self.inbox[rank, rows, :].astype(F32), 0.0)
        from_right = jnp.where(rank < count - 1, self.inbox[count, rows, :].astype(F32), 0.0)
        return self.own_part(rank, piece) + from_left + from_right

    def out_copy(self, block, piece, sign):
        rows = pl.ds(pl.multiple_of(piece * PIECE, PIECE), PIECE)
        sems = self.out_right if sign > 0 else self.out_left
        return send_to(
            "seq",
            self.rank + sign,
            self.spread.at[block, rows],
            self.spread.at[block, rows],
            sems.at[block, piece],
            self.out_recv.at[block, piece],
        )

    def start_out(self, block, piece, sign):
        @pl.when(self.rank < self.count - 1 if sign > 0 else self.rank > 0)
        def _():
            self.out_copy(block, piece, sign).start()

    def pass_out(self, turn, pieces, away):
        for sign in (1, -1):
            block = self.rank - sign * away
            piece = turn - self.own_lag(block) - HOP * away
            inside = block >= 0 if sign > 0 else block < self.count

            @pl.when(inside & (piece >= 0) & (piece < pieces))
            def _():
                self.out_copy(block, piece, sign).wait_recv()
                self.start_out(block, piece, sign)

    def run(self, pieces, own_piece, before_own=None, after_own=None, flow=None, pace=2):
        count = self.count
        lag = self.own_lag(self.rank)
        turns = pieces + HOP * (2 if self.spread is not None else 1) * (count - 1)
        if flow is not None:
            turns = max(turns, flow.turns(pace))

        def step(turn, _):
            self.pass_sums(turn, pieces)
            if self.spread is not None:
                for away in range(1, count):
                    self.pass_out(turn, pieces, away)
            if before_own is not None:

                @pl.when(turn == lag)
                def _():
                    before_own()

            piece = turn - lag

            @pl.when((piece >= 0) & (piece < pieces))
            def _():
                own_piece(piece, self.own_total(piece))
                if self.spread is not None:
                    self.start_out(self.rank, piece, 1)
                    self.start_out(self.rank, piece, -1)

            if after_own is not None:

                @pl.when(piece == pieces - 1)
                def _():
                    after_own()

            if flow is not None:
                flow.turn(turn, pace)
            return 0

        lax.fori_loop(0, turns, step, 0)

        def settle(piece, _):
            for block in range(count):
                right = (block > self.rank) & (self.rank < count - 1)
                left = (block < self.rank) & (self.rank > 0)

                @pl.when(right | left)
                def _():
                    self.sum_copy(block, block, self.rank, piece).wait_send()

                if self.spread is not None:

                    @pl.when((block <= self.rank) & (self.rank < count - 1))
                    def _():
                        self.out_copy(block, piece, 1).wait_send()

                    @pl.when((block >= self.rank) & (self.rank > 0))
                    def _():
                        self.out_copy(block, piece, -1).wait_send()

            return 0

        lax.fori_loop(0, pieces, settle, 0)


def line_sems(count, pieces):
    return [
        pltpu.SemaphoreType.DMA((count + 1, pieces)),
        pltpu.SemaphoreType.DMA((count + 1, pieces)),
        pltpu.SemaphoreType.DMA((count, pieces)),
        pltpu.SemaphoreType.DMA((count, pieces)),
        pltpu.SemaphoreType.DMA((count, pieces)),
    ]


def row_to_columns(row):
    return jnp.transpose(jnp.broadcast_to(row, (128, SPAN)))


def sum_forward_kernel(
    count,
    whole_inner,
    part,
    stat,
    stream,
    gain,
    spread,
    scales,
    hidden,
    product,
    inbox,
    slots,
    columns,
    stat_send,
    stat_recv,
    *sems,
):
    rank = lax.axis_index("seq")
    greet("seq", count, rank)
    share = (count, rank, stat, slots, stat_send, stat_recv)
    share_with_all(*share)
    line = Line(count, rank, part, inbox, spread, sems)

    def before_own():
        share_wait_recv(*share)
        for block in range(count):
            lanes = slice(block * SPAN, (block + 1) * SPAN)
            total = stat[:, lanes]
            for origin in range(count):
                total = total + jnp.where(origin == rank, 0.0, slots[origin, :, lanes])
            scales[block] = lax.rsqrt(total / whole_inner + EPSILON)
        columns[...] = row_to_columns(scales[rank][0:1, :])

    def own_piece(piece, total):
        rows = pl.ds(pl.multiple_of(piece * PIECE, PIECE), PIECE)
        y = total * columns[rows, 0:1]
        low = (stream[rows, :].astype(F32) + y).astype(BF16)
        hidden[rows, :] = low
        product[rows, :] = y
        spread[rank, rows, :] = norm_rows(low.astype(F32), gain[0:1, :]).astype(BF16)

    line.run(SPAN // PIECE, own_piece, before_own)
    share_wait_send(*share)


def sum_plain_kernel(count, part, stream, gain, outer, grad, gain_grad, inbox, *sems):
    rank = lax.axis_index("seq")
    greet("seq", count, rank)
    line = Line(count, rank, part, inbox, None, tuple(sems) + (None,) * 3)
    gain_grad[...] = jnp.zeros_like(gain_grad)

    def own_piece(piece, total):
        rows = pl.ds(pl.multiple_of(piece * PIECE, PIECE), PIECE)
        back, gain_part = norm_back(stream[rows, :].astype(F32), gain[0:1, :], total)
        gain_grad[0:1, :] += gain_part
        grad[rows, :] = outer[rows, :].astype(F32) + back

    line.run(SPAN // PIECE, own_piece)


def sum_stats_kernel(count, whole_inner, stat, scales, means, slots, stat_send, stat_recv):
    rank = lax.axis_index("seq")
    greet("seq", count, rank)
    share = (count, rank, stat, slots, stat_send, stat_recv)
    share_with_all(*share)
    share_wait_recv(*share)
    for block in range(count):
        lanes = slice(block * SPAN, (block + 1) * SPAN)
        total = stat[:, lanes]
        for origin in range(count):
            total = total + jnp.where(origin == rank, 0.0, slots[origin, :, lanes])
        scale = lax.rsqrt(total[0:1, :] / whole_inner + EPSILON)
        scales[block] = jnp.broadcast_to(scale, (8, SPAN))
        means[block] = jnp.broadcast_to(total[1:2, :] * scale / whole_inner, (8, SPAN))
    share_wait_send(*share)


IN_VMEM = pl.BlockSpec(memory_space=pltpu.VMEM)


def line_call(kernel, name, collective_id, operands, out_shape, scratch):
    return pl.pallas_call(
        kernel,
        out_shape=out_shape,
        in_specs=[IN_VMEM] * len(operands),
        out_specs=[IN_VMEM] * len(out_shape),
        scratch_shapes=scratch,
        compiler_params=pltpu.CompilerParams(
            collective_id=collective_id, has_side_effects=True, vmem_limit_bytes=LINE_VMEM
        ),
        name=name,
    )(*operands)


LINE_VMEM = 60 * 2**20


def sum_forward(part, stat, stream, gain, whole_inner):
    count = lax.axis_size("seq")
    length, width = part.shape
    pieces = SPAN // PIECE
    return line_call(
        functools.partial(sum_forward_kernel, count, whole_inner),
        "sum_forward",
        1,
        [part, stat, stream, gain],
        [
            jax.ShapeDtypeStruct((count, SPAN, width), BF16),
            jax.ShapeDtypeStruct((count, 8, SPAN), F32),
            jax.ShapeDtypeStruct((SPAN, width), BF16),
            jax.ShapeDtypeStruct((SPAN, width), F32),
        ],
        [
            pltpu.VMEM((count + 1, SPAN, width), BF16),
            pltpu.VMEM((count, 8, length), F32),
            pltpu.VMEM((SPAN, 128), F32),
            pltpu.SemaphoreType.DMA((count,)),
            pltpu.SemaphoreType.DMA((count,)),
        ]
        + line_sems(count, pieces),
    )


def sum_plain(part, stream, gain, outer):
    count = lax.axis_size("seq")
    length, width = part.shape
    pieces = SPAN // PIECE
    return line_call(
        functools.partial(sum_plain_kernel, count),
        "sum_plain",
        3,
        [part, stream, gain, outer],
        [
            jax.ShapeDtypeStruct((SPAN, width), F32),
            jax.ShapeDtypeStruct((8, width), F32),
        ],
        [pltpu.VMEM((count + 1, SPAN, width), BF16)] + line_sems(count, pieces)[:2],
    )


def sum_stats(stat, whole_inner):
    count = lax.axis_size("seq")
    length = stat.shape[1]
    return line_call(
        functools.partial(sum_stats_kernel, count, whole_inner),
        "sum_stats",
        4,
        [stat],
        [
            jax.ShapeDtypeStruct((count, 8, SPAN), F32),
            jax.ShapeDtypeStruct((count, 8, SPAN), F32),
        ],
        [
            pltpu.VMEM((count, 8, length), F32),
            pltpu.SemaphoreType.DMA((count,)),
            pltpu.SemaphoreType.DMA((count,)),
        ],
    )


def other_core(array):
    return lax.ppermute(array, "section", [(0, 1), (1, 0)])


def both_layers(array):
    core = lax.axis_index("section")
    theirs = other_core(array)
    return (
        jnp.where(core == 0, array, theirs),
        jnp.where(core == 0, theirs, array),
    )


IN_HBM = pl.BlockSpec(memory_space=pl.ANY)


def greet_all(sizes, ranks):
    barrier = pltpu.get_barrier_semaphore()
    total = 0
    for axis, size in sizes.items():
        for step in range(1, size):
            to = lax.rem(ranks[axis] + step, size)
            pl.semaphore_signal(barrier, inc=1, device_id={axis: to}, device_id_type=MESH)
            total += 1
    pl.semaphore_wait(barrier, total)


def push(axis, index, source, target, send_sem, recv_sem):
    return pltpu.make_async_remote_copy(
        src_ref=source,
        dst_ref=target,
        send_sem=send_sem,
        recv_sem=recv_sem,
        device_id={axis: index},
        device_id_type=MESH,
    )


def start_kernel(
    sizes,
    small,
    hidden,
    bundle,
    out_weight,
    normed,
    columns,
    rows_out,
    smalls,
    local_sem,
    split_send,
    split_recv,
    copy_send,
    copy_recv,
    core_send,
    core_recv,
    out_send,
    out_recv,
    small_send,
    small_recv,
    small_core_send,
    small_core_recv,
    right_send,
    left_send,
    block_recv,
):
    ranks = {axis: lax.axis_index(axis) for axis in sizes}
    core, rank, stream = ranks["section"], ranks["seq"], ranks["dp"]
    count, copies = sizes["seq"], sizes["dp"]
    part = bundle.shape[1]
    depth = part * copies
    greet_all(sizes, ranks)

    smalls[core, rank] = small[...]
    for step in range(1, count):
        to = lax.rem(rank + step, count)
        place = smalls.at[core, rank]
        push("seq", to, place, place, small_send.at[step], small_recv.at[rank]).start()
    push(
        "section", 1 - core, out_weight.at[0], rows_out.at[core], out_send, out_recv
    ).start()

    def slot(origin, share):
        return pl.ds(pl.multiple_of(origin * depth + share * part, part), part)

    def split_copy(step):
        to = lax.rem(rank + step, count)
        return push(
            "seq",
            to,
            bundle.at[to],
            columns.at[core, slot(rank, stream)],
            split_send.at[step],
            split_recv.at[rank],
        )

    for step in range(count - 1, 0, -1):
        split_copy(step).start()
    own = pltpu.make_async_copy(bundle.at[rank], columns.at[core, slot(rank, stream)], local_sem)
    own.start()

    def spread_slot(origin, held=None):
        place = columns.at[core, slot(origin, stream)]
        source = place if held is None else held
        for step in range(1, copies):
            to = lax.rem(stream + step, copies)
            push(
                "dp", to, source, place, copy_send.at[origin, step], copy_recv.at[origin, stream]
            ).start()
        push(
            "section",
            1 - core,
            source,
            place,
            core_send.at[origin, stream],
            core_recv.at[origin, stream],
        ).start()

    spread_slot(rank, bundle.at[rank])
    rows_out[core] = out_weight[0]

    for step in range(1, count):
        origin = lax.rem(rank + step, count)
        place = smalls.at[core, origin]
        push("seq", origin, place, place, small_send.at[step], small_recv.at[origin]).wait_recv()
    push(
        "section", 1 - core, smalls.at[core], smalls.at[core], small_core_send, small_core_recv
    ).start()

    for step in range(1, count):
        origin = lax.rem(rank + step, count)
        place = columns.at[core, slot(origin, stream)]
        push("seq", origin, place, place, split_send.at[step], split_recv.at[origin]).wait_recv()
        spread_slot(origin)

    push(
        "section",
        1 - core,
        smalls.at[1 - core],
        smalls.at[1 - core],
        small_core_send,
        small_core_recv,
    ).wait_recv()
    gain = jnp.concatenate([smalls[0, origin, 5:6, :depth] for origin in range(count)], axis=1)
    normed[rank] = norm_rows(hidden[core].astype(F32), gain).astype(BF16)

    def block_copy(block, sign):
        return push(
            "seq",
            rank + sign,
            normed.at[block],
            normed.at[block],
            (right_send if sign > 0 else left_send).at[block],
            block_recv.at[block],
        )

    def open_end(sign):
        return rank < count - 1 if sign > 0 else rank > 0

    for sign in (1, -1):

        @pl.when(open_end(sign))
        def _():
            block_copy(rank, sign).start()

    for away in range(1, count):
        for sign in (1, -1):
            block = rank - sign * away

            @pl.when(block >= 0 if sign > 0 else block < count)
            def _():
                block_copy(block, sign).wait_recv()

                @pl.when(open_end(sign))
                def _():
                    block_copy(block, sign).start()

    for origin in range(count):
        for step in range(1, copies):
            share = lax.rem(stream + step, copies)
            place = columns.at[core, slot(origin, share)]
            push(
                "dp", share, place, place, copy_send.at[origin, step], copy_recv.at[origin, share]
            ).wait_recv()
            push(
                "section",
                1 - core,
                place,
                place,
                core_send.at[origin, share],
                core_recv.at[origin, share],
            ).start()
    for origin in range(count):
        for share in range(copies):
            theirs = columns.at[1 - core, slot(origin, share)]
            copy = push(
                "section",
                1 - core,
                theirs,
                theirs,
                core_send.at[origin, share],
                core_recv.at[origin, share],
            )
            copy.wait_recv()
            copy.wait_send()
        for step in range(1, copies):
            place = columns.at[core, slot(origin, stream)]
            push(
                "dp", stream, place, place, copy_send.at[origin, step], copy_recv.at[origin, stream]
            ).wait_send()
    own.wait()
    rows_copy = push(
        "section", 1 - core, out_weight.at[0], rows_out.at[1 - core], out_send, out_recv
    )
    rows_copy.wait_recv()
    rows_copy.wait_send()
    push(
        "section", 1 - core, smalls.at[core], smalls.at[core], small_core_send, small_core_recv
    ).wait_send()
    for step in range(1, count):
        to = lax.rem(rank + step, count)
        place = smalls.at[core, rank]
        push("seq", to, place, place, small_send.at[step], small_recv.at[rank]).wait_send()
        split_copy(step).wait_send()
    for block in range(count):

        @pl.when((block <= rank) & (rank < count - 1))
        def _():
            block_copy(block, 1).wait_send()

        @pl.when((block >= rank) & (rank > 0))
        def _():
            block_copy(block, -1).wait_send()


def axis_sizes():
    return {axis: lax.axis_size(axis) for axis in ("section", "seq", "dp")}


def start(small, hidden, bundle, out_weight):
    sizes = axis_sizes()
    count, copies = sizes["seq"], sizes["dp"]
    depth, inner, width = bundle.shape[1] * copies, out_weight.shape[1], out_weight.shape[2]
    dma = pltpu.SemaphoreType.DMA
    return pl.pallas_call(
        functools.partial(start_kernel, sizes),
        out_shape=[
            jax.ShapeDtypeStruct((count,) + hidden.shape[1:], BF16),
            jax.ShapeDtypeStruct((2, count * depth, 2 * inner + 3 * STATE), BF16),
            jax.ShapeDtypeStruct((2, inner, width), BF16),
            jax.ShapeDtypeStruct((2, count) + small.shape, F32),
        ],
        in_specs=[IN_VMEM, IN_VMEM, IN_HBM, IN_VMEM],
        out_specs=[IN_VMEM, IN_HBM, IN_VMEM, IN_VMEM],
        scratch_shapes=[
            dma,
            dma((count,)),
            dma((count,)),
            dma((count, copies)),
            dma((count, copies)),
            dma((count, copies)),
            dma((count, copies)),
            dma,
            dma,
            dma((count,)),
            dma((count,)),
            dma,
            dma,
            dma((count,)),
            dma((count,)),
            dma((count,)),
        ],
        compiler_params=pltpu.CompilerParams(
            collective_id=5, has_side_effects=True, vmem_limit_bytes=LINE_VMEM
        ),
        name="start",
    )(small, hidden, bundle, out_weight)


def small_rows(conv_weight, conv_bias, norm_gain):
    part = conv_bias.shape[1]
    pad = -part % 128
    rows = jnp.concatenate([conv_weight[0], conv_bias], axis=0).astype(F32)
    rows = jnp.pad(rows, ((0, 0), (0, pad)))
    gain = jnp.pad(norm_gain.astype(F32), ((0, 0), (0, part + pad - norm_gain.shape[1])))
    return jnp.concatenate([rows, gain, jnp.zeros((2, part + pad), F32)], axis=0)


def step_columns(rows, whole_inner):
    rows = rows[:, 2 * whole_inner :]
    return jnp.pad(rows, ((0, 0), (0, 3 * STATE - rows.shape[1])))


def layer_facts(smalls, step_bias, decay_log, skip_gain, gate_gain, part, depth):
    count = lax.axis_size("seq")
    rank = lax.axis_index("seq")
    inner = gate_gain.shape[1]
    heads = step_bias.shape[1]
    own = jnp.concatenate([step_bias, decay_log, skip_gain], axis=0)
    own = jnp.pad(own, ((0, 5), (0, 128 - heads)))
    own = both_layers(own.astype(F32))
    gate = both_layers(jnp.broadcast_to(gate_gain, (8, inner)).astype(F32))
    facts = []
    for layer in range(2):
        rows = smalls[layer]
        taps = rows[:, :, :part].transpose(1, 0, 2).reshape(8, count * part)
        gain = jnp.broadcast_to(rows[:, 5, :depth].reshape(1, -1), (8, count * depth))
        facts.append(
            (
                lax.dynamic_slice_in_dim(taps, rank * inner, inner, 1),
                taps[:, count * inner :],
                own[layer],
                gate[layer],
                gain,
            )
        )
    return facts


def column_bundle(in_weight, inner):
    count, copies = lax.axis_size("seq"), lax.axis_size("dp")
    part = in_weight.shape[1] // copies
    rows = lax.dynamic_slice_in_dim(in_weight[0], lax.axis_index("dp") * part, part, 0)
    kinds = [
        rows[:, kind * count * inner : (kind + 1) * count * inner]
        .reshape(part, count, inner)
        .transpose(1, 0, 2)
        for kind in range(2)
    ]
    rest = step_columns(rows, count * inner)
    kinds.append(jnp.broadcast_to(rest[None], (count,) + rest.shape))
    return jnp.concatenate(kinds, axis=2)


def columns_by_collectives(in_weight, inner):
    count = lax.axis_size("seq")
    depth = in_weight.shape[1]
    rows = in_weight[0]
    kinds = []
    for kind in range(2):
        part = rows[:, kind * count * inner : (kind + 1) * count * inner]
        part = part.reshape(depth, count, inner).transpose(1, 0, 2)
        part = lax.all_to_all(part, "seq", split_axis=0, concat_axis=0, tiled=True)
        kinds.append(both_layers(part.reshape(count * depth, inner)))
    step_weight = step_columns(rows, count * inner)
    kinds.append(both_layers(lax.all_gather(step_weight, "seq", axis=0, tiled=True)))
    return [[(kind[layer], whole(kind[layer])) for kind in kinds] for layer in range(2)]


class Flow:
    def __init__(self, sizes, ranks, left_in, right_in, left_out, right_out, final, out_final, scratch, sems):
        self.sizes, self.ranks = sizes, ranks
        self.left_in, self.right_in, self.left_out, self.right_out = (
            left_in,
            right_in,
            left_out,
            right_out,
        )
        self.final, self.out_final = final, out_final
        self.full, self.got, self.parts, self.sums = scratch
        (
            self.core_send,
            self.core_recv,
            self.part_send,
            self.part_recv,
            self.z_send,
            self.z_recv,
            self.give_send,
            self.give_recv,
        ) = sems
        self.count, self.copies = sizes["seq"], sizes["dp"]
        self.core, self.rank, self.stream = ranks["section"], ranks["seq"], ranks["dp"]
        self.depth = self.full.shape[1]
        self.half = self.depth // 2
        self.share = self.half // self.copies
        self.units = self.full.shape[0]

    def half_rows(self, core):
        return pl.ds(pl.multiple_of(core * self.half, self.half), self.half)

    def multiply(self, unit):
        depth = self.depth
        tile = 384
        full = self.full

        def columns(left, right, at):
            def body(index, _):
                low = pl.multiple_of(index * tile, tile)
                full[unit, :, pl.ds(low, tile)] = mm_tn(left, right[:, pl.ds(low, tile)]).astype(BF16)
                return 0

            lax.fori_loop(0, right.shape[1] // tile, body, 0)

        @pl.when(unit < self.count)
        def _():
            at = pl.multiple_of(unit * depth, depth)
            columns(self.left_in[:, pl.ds(at, depth)], self.right_in, at)

        @pl.when(unit >= self.count)
        def _():
            at = pl.multiple_of((unit - self.count) * depth, depth)
            columns(self.left_out[:, pl.ds(at, depth)], self.right_out, at)

    def core_copy(self, unit):
        return push(
            "section",
            1 - self.core,
            self.full.at[unit, self.half_rows(1 - self.core)],
            self.got.at[unit],
            self.core_send.at[unit],
            self.core_recv.at[unit],
        )

    def part_rows(self, member):
        start = self.core * self.half + member * self.share
        return pl.ds(pl.multiple_of(start, self.share), self.share)

    def bits(self, unit):
        first = 1 + lax.rem(unit, 2)
        return first, 3 - first

    def flip(self, bit):
        low = lax.rem(lax.div(self.stream, bit), 2)
        return self.stream + bit - 2 * bit * low

    def step_copy(self, unit, step):
        first, second = self.bits(unit)
        partner, opposite = self.flip(first), self.flip(second)
        member = (partner, partner + opposite - self.stream, opposite)[step]
        return push(
            "dp",
            opposite if step == 2 else partner,
            self.full.at[unit, self.part_rows(member)],
            self.parts.at[unit, step],
            self.part_send.at[unit, step],
            self.part_recv.at[unit, step],
        )

    def z_copy(self, unit):
        return push(
            "seq",
            unit,
            self.sums.at[unit],
            self.final.at[self.core, self.rank],
            self.z_send.at[unit],
            self.z_recv.at[self.rank],
        )

    def first(self, unit):
        self.multiply(unit)
        self.core_copy(unit).start()

    def second(self, unit):
        self.core_copy(unit).wait_recv()
        rows = self.half_rows(self.core)
        total = self.full[unit, rows, :].astype(F32) + self.got[unit].astype(F32)
        self.full[unit, rows, :] = total.astype(BF16)
        self.step_copy(unit, 0).start()
        self.step_copy(unit, 1).start()

    def third(self, unit):
        opposite = self.flip(self.bits(unit)[1])
        for step, member in ((1, opposite), (0, self.stream)):
            self.step_copy(unit, step).wait_recv()
            rows = self.part_rows(member)
            total = self.full[unit, rows, :].astype(F32) + self.parts[unit, step].astype(F32)
            self.full[unit, rows, :] = total.astype(BF16)
            if step:
                self.step_copy(unit, 2).start()

    def fourth(self, unit):
        self.step_copy(unit, 2).wait_recv()
        total = self.full[unit, self.part_rows(self.stream), :].astype(F32)
        total = (total + self.parts[unit, 2].astype(F32)).astype(BF16)

        @pl.when(unit < self.count)
        def _():
            @pl.when(unit == self.rank)
            def _():
                self.final[self.core, self.rank] = total

            @pl.when(unit != self.rank)
            def _():
                self.sums[unit] = total
                self.z_copy(unit).start()

        @pl.when(unit >= self.count)
        def _():
            self.out_final[self.core, unit - self.count] = total[:, : self.out_final.shape[3]]

    LAGS = (0, 1, 4, 6)

    def turn(self, turn, pace):
        for stage, lag in zip((self.first, self.second, self.third, self.fourth), self.LAGS):
            at = turn - lag

            @pl.when((at >= 0) & (at < self.units * pace) & (lax.rem(at, pace) == 0))
            def _():
                stage(lax.div(at, pace))

    def turns(self, pace):
        return (self.units - 1) * pace + self.LAGS[3] + 1

    def finals_here(self, layer):
        for step in range(1, self.count):
            origin = lax.rem(self.rank + step, self.count)
            place = self.final.at[self.core, origin]
            push("seq", origin, place, place, self.z_send.at[origin], self.z_recv.at[origin]).wait_recv()
        for kind in range(2):

            @pl.when(self.core != layer)
            def _():
                self.give_copy(kind).start()

    def give_copy(self, kind):
        final = (self.final, self.out_final)[kind]
        place = final.at[self.core]
        return push(
            "section", 1 - self.core, place, place, self.give_send.at[kind], self.give_recv.at[kind]
        )

    def finals_given(self, layer):
        for kind in range(2):
            final = (self.final, self.out_final)[kind]

            @pl.when(self.core == layer)
            def _():
                place = final.at[1 - self.core]
                push(
                    "section", 1 - self.core, place, place, self.give_send.at[kind], self.give_recv.at[kind]
                ).wait_recv()

            @pl.when(self.core != layer)
            def _():
                self.give_copy(kind).wait_send()

    def settle(self):
        def body(unit, _):
            self.core_copy(unit).wait_send()
            for step in range(3):
                self.step_copy(unit, step).wait_send()

            @pl.when((unit < self.count) & (unit != self.rank))
            def _():
                self.z_copy(unit).wait_send()

            return 0

        lax.fori_loop(0, self.units, body, 0)


class Square:
    def __init__(self, member, sources, slots, sems):
        self.member, self.sources, self.slots = member, sources, slots
        self.own_sem, self.send, self.recv = sems

    def flip(self, bit):
        return self.member + bit - 2 * bit * lax.rem(lax.div(self.member, bit), 2)

    def own_copy(self, kind):
        return pltpu.make_async_copy(
            self.sources[kind], self.slots[kind].at[self.member], self.own_sem.at[kind]
        )

    def near_copy(self, kind, way):
        return push(
            "dp",
            self.flip(1 + way),
            self.sources[kind],
            self.slots[kind].at[self.member],
            self.send.at[kind, way],
            self.recv.at[kind, way],
        )

    def far_copy(self, kind, way):
        place = self.slots[kind].at[self.flip(1 + way), way]
        return push(
            "dp", self.flip(2 - way), place, place, self.send.at[kind, 2 + way], self.recv.at[kind, 2 + way]
        )

    def begin(self, kind):
        self.own_copy(kind).start()
        for way in range(2):
            self.near_copy(kind, way).start()

    def middle(self, kind):
        for way in range(2):
            self.near_copy(kind, way).wait_recv()
            self.far_copy(kind, way).start()

    def end(self, kind):
        for way in range(2):
            self.far_copy(kind, way).wait_recv()
        for way in range(2):
            self.near_copy(kind, way).wait_send()
            self.far_copy(kind, way).wait_send()
        self.own_copy(kind).wait()


def square_sems():
    dma = pltpu.SemaphoreType.DMA
    return [dma((2,)), dma((2, 4)), dma((2, 4))]


def flow_shapes(sizes, depth, inner, width, wide):
    units = sizes["seq"] + inner // depth
    share = depth // 2 // sizes["dp"]
    dma = pltpu.SemaphoreType.DMA
    scratch = [
        pltpu.VMEM((units, depth, wide), BF16),
        pltpu.VMEM((units, depth // 2, wide), BF16),
        pltpu.VMEM((units, 3, share, wide), BF16),
        pltpu.VMEM((sizes["seq"], share, wide), BF16),
    ]
    sems = [
        dma((units,)),
        dma((units,)),
        dma((units, 3)),
        dma((units, 3)),
        dma((sizes["seq"],)),
        dma((sizes["seq"],)),
        dma((2,)),
        dma((2,)),
    ]
    finals = [
        jax.ShapeDtypeStruct((2, sizes["seq"], share, wide), BF16),
        jax.ShapeDtypeStruct((2, inner // depth, share, width), BF16),
    ]
    return scratch, sems, finals


def sum_backward_kernel(
    sizes,
    with_flow,
    whole_inner,
    part,
    stream,
    gain,
    outer,
    product,
    *rest,
):
    ranks = {axis: lax.axis_index(axis) for axis in sizes}
    rank, count = ranks["seq"], sizes["seq"]
    if with_flow:
        factors, rest = rest[:4], rest[4:]
        finals, rest = rest[4:6], rest[:4] + rest[6:]
    spread, means, grad, gain_grad, inbox, columns, *rest = rest
    if with_flow:
        scratch, rest = rest[:4], rest[4:]
    row_send, row_recv, *sems = rest
    greet_all(sizes if with_flow else {"seq": count}, ranks)
    line = Line(count, rank, part, inbox, spread, sems[:5])
    flow = None
    if with_flow:
        flow = Flow(sizes, ranks, *factors, *finals, scratch, sems[5:])
    gain_grad[...] = jnp.zeros_like(gain_grad)
    share = (count, rank, means.at[rank], means, row_send, row_recv)

    def own_piece(piece, total):
        rows = pl.ds(pl.multiple_of(piece * PIECE, PIECE), PIECE)
        back, gain_part = norm_back(stream[rows, :].astype(F32), gain[0:1, :], total)
        gain_grad[0:1, :] += gain_part
        whole = outer[rows, :].astype(F32) + back
        grad[rows, :] = whole
        low = whole.astype(BF16)
        spread[rank, rows, :] = low
        along_rows = jnp.sum(low.astype(F32) * product[rows, :], axis=1, keepdims=True)
        columns[rows, :] = jnp.broadcast_to(along_rows / whole_inner, (PIECE, 128))

    def after_own():
        means[rank] = jnp.transpose(columns[...])[0:8, :]
        share_with_all(*share)

    line.run(SPAN // PIECE, own_piece, None, after_own, flow)
    if with_flow:
        flow.finals_here(1)
    share_wait_recv(*share)
    share_wait_send(*share)
    if with_flow:
        flow.finals_given(1)
        flow.settle()


def sum_backward(part, stream, gain, outer, product, whole_inner, grads_of):
    sizes = axis_sizes()
    count = sizes["seq"]
    length, width = part.shape
    pieces = SPAN // PIECE
    factors, scratch, sems, finals = [], [], [], []
    if grads_of is not None:
        factors = list(grads_of)
        scratch, sems, finals = flow_shapes(
            sizes, width // count, factors[2].shape[1], width, factors[1].shape[1]
        )
    return line_call(
        functools.partial(sum_backward_kernel, sizes, grads_of is not None, whole_inner),
        "sum_backward",
        2,
        [part, stream, gain, outer, product] + factors,
        [
            jax.ShapeDtypeStruct((count, SPAN, width), BF16),
            jax.ShapeDtypeStruct((count, 8, SPAN), F32),
            jax.ShapeDtypeStruct((SPAN, width), F32),
            jax.ShapeDtypeStruct((8, width), F32),
        ]
        + finals,
        [
            pltpu.VMEM((count + 1, SPAN, width), BF16),
            pltpu.VMEM((SPAN, 128), F32),
        ]
        + scratch
        + [pltpu.SemaphoreType.DMA((count,)), pltpu.SemaphoreType.DMA((count,))]
        + line_sems(count, pieces)
        + sems,
    )


SMALL_COLUMNS = 1280


def sum_last_kernel(
    sizes,
    part,
    stream,
    gain,
    outer,
    left_in,
    right_in,
    left_out,
    right_out,
    small,
    gain_grad_1,
    grad,
    halves_0,
    halves_out_0,
    smalls,
    inbox,
    gain_grad,
    final,
    out_final,
    full,
    got,
    parts,
    sums,
    packed,
    theirs,
    dp_sum,
    dp_slots,
    *sems,
):
    ranks = {axis: lax.axis_index(axis) for axis in sizes}
    core, rank, member = ranks["section"], ranks["seq"], ranks["dp"]
    count, copies = sizes["seq"], sizes["dp"]
    greet_all(sizes, ranks)
    line = Line(count, rank, part, inbox, None, tuple(sems[:2]) + (None,) * 3)
    flow = Flow(
        sizes,
        ranks,
        left_in,
        right_in,
        left_out,
        right_out,
        final,
        out_final,
        (full, got, parts, sums),
        sems[2:10],
    )
    square = Square(member, (final, out_final), (halves_0, halves_out_0), sems[10:13])
    s_core_send, s_core_recv, s_dp_send, s_dp_recv, s_z_send, s_z_recv = sems[13:]
    gain_grad[...] = jnp.zeros_like(gain_grad)

    def own_piece(piece, total):
        rows = pl.ds(pl.multiple_of(piece * PIECE, PIECE), PIECE)
        back, gain_part = norm_back(stream[rows, :].astype(F32), gain[0:1, :], total)
        gain_grad[0:1, :] += gain_part
        grad[rows, :] = outer[rows, :].astype(F32) + back

    def s_core_copy():
        return push("section", 1 - core, packed, theirs, s_core_send, s_core_recv)

    def s_dp_copy(step):
        to = lax.rem(member + step, copies)
        return push(
            "dp", to, dp_sum, dp_slots.at[member], s_dp_send.at[step], s_dp_recv.at[member]
        )

    def s_z_copy(step):
        to = lax.rem(rank + step, count)
        return push(
            "seq", to, smalls.at[rank], smalls.at[rank], s_z_send.at[step], s_z_recv.at[rank]
        )

    def after_own():
        packed[...] = small[...]
        wide = SMALL_COLUMNS - 256
        for layer, source in ((0, gain_grad), (1, gain_grad_1)):
            for row in range(source.shape[1] // 256):
                packed[layer, row : row + 1, wide:] = source[0:1, row * 256 : (row + 1) * 256]
        s_core_copy().start()

    line.run(SPAN // PIECE, own_piece, None, after_own, flow, pace=2)
    flow.finals_here(0)
    s_core_copy().wait_recv()
    dp_sum[...] = packed[...] + theirs[...]
    flow.finals_given(0)

    @pl.when(core == 0)
    def _():
        square.begin(0)
        square.begin(1)

    for step in range(1, copies):
        s_dp_copy(step).start()
    total = dp_sum[...]
    for step in range(1, copies):
        origin = lax.rem(member + step, copies)
        place = dp_slots.at[origin]
        push("dp", origin, place, place, s_dp_send.at[step], s_dp_recv.at[origin]).wait_recv()
        total = total + dp_slots[origin]
    smalls[rank] = total
    for step in range(1, count):
        s_z_copy(step).start()
    for step in range(1, count):
        origin = lax.rem(rank + step, count)
        place = smalls.at[origin]
        push("seq", origin, place, place, s_z_send.at[step], s_z_recv.at[origin]).wait_recv()

    @pl.when(core == 0)
    def _():
        square.middle(0)
        square.middle(1)
        square.end(0)
        square.end(1)

    s_core_copy().wait_send()
    for step in range(1, copies):
        s_dp_copy(step).wait_send()
    for step in range(1, count):
        s_z_copy(step).wait_send()
    flow.settle()


def sum_last(part, stream, gain, outer, grads_of, small, gain_grad_1):
    sizes = axis_sizes()
    count, copies = sizes["seq"], sizes["dp"]
    length, width = part.shape
    pieces = SPAN // PIECE
    left_in, right_in, left_out, right_out = grads_of
    depth, inner, wide = width // count, left_out.shape[1], right_in.shape[1]
    scratch, sems, finals = flow_shapes(sizes, depth, inner, width, wide)
    dma = pltpu.SemaphoreType.DMA
    halves = [jax.ShapeDtypeStruct((copies,) + f.shape, f.dtype) for f in finals]
    small_shape = pltpu.VMEM((2, 8, SMALL_COLUMNS), F32)
    operands = [
        part, stream, gain, outer, left_in, right_in, left_out, right_out, small, gain_grad_1,
    ]
    return pl.pallas_call(
        functools.partial(sum_last_kernel, sizes),
        out_shape=[jax.ShapeDtypeStruct((SPAN, width), F32)]
        + halves
        + [jax.ShapeDtypeStruct((count, 2, 8, SMALL_COLUMNS), F32)],
        in_specs=[IN_VMEM] * len(operands),
        out_specs=[IN_VMEM] + [IN_HBM] * 2 + [IN_VMEM],
        scratch_shapes=[
            pltpu.VMEM((count + 1, SPAN, width), BF16),
            pltpu.VMEM((8, width), F32),
        ]
        + [pltpu.VMEM(f.shape, f.dtype) for f in finals]
        + scratch
        + [small_shape, small_shape, small_shape, pltpu.VMEM((copies, 2, 8, SMALL_COLUMNS), F32)]
        + line_sems(count, pieces)[:2]
        + sems
        + square_sems()
        + [
            dma,
            dma,
            dma((copies,)),
            dma((copies,)),
            dma((count,)),
            dma((count,)),
        ],
        compiler_params=pltpu.CompilerParams(
            collective_id=3, has_side_effects=True, vmem_limit_bytes=LINE_VMEM
        ),
        name="sum_last",
    )(*operands)


def grads_by_collectives(in_parts, out_part, inner):
    core = lax.axis_index("section")
    count = lax.axis_size("seq")

    def to_core(pair):
        theirs = other_core(jnp.where(core == 0, pair[1], pair[0]).astype(BF16))
        return (jnp.where(core == 0, pair[0], pair[1]) + theirs.astype(F32)).astype(BF16)

    gate, x, rest = (to_core(pair) for pair in in_parts)
    out = to_core(out_part)
    depth = gate.shape[0] // count

    def rows_of(part):
        part = part.reshape(count, depth, -1)
        part = lax.all_to_all(part, "seq", split_axis=0, concat_axis=0, tiled=True)
        return lax.psum(part, "dp").astype(F32)

    gate, x, rest = rows_of(gate), rows_of(x), rows_of(rest)
    columns = [part.transpose(1, 0, 2).reshape(depth, -1) for part in (gate, x)]
    return jnp.concatenate(columns + [jnp.sum(rest, axis=0)], axis=1), lax.psum(out, "dp").astype(F32)


def local(
    hidden_in,
    doc_starts,
    cotangent,
    norm_gain,
    in_weight,
    conv_weight,
    conv_bias,
    step_bias,
    decay_log,
    skip_gain,
    gate_gain,
    out_weight,
):
    sizes = axis_sizes()
    core = lax.axis_index("section")
    rank = lax.axis_index("seq")
    count, copies = sizes["seq"], sizes["dp"]
    inner = out_weight.shape[1]
    heads = step_bias.shape[1]
    whole_inner = inner * count
    depth = in_weight.shape[1]
    part = conv_bias.shape[1]
    tokens = hidden_in.shape[1]
    regular = inner % depth == 0 and depth % 128 == 0 and depth % (32 * copies) == 0 and copies == 4

    gather = lambda array: lax.all_gather(array, "seq", axis=0, tiled=True)
    stream = lax.dynamic_index_in_dim(hidden_in, core, 0, keepdims=False)
    outer = lax.dynamic_index_in_dim(cotangent, core, 0, keepdims=False)
    starts = lax.dynamic_index_in_dim(doc_starts, core, 0, keepdims=False)
    small = small_rows(conv_weight, conv_bias, norm_gain)
    if regular:
        normed_0, columns, out_rows, smalls = start(
            small, hidden_in, column_bundle(in_weight, inner), out_weight
        )
        normed_0 = normed_0.reshape(count * tokens, -1)
        columns = [[(columns, of_layer(columns, layer))] for layer in range(2)]
        out_rows = [(out_rows, of_layer(out_rows, layer)) for layer in range(2)]
    else:
        smalls = lax.all_gather(lax.all_gather(small, "seq", axis=0), "section", axis=0)
        columns = columns_by_collectives(in_weight, inner)
        out_rows = [(array, whole(array)) for array in both_layers(out_weight[0])]
    facts = layer_facts(smalls, step_bias, decay_log, skip_gain, gate_gain, part, depth)
    gains = [fact[4] for fact in facts]
    if not regular:
        normed_0 = gather(norm_rows(stream.astype(F32), gains[0][0:1]).astype(BF16))
    layers = [(columns[layer],) + facts[layer][:4] + (out_rows[layer],) for layer in range(2)]

    outer_after, normed_0 = lax.optimization_barrier((outer, normed_0))
    dh_whole = gather(outer_after)
    fwd_0 = run_forward(starts, normed_0, layers[0])
    normed_1, scales_0, hidden_1, product_0 = sum_forward(
        fwd_0[6], fwd_0[7], stream, gains[1], whole_inner
    )
    normed_1 = normed_1.reshape(normed_0.shape)
    fwd_1 = run_forward(starts, normed_1, layers[1], dh_whole)
    scales_1, means_1 = sum_stats(fwd_1[7], whole_inner)

    back_1 = run_backward(starts, dh_whole, scales_1, means_1, layers[1], fwd_1[:6])
    kinds = len(columns[0])
    gated_1, dnormed_1 = back_1[kinds : kinds + 2]
    grads_of = (normed_1, back_1[0], gated_1, dh_whole) if regular else None
    dh_0, means_0, input_grad_1, gain_grad_1, *mine_1 = sum_backward(
        dnormed_1, hidden_1, gains[1], outer, product_0, whole_inner, grads_of
    )
    own_dh_0 = lax.dynamic_index_in_dim(dh_0, rank, 0, keepdims=False)
    part_1, dh_0 = lax.optimization_barrier((fwd_1[6].astype(BF16), dh_0))
    product_1 = lax.psum_scatter(part_1, "seq", scatter_dimension=0, tiled=True)
    own_scale = lax.dynamic_index_in_dim(scales_1, rank, 0, keepdims=False)[0]
    hidden_2 = (hidden_1.astype(F32) + product_1.astype(F32) * own_scale[:, None]).astype(BF16)
    dh_0 = dh_0.reshape(dh_whole.shape)
    back_0 = run_backward(starts, dh_0, scales_0, means_0, layers[0], fwd_0[:6], mine_1)
    gated_0, dnormed_0 = back_0[kinds : kinds + 2]

    def packed(back):
        gx, gbc, gheads = back[kinds + 2 : kinds + 5]
        rest = jnp.concatenate([gbc[:5], jnp.pad(gheads[:2], ((0, 0), (0, 128))), gbc[7:]], axis=0)
        return jnp.concatenate([gx, rest, jnp.zeros((8, 256), F32)], axis=1)

    small_grads = jnp.stack([packed(back_0), packed(back_1)])
    if regular:
        grads_of = (normed_0, back_0[0], gated_0, dh_0)
        input_grad_0, halves_0, halves_out_0, smalls = sum_last(
            dnormed_0, stream, gains[0], own_dh_0, grads_of, small_grads, gain_grad_1
        )
        halves_1, halves_out_1 = back_0[-2:]
        halves = jnp.where(core == 0, halves_0, halves_1)
        halves_out = jnp.where(core == 0, halves_out_0, halves_out_1)

        def side_by_side(low, high):
            wide = halves[..., low:high].transpose(1, 0, 3, 2, 4)
            return wide.reshape(depth, -1).astype(F32)

        rest = jnp.sum(halves[..., 2 * inner :].astype(F32), axis=2).transpose(1, 0, 2, 3)
        rest = rest.reshape(depth, -1)
        grad_in = jnp.concatenate(
            [side_by_side(0, inner), side_by_side(inner, 2 * inner), rest], axis=1
        )
        grad_out = halves_out.transpose(2, 1, 0, 3, 4).reshape(inner, -1).astype(F32)
    else:
        input_grad_0, gain_grad_0 = sum_plain(dnormed_0, stream, gains[0], own_dh_0)
        pairs = [
            (mm_tn(normed_0, back_0[kind]), mm_tn(normed_1, back_1[kind])) for kind in range(kinds)
        ]
        grad_in, grad_out = grads_by_collectives(
            pairs, (mm_tn(gated_0, dh_0), mm_tn(gated_1, dh_whole)), inner
        )
        gain_rows = jnp.stack([gain_grad_0[0], gain_grad_1[0]]).reshape(2, -1, 256)
        small_grads = small_grads.at[:, : gain_rows.shape[1], inner + 256 :].set(gain_rows)
        smalls = lax.all_gather(lax.psum(small_grads, ("section", "dp")), "seq", axis=0)
    grad_in = grad_in[:, : in_weight.shape[2]]

    mine = lax.dynamic_index_in_dim(smalls, core, 1, keepdims=False)
    x_part = mine[:, :5, :inner].transpose(1, 0, 2).reshape(5, whole_inner)
    bc_part = jnp.sum(mine[:, :5, inner : inner + 256], axis=0)
    channels = lax.dynamic_slice_in_dim(
        jnp.concatenate([x_part, bc_part], axis=1), rank * part, part, 1
    )
    gain_rows = norm_gain.shape[1] * count // 256
    norm_grad = jnp.sum(mine[:, :gain_rows, inner + 256 :], axis=0).reshape(-1)
    norm_grad = lax.dynamic_slice_in_dim(norm_grad, rank * norm_gain.shape[1], norm_gain.shape[1], 0)
    own = lax.dynamic_index_in_dim(mine, rank, 0, keepdims=False)

    def by_layer(first, second):
        kept = jnp.where(core == 0, first, second)
        theirs = other_core(jnp.where(core == 0, second, first))
        return jnp.stack([jnp.where(core == 0, kept, theirs), jnp.where(core == 0, theirs, kept)])

    return (
        by_layer(hidden_1, hidden_2)[None],
        by_layer(input_grad_0, input_grad_1)[None],
        norm_grad[None],
        grad_in[None],
        channels[None, :TAPS],
        channels[TAPS:],
        own[5:6, inner : inner + heads],
        own[6:7, inner : inner + heads],
        jnp.sum(own[5, :inner].reshape(1, heads, HEAD), axis=2),
        own[6:7, :inner],
        grad_out[None],
    )


def solution(mesh):
    return jax.shard_map(
        local,
        mesh=mesh,
        in_specs=(
            P("dp", "seq", None),
            P("dp", None),
            P("dp", "seq", None),
            P("section", "seq"),
            P("section", "seq", None),
            P("section", None, "seq"),
            P("section", "seq"),
            P("section", "seq"),
            P("section", "seq"),
            P("section", "seq"),
            P("section", "seq"),
            P("section", "seq", None),
        ),
        out_specs=(
            P("section", "dp", "seq", None),
            P("section", "dp", "seq", None),
            P("section", "seq"),
            P("section", "seq", None),
            P("section", None, "seq"),
            P("section", "seq"),
            P("section", "seq"),
            P("section", "seq"),
            P("section", "seq"),
            P("section", "seq"),
            P("section", "seq", None),
        ),
        check_vma=False,
    )
```

```python
import functools

import jax
import jax.numpy as jnp
from jax import lax
from jax.experimental import pallas as pl
from jax.experimental.pallas import tpu as pltpu
from jax.sharding import PartitionSpec as P

SPAN = 256
HEAD = 64
STATE = 128
TAPS = 4
EPSILON = 1e-05
HIGHEST = lax.Precision.HIGHEST
F32 = jnp.float32
BF16 = jnp.bfloat16
FAR = -1e30


def mm(a, b):
    return jnp.dot(a, b, preferred_element_type=F32)


def mm_nt(a, b):
    return lax.dot_general(a, b, (((1,), (1,)), ((), ())), preferred_element_type=F32)


def mm_tn(a, b):
    return lax.dot_general(a, b, (((0,), (0,)), ((), ())), preferred_element_type=F32)


def exact(a, b):
    return lax.dot_general(
        a, b, (((1,), (0,)), ((), ())), precision=HIGHEST, preferred_element_type=F32
    )


def doc_of(starts_ref, position):
    total = jnp.zeros(position.shape, jnp.int32)
    for entry in range(starts_ref.shape[0]):
        total = total + (starts_ref[entry] <= position).astype(jnp.int32)
    return total


def tiles_of(width):
    return [(low, min(low + 128, width)) for low in range(0, width, 128)]


def spread_pair(columns, tile, width):
    rows = columns.shape[0]
    first = jnp.broadcast_to(columns[:, 2 * tile : 2 * tile + 1], (rows, width))
    if width <= HEAD:
        return first
    second = jnp.broadcast_to(columns[:, 2 * tile + 1 : 2 * tile + 2], (rows, width))
    lane = lax.broadcasted_iota(jnp.int32, (rows, width), 1)
    return jnp.where(lane < HEAD, first, second)


def block_facts(starts_ref, block, length):
    base = block * SPAN
    column = base + lax.broadcasted_iota(jnp.int32, (SPAN, 128), 0)
    doc_col = doc_of(starts_ref, column)
    before = []
    for lag in range(1, TAPS):
        same = (doc_of(starts_ref, column - lag) == doc_col) & (column >= lag)
        before.append(same.astype(F32))
    row = base + lax.broadcasted_iota(jnp.int32, (8, SPAN), 1)
    doc_row = doc_of(starts_ref, row)
    same_square = doc_col[:, 0:1] == doc_row[0:1, :]
    edge_before = jnp.full((8, 128), base - 1, jnp.int32)
    last_doc_before = doc_of(starts_ref, edge_before)[0:1, :]
    last_doc = doc_of(starts_ref, jnp.full((8, 128), base + SPAN - 1, jnp.int32))[0:1, :]
    carried = ((doc_col == last_doc_before) & (base > 0)).astype(F32)
    to_last = (doc_col == last_doc).astype(F32)
    return doc_col, column, before, same_square, carried, to_last


def taps_sum(ext_ref, low, high, before, kernel, bias):
    summed = ext_ref[pl.ds(8, SPAN), low:high] * kernel[TAPS - 1 : TAPS, low:high] + bias[0:1, low:high]
    for lag in range(1, TAPS):
        summed = summed + (
            ext_ref[pl.ds(8 - lag, SPAN), low:high]
            * before[lag - 1][:, : high - low]
            * kernel[TAPS - 1 - lag : TAPS - lag, low:high]
        )
    return summed


def sigmoid(value):
    return 1.0 / (1.0 + jnp.exp(-value))


def softplus(value):
    small = jnp.exp(-jnp.abs(value))
    series = small * (1.0 - small * (0.5 - small * (1.0 / 3.0)))
    return jnp.maximum(value, 0.0) + jnp.where(small < 0.01, series, jnp.log(1.0 + small))


def lower_ones():
    row = lax.broadcasted_iota(jnp.int32, (SPAN, SPAN), 0)
    col = lax.broadcasted_iota(jnp.int32, (SPAN, SPAN), 1)
    return row, col


def split_weights(inner, refs):
    if refs[0].shape[1] > inner:
        parts = [(0, inner), (inner, 2 * inner), (2 * inner, 2 * inner + 3 * STATE)]
        return [refs[0].at[:, low:high] for low, high in parts] + [refs[1:]]
    return [refs[0], refs[1], refs[2], refs[3:]]


def own_heads(columns, heads, sign):
    shift = lax.rem(128 + sign * heads * lax.axis_index("seq"), 128)
    return pltpu.roll(columns, shift, 1)


TOTAL, DELTA, GROWN, ENDING, BEFORE = 0, 1, 2, 3, 4


def forward_kernel(
    with_back,
    length,
    starts_ref,
    normed_ref,
    kx_ref,
    kbc_ref,
    heads_ref,
    gain_ref,
    wo_ref,
    *rest,
):
    inner = kx_ref.shape[1]
    wg_ref, wx_ref, wbc_ref, rest = split_weights(inner, rest)
    if with_back:
        dh_ref, rest = rest[0], rest[1:]
    (
        gate_ref,
        x_ref,
        bc_ref,
        dt_ref,
        scan_ref,
        state_ref,
        part_ref,
        stat_ref,
        ext_x,
        ext_bc,
        memory,
        gu_ref,
    ) = rest
    block = pl.program_id(0)

    @pl.when(block == 0)
    def _():
        ext_x[...] = jnp.zeros_like(ext_x)
        ext_bc[...] = jnp.zeros_like(ext_bc)
        memory[...] = jnp.zeros_like(memory)

    @pl.when(block > 0)
    def _():
        ext_x[0:8, :] = ext_x[SPAN : SPAN + 8, :]
        ext_bc[0:8, :] = ext_bc[SPAN : SPAN + 8, :]

    normed = normed_ref[...]
    bcdt = mm(normed, wbc_ref[...]).astype(BF16)
    bc_ref[...] = bcdt[:, : 2 * STATE]
    ext_bc[8 : SPAN + 8, :] = bcdt[:, : 2 * STATE].astype(F32)
    dt_low = own_heads(bcdt[:, 2 * STATE :].astype(F32), inner // HEAD, -1)
    dt_ref[...] = dt_low
    x_low = mm(normed, wx_ref[...]).astype(BF16)
    x_ref[...] = x_low
    ext_x[8 : SPAN + 8, :] = x_low.astype(F32)
    gate_low = mm(normed, wg_ref[...]).astype(BF16)
    gate_ref[...] = gate_low

    _, _, before, same_square, carried, to_last = block_facts(starts_ref, block, length)
    row, col = lower_ones()
    lower = (row >= col).astype(F32)
    keep = jnp.where(same_square & (row >= col), 0.0, FAR)

    delta = softplus(dt_low + heads_ref[0:1, :])
    rate = -jnp.exp(heads_ref[1:2, :]) * delta
    total = exact(lower, rate)
    total_rows = jnp.transpose(total)
    grown = carried * jnp.exp(total)
    last_total = total[SPAN - 1 : SPAN, :]
    ending = to_last * jnp.exp(last_total - total)
    carry_last = grown[SPAN - 1 : SPAN, :]

    kbc = kbc_ref[...]
    b_conv = taps_sum(ext_bc, 0, STATE, before, kbc, kbc[TAPS : TAPS + 1])
    c_conv = taps_sum(ext_bc, STATE, 2 * STATE, before, kbc, kbc[TAPS : TAPS + 1])
    b_low = (b_conv * sigmoid(b_conv)).astype(BF16)
    c_low = (c_conv * sigmoid(c_conv)).astype(BF16)
    scores = mm_nt(c_low, b_low)
    b_flip = jnp.transpose(b_low.astype(F32)).astype(BF16)

    state_ref[0] = memory[...].astype(BF16)
    kx = kx_ref[...]
    squares = jnp.zeros((SPAN, 128), F32)
    for tile, (low, high) in enumerate(tiles_of(inner)):
        width = high - low
        lane = lax.broadcasted_iota(jnp.int32, (SPAN, width), 1)
        conv = taps_sum(ext_x, low, high, before, kx, kx[TAPS : TAPS + 1])
        values = conv * sigmoid(conv)
        weighted = spread_pair(delta, tile, width) * values
        w_low = weighted.astype(BF16)
        mixed = None
        for half in range(width // HEAD):
            head = 2 * tile + half
            decay = jnp.exp(total[:, head : head + 1] - total_rows[head : head + 1, :] + keep)
            part = mm((scores * decay).astype(BF16), w_low)
            mixed = part if mixed is None else jnp.where(lane < HEAD, mixed, part)
        mem = memory[:, low:high]
        mixed = mixed + mm(c_low, mem.astype(BF16)) * spread_pair(grown, tile, width)
        scan_ref[:, low:high] = mixed
        fresh = mm(b_flip, (weighted * spread_pair(ending, tile, width)).astype(BF16))
        memory[:, low:high] = mem * spread_pair(carry_last, tile, width) + fresh
        mixed = (
            (mixed + spread_pair(heads_ref[2:3, :], tile, width) * values).astype(BF16).astype(F32)
        )
        gate = gate_ref[:, low:high].astype(F32)
        g = mixed * (gate * sigmoid(gate))
        if width == 128:
            squares = squares + g * g
        else:
            squares = squares + jnp.concatenate([g * g, jnp.zeros((SPAN, 128 - width), F32)], axis=1)
        gu_ref[:, low:high] = (g * gain_ref[0:1, low:high]).astype(BF16)

    stats = jnp.sum(squares, axis=1, keepdims=True)
    gu = gu_ref[...]
    part_ref[...] = mm(gu, wo_ref[...]).astype(part_ref.dtype)
    if with_back:
        dgated = mm_nt(dh_ref[...], wo_ref[...])
        along = jnp.sum(dgated * gu.astype(F32), axis=1, keepdims=True)
        lane = lax.broadcasted_iota(jnp.int32, (SPAN, 128), 1)
        both = jnp.where(lane == 0, stats, jnp.where(lane == 1, along, 0.0))
    else:
        both = jnp.broadcast_to(stats, (SPAN, 128))
    stat_ref[...] = jnp.transpose(both)[0:8, :]


BACKWARD_STEPS = 5
AFTER, SCALE, MEAN, DTOTAL, DDELTA = 7, 10, 11, 12, 13


def backward_steps(
    step, is_last, block, length, starts_ref, dh, stat_refs, small_refs, weight_refs, wo_ref,
    saved_refs, grad_refs, sum_refs, scratch, finish,
):
    scale_ref, mean_ref = stat_refs
    kx_ref, kbc_ref, heads_ref, gain_ref = small_refs
    gate_ref, x_ref, xh_ref, bc_ref, bch_ref, dt_ref, scan_ref, state_ref = saved_refs
    dgate_ref, dx_ref, dbc_ref, gated_ref = grad_refs
    gx_ref, gbc_ref, gheads_ref = sum_refs
    (
        ext_x, ext_bc, ext_dx, ext_dbc, dmemory, columns, total_rows, squares, dgated_ref, pair_ref,
        c_flip_ref, dpair_ref, dlast_ref,
    ) = scratch
    inner = kx_ref.shape[1]

    @pl.when((step == 0) & is_last)
    def _():
        ext_dx[...] = jnp.zeros_like(ext_dx)
        ext_dbc[...] = jnp.zeros_like(ext_dbc)
        dmemory[...] = jnp.zeros_like(dmemory)
        gx_ref[...] = jnp.zeros_like(gx_ref)
        gbc_ref[...] = jnp.zeros_like(gbc_ref)
        gheads_ref[...] = jnp.zeros_like(gheads_ref)

    @pl.when((step == 0) & jnp.logical_not(is_last))
    def _():
        ext_dx[SPAN : SPAN + 8, :] = ext_dx[0:8, :]
        ext_dbc[SPAN : SPAN + 8, :] = ext_dbc[0:8, :]

    def convs(before):
        kbc = kbc_ref[...]
        return [
            taps_sum(ext_bc, low, low + STATE, before, kbc, kbc[TAPS : TAPS + 1])
            for low in (0, STATE)
        ]

    def before_rows():
        return [columns[BEFORE + lag] for lag in range(TAPS - 1)]

    @pl.when(step == 0)
    def _():
        ext_x[0:8, :] = xh_ref[8:16, :].astype(F32)
        ext_x[8 : SPAN + 8, :] = x_ref[...].astype(F32)
        ext_bc[0:8, :] = bch_ref[8:16, :].astype(F32)
        ext_bc[8 : SPAN + 8, :] = bc_ref[...].astype(F32)
        doc_col, column, before, same_square, carried, to_last = block_facts(
            starts_ref, block, length
        )
        for lag in range(1, TAPS):
            same = (doc_of(starts_ref, column + lag) == doc_col) & (column + lag < length)
            columns[AFTER + lag - 1] = same.astype(F32)
            columns[BEFORE + lag - 1] = before[lag - 1]
        row, col = lower_ones()
        squares[0] = jnp.where(same_square & (row <= col), 0.0, FAR)
        delta = softplus(dt_ref[...] + heads_ref[0:1, :])
        total = exact((row >= col).astype(F32), -jnp.exp(heads_ref[1:2, :]) * delta)
        total_rows[...] = jnp.transpose(total)
        columns[TOTAL] = total
        columns[DELTA] = delta
        columns[GROWN] = carried * jnp.exp(total)
        columns[ENDING] = to_last * jnp.exp(total[SPAN - 1 : SPAN, :] - total)
        columns[SCALE] = row_to_columns(scale_ref[0, 0:1, :])
        columns[MEAN] = row_to_columns(mean_ref[0, 0:1, :])
        columns[DTOTAL] = jnp.zeros((SPAN, 128), F32)
        columns[DDELTA] = jnp.zeros((SPAN, 128), F32)
        dlast_ref[...] = jnp.zeros_like(dlast_ref)
        b_conv, c_conv = convs(before)
        b_low = (b_conv * sigmoid(b_conv)).astype(BF16)
        c_low = (c_conv * sigmoid(c_conv)).astype(BF16)
        pair_ref[0] = b_low
        pair_ref[1] = c_low
        squares[1] = mm_nt(b_low, c_low)
        squares[2] = jnp.zeros((SPAN, SPAN), F32)
        c_flip_ref[...] = jnp.transpose(c_low.astype(F32)).astype(BF16)
        dpair_ref[...] = jnp.zeros_like(dpair_ref)
        dgated_ref[...] = mm_nt(dh[...], wo_ref[...])

    def one_tile(tile, low, high):
        width = high - low
        before = before_rows()
        after = [columns[AFTER + lag] for lag in range(TAPS - 1)]
        total, delta, grown, ending = (columns[at] for at in (TOTAL, DELTA, GROWN, ENDING))
        keep, scores = squares[0], squares[1]
        carry_last = grown[SPAN - 1 : SPAN, :]
        b_low = pair_ref[0]
        kx = kx_ref[...]
        lane = lax.broadcasted_iota(jnp.int32, (SPAN, width), 1)
        picker = (
            lax.broadcasted_iota(jnp.int32, (width, 128), 1)
            == 2 * tile + lax.broadcasted_iota(jnp.int32, (width, 128), 0) // HEAD
        ).astype(F32)
        skip = spread_pair(heads_ref[2:3, :], tile, width)
        conv = taps_sum(ext_x, low, high, before, kx, kx[TAPS : TAPS + 1])
        sig = sigmoid(conv)
        values = conv * sig
        delta_t = spread_pair(delta, tile, width)
        weighted = delta_t * values
        w_low = weighted.astype(BF16)
        scanned = scan_ref[:, low:high]
        mixed = (scanned + skip * values).astype(BF16).astype(F32)
        gate = gate_ref[:, low:high].astype(F32)
        gate_sig = sigmoid(gate)
        silu = gate * gate_sig
        scale = columns[SCALE, :, :width]
        n = mixed * silu * scale
        gain = gain_ref[0:1, low:high]
        dgated_t = dgated_ref[:, low:high]
        gated_ref[:, low:high] = (n * gain).astype(BF16)
        dg = scale * (dgated_t * gain - n * columns[MEAN, :, :width])
        dgate_ref[:, low:high] = (
            dg * mixed * (gate_sig * (1.0 + gate * (1.0 - gate_sig)))
        ).astype(BF16)
        dy_low = (dg * silu).astype(BF16)
        dy = dy_low.astype(F32)
        grad_w = None
        for half in range(width // HEAD):
            head = 2 * tile + half
            decay = jnp.exp(total_rows[head : head + 1, :] - total[:, head : head + 1] + keep)
            mine = (lane // HEAD) == half
            pairs = mm_nt(jnp.where(mine, w_low, jnp.zeros_like(w_low)), dy_low)
            squares[2] += decay * pairs
            part = mm((scores * decay).astype(BF16), dy_low)
            grad_w = part if grad_w is None else jnp.where(lane < HEAD, grad_w, part)
        dmem = dmemory[:, low:high]
        dmem_low = dmem.astype(BF16)
        mem_low = state_ref[0, :, low:high]
        ending_t = spread_pair(ending, tile, width)
        from_state = mm(b_low, dmem_low) * ending_t
        grad_w = grad_w + from_state
        dpair_ref[0] += mm_nt((weighted * ending_t).astype(BF16), dmem_low)
        dy_grown = (dy * spread_pair(grown, tile, width)).astype(BF16)
        dpair_ref[1] += mm_nt(dy_grown, mem_low)
        carry_t = spread_pair(carry_last, tile, width)
        w_round = w_low.astype(F32)
        at_last = jnp.sum(w_round * from_state, axis=0, keepdims=True) + jnp.sum(
            dmem * mem_low.astype(F32) * carry_t, axis=0, keepdims=True
        )
        dlast_ref[...] += exact(jnp.broadcast_to(at_last, (8, width)), picker)
        dmemory[:, low:high] = dmem * carry_t + mm(c_flip_ref[...], dy_grown)
        columns[DTOTAL] += exact(dy * scanned - w_round * grad_w, picker)
        columns[DDELTA] += exact(values * grad_w, picker)
        dconv = (delta_t * grad_w + skip * dy) * (sig * (1.0 + conv * (1.0 - sig)))
        ext_dx[0:SPAN, low:high] = dconv
        sums = [jnp.sum(dconv * ext_x[pl.ds(8, SPAN), low:high], axis=0, keepdims=True)]
        for lag in range(1, TAPS):
            masked = dconv * before[lag - 1][:, :width]
            sums.append(
                jnp.sum(masked * ext_x[pl.ds(8 - lag, SPAN), low:high], axis=0, keepdims=True)
            )
        sums = sums[::-1] + [
            jnp.sum(dconv, axis=0, keepdims=True),
            jnp.sum(dy * values, axis=0, keepdims=True),
            jnp.sum(dgated_t * n, axis=0, keepdims=True),
            jnp.zeros((1, width), F32),
        ]
        gx_ref[:, low:high] += jnp.concatenate(sums, axis=0)
        back = ext_dx[0:SPAN, low:high] * kx[TAPS - 1 : TAPS, low:high]
        for lag in range(1, TAPS):
            back = back + (
                ext_dx[pl.ds(lag, SPAN), low:high]
                * after[lag - 1][:, :width]
                * kx[TAPS - 1 - lag : TAPS - lag, low:high]
            )
        dx_ref[:, low:high] = back.astype(BF16)

    tiles = list(enumerate(tiles_of(inner)))
    cut = -(-len(tiles) // (BACKWARD_STEPS - 2))
    for at in range(BACKWARD_STEPS - 2):
        group = tiles[at * cut : (at + 1) * cut]
        if group:

            @pl.when(step == at + 1)
            def _():
                for tile, (low, high) in group:
                    one_tile(tile, low, high)

    @pl.when(step == BACKWARD_STEPS - 1)
    def _():
        before = before_rows()
        kbc = kbc_ref[...]
        score_grad = squares[2]
        db = dpair_ref[0] + mm(score_grad.astype(BF16), pair_ref[1])
        dc = dpair_ref[1] + mm(jnp.transpose(score_grad).astype(BF16), pair_ref[0])
        for part, (conv, grad) in enumerate(zip(convs(before), (db, dc))):
            low, high = part * STATE, (part + 1) * STATE
            sig = sigmoid(conv)
            dconv = grad * (sig * (1.0 + conv * (1.0 - sig)))
            ext_dbc[0:SPAN, low:high] = dconv
            sums = [jnp.sum(dconv * ext_bc[pl.ds(8, SPAN), low:high], axis=0, keepdims=True)]
            for lag in range(1, TAPS):
                masked = dconv * before[lag - 1]
                sums.append(
                    jnp.sum(masked * ext_bc[pl.ds(8 - lag, SPAN), low:high], axis=0, keepdims=True)
                )
            sums = sums[::-1] + [jnp.sum(dconv, axis=0, keepdims=True), jnp.zeros((3, STATE), F32)]
            gbc_ref[:, low:high] += jnp.concatenate(sums, axis=0)
            back = dconv * kbc[TAPS - 1 : TAPS, low:high]
            for lag in range(1, TAPS):
                back = back + (
                    ext_dbc[pl.ds(lag, SPAN), low:high]
                    * columns[AFTER + lag - 1]
                    * kbc[TAPS - 1 - lag : TAPS - lag, low:high]
                )
            dbc_ref[:, low:high] = back.astype(BF16)
        row, col = lower_ones()
        slope = -jnp.exp(heads_ref[1:2, :])
        rate = slope * columns[DELTA]
        drate = exact((row <= col).astype(F32), columns[DTOTAL]) + dlast_ref[0:1, :]
        ddt = (columns[DDELTA] + slope * drate) * sigmoid(dt_ref[...] + heads_ref[0:1, :])
        lane = lax.broadcasted_iota(jnp.int32, (SPAN, 128), 1)
        own_ddt = jnp.where(lane < inner // HEAD, ddt, 0.0)
        dbc_ref[:, 2 * STATE :] = own_heads(own_ddt, inner // HEAD, 1).astype(BF16)
        gheads_ref[...] += jnp.concatenate(
            [
                jnp.sum(ddt, axis=0, keepdims=True),
                jnp.sum(drate * rate, axis=0, keepdims=True),
                jnp.zeros((6, 128), F32),
            ],
            axis=0,
        )
        finish(
            mm_nt(dgate_ref[...], weight_refs[0][...])
            + mm_nt(dx_ref[...], weight_refs[1][...])
            + mm_nt(dbc_ref[...], weight_refs[2][...])
        )


def backward_scratch(inner):
    return [
        pltpu.VMEM((SPAN + 8, inner), F32),
        pltpu.VMEM((SPAN + 8, 2 * STATE), F32),
        pltpu.VMEM((SPAN + 8, inner), F32),
        pltpu.VMEM((SPAN + 8, 2 * STATE), F32),
        pltpu.VMEM((STATE, inner), F32),
        pltpu.VMEM((14, SPAN, 128), F32),
        pltpu.VMEM((128, SPAN), F32),
        pltpu.VMEM((3, SPAN, SPAN), F32),
        pltpu.VMEM((SPAN, inner), F32),
        pltpu.VMEM((2, SPAN, STATE), BF16),
        pltpu.VMEM((STATE, SPAN), BF16),
        pltpu.VMEM((2, SPAN, STATE), F32),
        pltpu.VMEM((8, 128), F32),
    ]


def plain_backward_kernel(length, starts_ref, dh_ref, scale_ref, mean_ref, *rest):
    small, wo_ref, saved, rest = rest[:4], rest[4], rest[5:13], rest[13:]
    inner = small[0].shape[1]
    *weights, rest = split_weights(inner, rest)
    *grads, rest = split_weights(inner, rest)
    gated_ref, dnormed_ref, *rest = rest
    sums, scratch = rest[:3], rest[3:]
    turn = pl.program_id(0)

    def finish(total):
        dnormed_ref[...] = total.astype(dnormed_ref.dtype)

    for step in range(BACKWARD_STEPS):
        backward_steps(
            step, turn == 0, pl.num_programs(0) - 1 - turn, length, starts_ref, dh_ref,
            (scale_ref, mean_ref), small, weights, wo_ref, saved, grads + [gated_ref], sums, scratch,
            finish,
        )


def fused_backward_kernel(sizes, whole_inner, length, outer_layer, starts_ref, dh, scale_ref, mean_ref, *rest):
    small, wo_ref, saved, rest = rest[:4], rest[4], rest[5:13], rest[13:]
    columns, normed, stream, gain, outer, rest = *rest[:5], rest[5:]
    if outer_layer:
        product, rest = rest[0], rest[1:]
        grad, gain_out, gx, gbc, gheads, means, gathered, finals, rest = *rest[:7], rest[7:9], rest[9:]
    else:
        other_sums, rest = rest[:4], rest[4:]
        carried, rest = rest[:2], rest[2:]
        grad, smalls_out, slots_0, slots_1, rest = *rest[:2], rest[2:4], rest[4:6], rest[6:]
    scratch, rest = rest[:13], rest[13:]
    weight, dproj, gated, part, inbox, load_sems, rest = *rest[:6], rest[6:]
    flow_scratch, flow_finals, rest = rest[:4], rest[4:6], rest[6:]
    ranks = {axis: lax.axis_index(axis) for axis in sizes}
    core, rank, member = ranks["section"], ranks["seq"], ranks["dp"]
    count, copies = sizes["seq"], sizes["dp"]
    if outer_layer:
        spread, mean_rows, tokens, rest = *rest[:3], rest[3:]
        row_send, row_recv, out_sems, rest = *rest[:3], rest[3:]
        line_refs, rest = rest[:5], rest[5:]
        flow_sems = rest
    else:
        gx, gbc, gheads, gain_out, rest = *rest[:4], rest[4:]
        packed, theirs, dp_sum, dp_slots, z_slots, rest = *rest[:5], rest[5:]
        small_sems, rest = rest[:6], rest[6:]
        squares_0, squares_1, rest = rest[:3], rest[3:6], rest[6:]
        line_refs, flow_sems = tuple(rest[:2]) + (None,) * 3, rest[2:]
        spread = None
    turn = pl.program_id(0)
    blocks = length // SPAN
    steps = blocks * BACKWARD_STEPS
    block = blocks - 1 - lax.div(turn, BACKWARD_STEPS)
    inner = small[0].shape[1]
    parts = ((0, inner), (inner, 2 * inner), (2 * inner, 2 * inner + 3 * STATE))
    width = dh.shape[1]
    line = Line(
        count,
        rank,
        part,
        inbox,
        spread,
        line_refs,
        (lambda at: (blocks - at) * BACKWARD_STEPS) if outer_layer else (lambda at: steps),
    )
    left_in = weight.at[0:length, 0:width]
    flow = Flow(
        sizes, ranks, left_in, dproj, gated, dh, *flow_finals, flow_scratch, flow_sems
    )
    weight_load = pltpu.make_async_copy(
        columns.at[1 if outer_layer else 0], weight, load_sems.at[0]
    )
    normed_load = pltpu.make_async_copy(normed, left_in, load_sems.at[1])

    @pl.when(turn == 0)
    def _():
        greet_all(sizes, ranks)
        weight_load.start()
        gain_out[...] = jnp.zeros_like(gain_out)

    @pl.when(turn == BACKWARD_STEPS - 1)
    def _():
        weight_load.wait()

    if not outer_layer:
        square = Square(member, carried, slots_1, squares_1)
        for when, stage in (
            (0, square.begin),
            (steps // 2, square.middle),
            (steps - 1, square.end),
        ):

            @pl.when((turn == when) & (core == 1))
            def _():
                stage(0)
                stage(1)

    @pl.when(turn < steps)
    def _():
        rows = pl.ds(pl.multiple_of(block * SPAN, SPAN), SPAN)

        def finish(total):
            part[rows, :] = total.astype(part.dtype)

        backward_steps(
            lax.rem(turn, BACKWARD_STEPS),
            turn < BACKWARD_STEPS,
            block,
            length,
            starts_ref,
            dh.at[rows],
            (scale_ref, mean_ref),
            small,
            [weight.at[:, low:high] for low, high in parts],
            wo_ref,
            saved,
            [dproj.at[rows, low:high] for low, high in parts] + [gated.at[rows]],
            (gx, gbc, gheads),
            scratch,
            finish,
        )

    def own_piece(piece, total):
        rows = pl.ds(pl.multiple_of(piece * PIECE, PIECE), PIECE)
        back, gain_part = norm_back(stream[rows, :].astype(F32), gain[0:1, :], total)
        gain_out[0:1, :] += gain_part
        whole_grad = outer[rows, :].astype(F32) + back
        grad[rows, :] = whole_grad
        if outer_layer:
            low = whole_grad.astype(BF16)
            spread[rank, rows, :] = low
            along_rows = jnp.sum(low.astype(F32) * product[rows, :], axis=1, keepdims=True)
            tokens[rows, :] = jnp.broadcast_to(along_rows / whole_inner, (PIECE, 128))

    if outer_layer:
        share = (count, rank, mean_rows.at[rank], mean_rows, row_send, row_recv)

        def after_own():
            mean_rows[rank] = jnp.transpose(tokens[...])[0:8, :]
            share_with_all(*share)

    else:
        s_core_send, s_core_recv, s_dp_send, s_dp_recv, s_z_send, s_z_recv = small_sems

        def s_core_copy():
            return push("section", 1 - core, packed, theirs, s_core_send, s_core_recv)

        def s_dp_copy(step):
            to = lax.rem(member + step, copies)
            return push(
                "dp", to, dp_sum, dp_slots.at[member], s_dp_send.at[step], s_dp_recv.at[member]
            )

        def s_z_copy(step):
            to = lax.rem(rank + step, count)
            return push(
                "seq", to, z_slots.at[rank], z_slots.at[rank], s_z_send.at[step], s_z_recv.at[rank]
            )

        def after_own():
            wide = SMALL_COLUMNS - 256
            mine = (gx, gbc, gheads, gain_out)
            packed[...] = jnp.zeros_like(packed)
            for layer, (x_sum, bc_sum, head_sum, gain_sum) in enumerate((mine, other_sums)):
                packed[layer, :, :inner] = x_sum[...]
                packed[layer, 0:5, inner:wide] = bc_sum[0:5, :]
                packed[layer, 5:7, inner : inner + 128] = head_sum[0:2, :]
                for row in range(width // 256):
                    packed[layer, row : row + 1, wide:] = gain_sum[0:1, row * 256 : (row + 1) * 256]
            s_core_copy().start()

    def serve(at, _):
        line.turn(at, own_piece, None, after_own)
        return 0

    square_here = None if outer_layer else Square(member, flow_finals, slots_0, squares_0)
    ready = flow.ready(2)

    def serve_both(at, _):
        line.turn(at, own_piece, None, after_own)
        flow.turn(at - steps, 2)
        for kind in range(2):

            @pl.when(at - steps == ready[kind])
            def _():
                flow.finals_here(kind, 1 if outer_layer else 0)

            if not outer_layer:

                @pl.when(at - steps == ready[kind] + 1)
                def _():
                    flow.finals_given(kind, 0)

                    @pl.when(core == 0)
                    def _():
                        square_here.begin(kind)

        return 0

    if outer_layer:

        @pl.when(turn < steps)
        def _():
            serve(turn, 0)

    @pl.when(turn == steps)
    def _():
        normed_load.start()
        normed_load.wait()
        lax.fori_loop(steps, steps + max(line.turns(), ready[1] + 2), serve_both, 0)
        if outer_layer:
            copies_out = [
                pltpu.make_async_copy(spread.at[at], gathered.at[at], out_sems.at[at])
                for at in range(count)
            ]
            for copy in copies_out:
                copy.start()
            share_wait_recv(*share)
            means[...] = mean_rows[...]
            share_wait_send(*share)
            flow.finals_given(0, 1)
            flow.finals_given(1, 1)
            for at in range(2):
                final_copy = pltpu.make_async_copy(
                    flow_finals[at], finals[at], out_sems.at[count + at]
                )
                final_copy.start()
                final_copy.wait()
            flow.settle()
            line.settle()
            for copy in copies_out:
                copy.wait()
        else:
            s_core_copy().wait_recv()
            dp_sum[...] = packed[...] + theirs[...]
            for step in range(1, copies):
                s_dp_copy(step).start()

            @pl.when(core == 0)
            def _():
                square_here.middle(0)
                square_here.middle(1)

            total = dp_sum[...]
            for step in range(1, copies):
                origin = lax.rem(member + step, copies)
                place = dp_slots.at[origin]
                push(
                    "dp", origin, place, place, s_dp_send.at[step], s_dp_recv.at[origin]
                ).wait_recv()
                total = total + dp_slots[origin]
            z_slots[rank] = total
            for step in range(1, count):
                s_z_copy(step).start()
            @pl.when(core == 0)
            def _():
                square_here.end(0)
                square_here.end(1)

            for step in range(1, count):
                origin = lax.rem(rank + step, count)
                place = z_slots.at[origin]
                push("seq", origin, place, place, s_z_send.at[step], s_z_recv.at[origin]).wait_recv()
            smalls_out[...] = z_slots[...]

            s_core_copy().wait_send()
            for step in range(1, copies):
                s_dp_copy(step).wait_send()
            for step in range(1, count):
                s_z_copy(step).wait_send()
            flow.settle()
            line.settle()


def whole(array):
    return pl.BlockSpec(array.shape, lambda i: (0,) * array.ndim, pipeline_mode=pl.Buffered(1))


def of_layer(array, layer):
    return pl.BlockSpec(
        (None,) + array.shape[1:],
        lambda i: (layer,) + (0,) * (array.ndim - 1),
        pipeline_mode=pl.Buffered(1),
    )


def cost(length, width, inner, passes):
    flops = 2 * length * width * (3 * inner + 384) * passes
    return pl.CostEstimate(flops=flops, bytes_accessed=length * width * 16, transcendentals=0)


VMEM_LIMIT = 48 * 2**20


def part_kind(length, width):
    return F32 if length * width * 4 <= 8 * 2**20 else BF16


def run_forward(starts, normed, weights, dh=None):
    columns, kx, kbc, heads, gain, wo = weights
    length, width = normed.shape
    inner = kx.shape[1]
    blocks = length // SPAN
    rows = lambda cols: pl.BlockSpec((SPAN, cols), lambda i: (i, 0))
    small = [kx, kbc, heads, gain]
    given = [wo] + list(columns)
    operands = [starts, normed] + small + [array for array, _ in given]
    in_specs = [pl.BlockSpec(memory_space=pltpu.SMEM), rows(width)]
    in_specs += [whole(array) for array in small] + [spec for _, spec in given]
    if dh is not None:
        operands.append(dh)
        in_specs.append(rows(width))
    out_shape = [
        jax.ShapeDtypeStruct((length, inner), BF16),
        jax.ShapeDtypeStruct((length, inner), BF16),
        jax.ShapeDtypeStruct((length, 2 * STATE), BF16),
        jax.ShapeDtypeStruct((length, 128), F32),
        jax.ShapeDtypeStruct((length, inner), F32),
        jax.ShapeDtypeStruct((blocks, STATE, inner), BF16),
        jax.ShapeDtypeStruct((length, width), BF16 if dh is not None else part_kind(length, width)),
        jax.ShapeDtypeStruct((8, length), F32),
    ]
    out_specs = [
        rows(inner),
        rows(inner),
        rows(2 * STATE),
        rows(128),
        rows(inner),
        pl.BlockSpec((1, STATE, inner), lambda i: (i, 0, 0)),
        rows(width),
        pl.BlockSpec((8, SPAN), lambda i: (0, i)),
    ]
    return pl.pallas_call(
        functools.partial(forward_kernel, dh is not None, length),
        grid=(blocks,),
        in_specs=in_specs,
        out_specs=out_specs,
        out_shape=out_shape,
        scratch_shapes=[
            pltpu.VMEM((SPAN + 8, inner), F32),
            pltpu.VMEM((SPAN + 8, 2 * STATE), F32),
            pltpu.VMEM((STATE, inner), F32),
            pltpu.VMEM((SPAN, inner), BF16),
        ],
        compiler_params=pltpu.CompilerParams(
            dimension_semantics=("arbitrary",), vmem_limit_bytes=VMEM_LIMIT
        ),
        cost_estimate=cost(length, width, inner, 1),
        name="layer_forward",
    )(*operands)


def run_backward(starts, dh, scales, means, weights, saved, fused=None):
    columns, kx, kbc, heads, gain, wo = weights
    gate, x, bc, dt, scanned, states = saved
    length, width = dh.shape
    inner = kx.shape[1]
    blocks = length // SPAN
    if fused is None:
        block = lambda i: blocks - 1 - i
    else:
        block = lambda i: blocks - 1 - jnp.minimum(lax.div(i, BACKWARD_STEPS), blocks - 1)
    rows = lambda cols: pl.BlockSpec((SPAN, cols), lambda i: (block(i), 0))
    halo = lambda cols: pl.BlockSpec(
        (16, cols), lambda i: (jnp.maximum(block(i) * (SPAN // 16) - 1, 0), 0)
    )
    fixed = lambda shape: pl.BlockSpec(shape, lambda i: (0,) * len(shape))
    stat = pl.BlockSpec((1, 8, SPAN), lambda i: (block(i), 0, 0))
    small = [kx, kbc, heads, gain]
    operands = [starts, dh, scales, means] + small + [wo[0]]
    in_specs = [pl.BlockSpec(memory_space=pltpu.SMEM), whole(dh) if fused else rows(width), stat, stat]
    in_specs += [whole(array) for array in small] + [wo[1]]
    operands += [gate, x, x, bc, bc, dt, scanned, states]
    in_specs += [
        rows(inner),
        rows(inner),
        halo(inner),
        rows(2 * STATE),
        halo(2 * STATE),
        rows(128),
        rows(inner),
        pl.BlockSpec((1, STATE, inner), lambda i: (block(i), 0, 0)),
    ]
    sums = [
        jax.ShapeDtypeStruct((8, inner), F32),
        jax.ShapeDtypeStruct((8, 2 * STATE), F32),
        jax.ShapeDtypeStruct((8, 128), F32),
    ]
    scratch = backward_scratch(inner)
    if fused is None:
        operands += [array for array, _ in columns]
        in_specs += [spec for _, spec in columns]
        widths = [2 * inner + 3 * STATE] if len(columns) == 1 else [inner, inner, 3 * STATE]
        out_shape = [jax.ShapeDtypeStruct((length, cols), BF16) for cols in widths] + [
            jax.ShapeDtypeStruct((length, inner), BF16),
            jax.ShapeDtypeStruct((length, width), part_kind(length, width)),
        ]
        out_specs = [rows(cols) for cols in widths] + [rows(inner), rows(width)]
        out_shape += sums
        out_specs += [fixed(array.shape) for array in sums]
        kernel, grid, settings = functools.partial(plain_backward_kernel, length), blocks, {}
    else:
        sizes = axis_sizes()
        count, copies = sizes["seq"], sizes["dp"]
        layer, whole_inner, normed, inputs, carried = fused
        stream, next_gain, outer, *more = inputs
        wide = columns.shape[2]
        dma = pltpu.SemaphoreType.DMA
        operands += [columns, normed] + list(inputs) + list(carried)
        in_specs += [IN_HBM, IN_HBM] + [whole(array) for array in list(inputs) + list(carried)]
        flow_scratch, flow_sems, finals = flow_shapes(sizes, width // count, inner, width, wide)
        scratch += [
            pltpu.VMEM((width, wide), BF16),
            pltpu.VMEM((length, wide), BF16),
            pltpu.VMEM((length, inner), BF16),
            pltpu.VMEM((length, width), BF16),
            pltpu.VMEM((count + 1, SPAN, width), BF16),
            dma((2,)),
        ]
        scratch += flow_scratch + [pltpu.VMEM(f.shape, f.dtype) for f in finals]
        out_shape = [jax.ShapeDtypeStruct((SPAN, width), F32)]
        if layer:
            out_shape += [jax.ShapeDtypeStruct((8, width), F32)] + sums
            out_shape += [jax.ShapeDtypeStruct((count, 8, SPAN), F32)]
            out_specs = [fixed(array.shape) for array in out_shape]
            out_shape += [jax.ShapeDtypeStruct((count, SPAN, width), BF16)] + finals
            out_specs += [IN_HBM] * 3
            scratch += [
                pltpu.VMEM((count, SPAN, width), BF16),
                pltpu.VMEM((count, 8, SPAN), F32),
                pltpu.VMEM((SPAN, 128), F32),
                dma((count,)),
                dma((count,)),
                dma((count + 2,)),
            ]
            scratch += line_sems(count, SPAN // PIECE)
        else:
            out_shape += [jax.ShapeDtypeStruct((count, 2, 8, SMALL_COLUMNS), F32)]
            out_specs = [fixed(array.shape) for array in out_shape]
            slots = [jax.ShapeDtypeStruct((copies,) + f.shape, f.dtype) for f in finals]
            out_shape += slots + slots
            out_specs += [IN_HBM] * 4
            scratch += [pltpu.VMEM(array.shape, F32) for array in sums] + [pltpu.VMEM((8, width), F32)]
            scratch += [pltpu.VMEM((2, 8, SMALL_COLUMNS), F32)] * 3
            scratch += [pltpu.VMEM((size, 2, 8, SMALL_COLUMNS), F32) for size in (copies, count)]
            scratch += [dma, dma, dma((copies,)), dma((copies,)), dma((count,)), dma((count,))]
            scratch += square_sems() + square_sems() + line_sems(count, SPAN // PIECE)[:2]
        scratch += flow_sems
        kernel = functools.partial(fused_backward_kernel, sizes, whole_inner, length, bool(layer))
        grid = blocks * BACKWARD_STEPS + 1
        settings = {"collective_id": 2 + layer, "has_side_effects": True}
    return pl.pallas_call(
        kernel,
        grid=(grid,),
        in_specs=in_specs,
        out_specs=out_specs,
        out_shape=out_shape,
        scratch_shapes=scratch,
        compiler_params=pltpu.CompilerParams(
            dimension_semantics=("arbitrary",), vmem_limit_bytes=BACK_VMEM, **settings
        ),
        cost_estimate=cost(length, width, inner, 2),
        name="layer_backward",
    )(*operands)


BACK_VMEM = 63 * 2**20


def norm_rows(rows_in, gain_vec):
    return (
        rows_in
        * lax.rsqrt(jnp.mean(rows_in * rows_in, axis=-1, keepdims=True) + EPSILON)
        * gain_vec
    )


def norm_back(rows_in, gain_vec, grad):
    inverse = lax.rsqrt(jnp.mean(rows_in * rows_in, axis=-1, keepdims=True) + EPSILON)
    unit = rows_in * inverse
    scaled = grad * gain_vec
    back = inverse * (scaled - unit * jnp.mean(scaled * unit, axis=-1, keepdims=True))
    return back, jnp.sum(grad * unit, axis=0, keepdims=True)


MESH = pl.DeviceIdType.MESH
PIECE = 16
HOP = 2


def along(axis, index):
    return {axis: index}


def greet(axis, count, rank):
    barrier = pltpu.get_barrier_semaphore()
    for step in range(1, count):
        pl.semaphore_signal(
            barrier, inc=1, device_id=along(axis, lax.rem(rank + step, count)), device_id_type=MESH
        )
    pl.semaphore_wait(barrier, count - 1)


def send_to(axis, index, source, target, send_sem, recv_sem):
    return pltpu.make_async_remote_copy(
        src_ref=source,
        dst_ref=target,
        send_sem=send_sem,
        recv_sem=recv_sem,
        device_id=along(axis, index),
        device_id_type=MESH,
    )


def share_with_all(count, rank, source, slots, send_sems, recv_sems):
    for step in range(1, count):
        to = lax.rem(rank + step, count)
        send_to("seq", to, source, slots.at[rank], send_sems.at[step], recv_sems.at[rank]).start()


def share_wait_recv(count, rank, source, slots, send_sems, recv_sems):
    for step in range(1, count):
        origin = lax.rem(rank + step, count)
        send_to(
            "seq", origin, source, slots.at[origin], send_sems.at[step], recv_sems.at[origin]
        ).wait_recv()


def share_wait_send(count, rank, source, slots, send_sems, recv_sems):
    for step in range(1, count):
        to = lax.rem(rank + step, count)
        send_to("seq", to, source, slots.at[rank], send_sems.at[step], recv_sems.at[rank]).wait_send()


class Line:
    def __init__(self, count, rank, part, inbox, spread, sems, born=lambda block: 0):
        self.count, self.rank = count, rank
        self.part, self.inbox, self.spread = part, inbox, spread
        self.sum_send, self.sum_recv, self.out_right, self.out_left, self.out_recv = sems
        self.born = born
        self.pieces = SPAN // PIECE

    def sum_copy(self, slot, target_slot, to, piece):
        rows = pl.ds(piece * PIECE, PIECE)
        return send_to(
            "seq",
            to,
            self.inbox.at[slot, rows],
            self.inbox.at[target_slot, rows],
            self.sum_send.at[slot, piece],
            self.sum_recv.at[target_slot, piece],
        )

    def arrived(self, slot, piece):
        self.sum_copy(slot, slot, self.rank, piece).wait_recv()

    def own_part(self, block, piece):
        start = pl.multiple_of(block * SPAN + piece * PIECE, PIECE)
        return self.part[pl.ds(start, PIECE), :].astype(F32)

    def pass_sum(self, piece, away, sign):
        count, rank = self.count, self.rank
        rows = pl.ds(pl.multiple_of(piece * PIECE, PIECE), PIECE)
        block = rank + sign * away
        first = rank == 0 if sign > 0 else rank == count - 1

        @pl.when(first)
        def _():
            self.inbox[block, rows, :] = self.own_part(block, piece).astype(BF16)

        @pl.when(jnp.logical_not(first))
        def _():
            self.arrived(block, piece)
            total = self.own_part(block, piece) + self.inbox[block, rows, :].astype(F32)
            self.inbox[block, rows, :] = total.astype(BF16)

        target = count if sign < 0 and away == 1 else block
        self.sum_copy(block, target, rank + sign, piece).start()

    def pass_sums(self, turn):
        count, rank, pieces = self.count, self.rank, self.pieces
        for away in range(count - 1, 0, -1):
            for sign in (1, -1):
                block = rank + sign * away
                inside = block < count if sign > 0 else block >= 0
                piece = turn - self.born(block) - HOP * (rank if sign > 0 else count - 1 - rank)

                @pl.when(inside & (piece >= 0) & (piece < pieces))
                def _():
                    self.pass_sum(piece, away, sign)

    def own_lag(self, block):
        return self.born(block) + HOP * jnp.maximum(block, self.count - 1 - block)

    def own_total(self, piece):
        count, rank = self.count, self.rank
        rows = pl.ds(pl.multiple_of(piece * PIECE, PIECE), PIECE)

        @pl.when(rank > 0)
        def _():
            self.arrived(rank, piece)

        @pl.when(rank < count - 1)
        def _():
            self.arrived(count, piece)

        from_left = jnp.where(rank > 0, self.inbox[rank, rows, :].astype(F32), 0.0)
        from_right = jnp.where(rank < count - 1, self.inbox[count, rows, :].astype(F32), 0.0)
        return self.own_part(rank, piece) + from_left + from_right

    def out_copy(self, block, piece, sign):
        rows = pl.ds(pl.multiple_of(piece * PIECE, PIECE), PIECE)
        sems = self.out_right if sign > 0 else self.out_left
        return send_to(
            "seq",
            self.rank + sign,
            self.spread.at[block, rows],
            self.spread.at[block, rows],
            sems.at[block, piece],
            self.out_recv.at[block, piece],
        )

    def start_out(self, block, piece, sign):
        @pl.when(self.rank < self.count - 1 if sign > 0 else self.rank > 0)
        def _():
            self.out_copy(block, piece, sign).start()

    def pass_out(self, turn, away):
        for sign in (1, -1):
            block = self.rank - sign * away
            piece = turn - self.own_lag(block) - HOP * away
            inside = block >= 0 if sign > 0 else block < self.count

            @pl.when(inside & (piece >= 0) & (piece < self.pieces))
            def _():
                self.out_copy(block, piece, sign).wait_recv()
                self.start_out(block, piece, sign)

    def turns(self):
        return self.pieces + HOP * (2 if self.spread is not None else 1) * (self.count - 1)

    def turn(self, turn, own_piece, before_own=None, after_own=None):
        self.pass_sums(turn)
        if self.spread is not None:
            for away in range(1, self.count):
                self.pass_out(turn, away)
        piece = turn - self.own_lag(self.rank)
        if before_own is not None:

            @pl.when(piece == 0)
            def _():
                before_own()

        @pl.when((piece >= 0) & (piece < self.pieces))
        def _():
            own_piece(piece, self.own_total(piece))
            if self.spread is not None:
                self.start_out(self.rank, piece, 1)
                self.start_out(self.rank, piece, -1)

        if after_own is not None:

            @pl.when(piece == self.pieces - 1)
            def _():
                after_own()

    def run(self, own_piece, before_own=None, after_own=None, flow=None, pace=2):
        turns = self.turns()
        if flow is not None:
            turns = max(turns, flow.turns(pace))

        def step(turn, _):
            self.turn(turn, own_piece, before_own, after_own)
            if flow is not None:
                flow.turn(turn, pace)
            return 0

        lax.fori_loop(0, turns, step, 0)
        self.settle()

    def settle(self):
        def body(piece, _):
            for block in range(self.count):
                right = (block > self.rank) & (self.rank < self.count - 1)
                left = (block < self.rank) & (self.rank > 0)

                @pl.when(right | left)
                def _():
                    self.sum_copy(block, block, self.rank, piece).wait_send()

                if self.spread is not None:

                    @pl.when((block <= self.rank) & (self.rank < self.count - 1))
                    def _():
                        self.out_copy(block, piece, 1).wait_send()

                    @pl.when((block >= self.rank) & (self.rank > 0))
                    def _():
                        self.out_copy(block, piece, -1).wait_send()

            return 0

        lax.fori_loop(0, self.pieces, body, 0)


def line_sems(count, pieces):
    return [
        pltpu.SemaphoreType.DMA((count + 1, pieces)),
        pltpu.SemaphoreType.DMA((count + 1, pieces)),
        pltpu.SemaphoreType.DMA((count, pieces)),
        pltpu.SemaphoreType.DMA((count, pieces)),
        pltpu.SemaphoreType.DMA((count, pieces)),
    ]


def row_to_columns(row):
    return jnp.transpose(jnp.broadcast_to(row, (128, SPAN)))


def sum_forward_kernel(
    count,
    whole_inner,
    part,
    stat,
    stream,
    gain,
    spread,
    scales,
    hidden,
    product,
    inbox,
    slots,
    columns,
    stat_send,
    stat_recv,
    *sems,
):
    rank = lax.axis_index("seq")
    greet("seq", count, rank)
    share = (count, rank, stat, slots, stat_send, stat_recv)
    share_with_all(*share)
    line = Line(count, rank, part, inbox, spread, sems)

    def before_own():
        share_wait_recv(*share)
        for block in range(count):
            lanes = slice(block * SPAN, (block + 1) * SPAN)
            total = stat[:, lanes]
            for origin in range(count):
                total = total + jnp.where(origin == rank, 0.0, slots[origin, :, lanes])
            scales[block] = lax.rsqrt(total / whole_inner + EPSILON)
        columns[...] = row_to_columns(scales[rank][0:1, :])

    def own_piece(piece, total):
        rows = pl.ds(pl.multiple_of(piece * PIECE, PIECE), PIECE)
        y = total * columns[rows, 0:1]
        low = (stream[rows, :].astype(F32) + y).astype(BF16)
        hidden[rows, :] = low
        product[rows, :] = y
        spread[rank, rows, :] = norm_rows(low.astype(F32), gain[0:1, :]).astype(BF16)

    line.run(own_piece, before_own)
    share_wait_send(*share)


def sum_plain_kernel(count, part, stream, gain, outer, grad, gain_grad, inbox, *sems):
    rank = lax.axis_index("seq")
    greet("seq", count, rank)
    line = Line(count, rank, part, inbox, None, tuple(sems) + (None,) * 3)
    gain_grad[...] = jnp.zeros_like(gain_grad)

    def own_piece(piece, total):
        rows = pl.ds(pl.multiple_of(piece * PIECE, PIECE), PIECE)
        back, gain_part = norm_back(stream[rows, :].astype(F32), gain[0:1, :], total)
        gain_grad[0:1, :] += gain_part
        grad[rows, :] = outer[rows, :].astype(F32) + back

    line.run(own_piece)


def sum_stats_kernel(count, whole_inner, stat, scales, means, slots, stat_send, stat_recv):
    rank = lax.axis_index("seq")
    greet("seq", count, rank)
    share = (count, rank, stat, slots, stat_send, stat_recv)
    share_with_all(*share)
    share_wait_recv(*share)
    for block in range(count):
        lanes = slice(block * SPAN, (block + 1) * SPAN)
        total = stat[:, lanes]
        for origin in range(count):
            total = total + jnp.where(origin == rank, 0.0, slots[origin, :, lanes])
        scale = lax.rsqrt(total[0:1, :] / whole_inner + EPSILON)
        scales[block] = jnp.broadcast_to(scale, (8, SPAN))
        means[block] = jnp.broadcast_to(total[1:2, :] * scale / whole_inner, (8, SPAN))
    share_wait_send(*share)


IN_VMEM = pl.BlockSpec(memory_space=pltpu.VMEM)


def line_call(kernel, name, collective_id, operands, out_shape, scratch):
    return pl.pallas_call(
        kernel,
        out_shape=out_shape,
        in_specs=[IN_VMEM] * len(operands),
        out_specs=[IN_VMEM] * len(out_shape),
        scratch_shapes=scratch,
        compiler_params=pltpu.CompilerParams(
            collective_id=collective_id, has_side_effects=True, vmem_limit_bytes=LINE_VMEM
        ),
        name=name,
    )(*operands)


LINE_VMEM = 60 * 2**20


def sum_forward(part, stat, stream, gain, whole_inner):
    count = lax.axis_size("seq")
    length, width = part.shape
    pieces = SPAN // PIECE
    return line_call(
        functools.partial(sum_forward_kernel, count, whole_inner),
        "sum_forward",
        1,
        [part, stat, stream, gain],
        [
            jax.ShapeDtypeStruct((count, SPAN, width), BF16),
            jax.ShapeDtypeStruct((count, 8, SPAN), F32),
            jax.ShapeDtypeStruct((SPAN, width), BF16),
            jax.ShapeDtypeStruct((SPAN, width), F32),
        ],
        [
            pltpu.VMEM((count + 1, SPAN, width), BF16),
            pltpu.VMEM((count, 8, length), F32),
            pltpu.VMEM((SPAN, 128), F32),
            pltpu.SemaphoreType.DMA((count,)),
            pltpu.SemaphoreType.DMA((count,)),
        ]
        + line_sems(count, pieces),
    )


def sum_plain(part, stream, gain, outer):
    count = lax.axis_size("seq")
    length, width = part.shape
    pieces = SPAN // PIECE
    return line_call(
        functools.partial(sum_plain_kernel, count),
        "sum_plain",
        8,
        [part, stream, gain, outer],
        [
            jax.ShapeDtypeStruct((SPAN, width), F32),
            jax.ShapeDtypeStruct((8, width), F32),
        ],
        [pltpu.VMEM((count + 1, SPAN, width), BF16)] + line_sems(count, pieces)[:2],
    )


def sum_stats(stat, whole_inner):
    count = lax.axis_size("seq")
    length = stat.shape[1]
    return line_call(
        functools.partial(sum_stats_kernel, count, whole_inner),
        "sum_stats",
        4,
        [stat],
        [
            jax.ShapeDtypeStruct((count, 8, SPAN), F32),
            jax.ShapeDtypeStruct((count, 8, SPAN), F32),
        ],
        [
            pltpu.VMEM((count, 8, length), F32),
            pltpu.SemaphoreType.DMA((count,)),
            pltpu.SemaphoreType.DMA((count,)),
        ],
    )


def other_core(array):
    return lax.ppermute(array, "section", [(0, 1), (1, 0)])


def both_layers(array):
    core = lax.axis_index("section")
    theirs = other_core(array)
    return (
        jnp.where(core == 0, array, theirs),
        jnp.where(core == 0, theirs, array),
    )


IN_HBM = pl.BlockSpec(memory_space=pl.ANY)


def greet_all(sizes, ranks):
    barrier = pltpu.get_barrier_semaphore()
    total = 0
    for axis, size in sizes.items():
        for step in range(1, size):
            to = lax.rem(ranks[axis] + step, size)
            pl.semaphore_signal(barrier, inc=1, device_id={axis: to}, device_id_type=MESH)
            total += 1
    pl.semaphore_wait(barrier, total)


def push(axis, index, source, target, send_sem, recv_sem):
    return pltpu.make_async_remote_copy(
        src_ref=source,
        dst_ref=target,
        send_sem=send_sem,
        recv_sem=recv_sem,
        device_id={axis: index},
        device_id_type=MESH,
    )


def start_kernel(
    sizes,
    small,
    hidden,
    bundle,
    out_weight,
    normed,
    columns,
    rows_out,
    smalls,
    local_sem,
    split_send,
    split_recv,
    copy_send,
    copy_recv,
    core_send,
    core_recv,
    out_send,
    out_recv,
    small_send,
    small_recv,
    small_core_send,
    small_core_recv,
    right_send,
    left_send,
    block_recv,
):
    ranks = {axis: lax.axis_index(axis) for axis in sizes}
    core, rank, stream = ranks["section"], ranks["seq"], ranks["dp"]
    count, copies = sizes["seq"], sizes["dp"]
    part = bundle.shape[1]
    depth = part * copies
    greet_all(sizes, ranks)

    smalls[core, rank] = small[...]
    for step in range(1, count):
        to = lax.rem(rank + step, count)
        place = smalls.at[core, rank]
        push("seq", to, place, place, small_send.at[step], small_recv.at[rank]).start()
    push(
        "section", 1 - core, out_weight.at[0], rows_out.at[core], out_send, out_recv
    ).start()

    def slot(origin, share):
        return pl.ds(pl.multiple_of(origin * depth + share * part, part), part)

    def split_copy(step):
        to = lax.rem(rank + step, count)
        return push(
            "seq",
            to,
            bundle.at[to],
            columns.at[core, slot(rank, stream)],
            split_send.at[step],
            split_recv.at[rank],
        )

    for step in range(count - 1, 0, -1):
        split_copy(step).start()
    own = pltpu.make_async_copy(bundle.at[rank], columns.at[core, slot(rank, stream)], local_sem)
    own.start()

    def spread_slot(origin, held=None):
        place = columns.at[core, slot(origin, stream)]
        source = place if held is None else held
        for step in range(1, copies):
            to = lax.rem(stream + step, copies)
            push(
                "dp", to, source, place, copy_send.at[origin, step], copy_recv.at[origin, stream]
            ).start()
        push(
            "section",
            1 - core,
            source,
            place,
            core_send.at[origin, stream],
            core_recv.at[origin, stream],
        ).start()

    spread_slot(rank, bundle.at[rank])
    rows_out[core] = out_weight[0]

    for step in range(1, count):
        origin = lax.rem(rank + step, count)
        place = smalls.at[core, origin]
        push("seq", origin, place, place, small_send.at[step], small_recv.at[origin]).wait_recv()
    push(
        "section", 1 - core, smalls.at[core], smalls.at[core], small_core_send, small_core_recv
    ).start()

    for step in range(1, count):
        origin = lax.rem(rank + step, count)
        place = columns.at[core, slot(origin, stream)]
        push("seq", origin, place, place, split_send.at[step], split_recv.at[origin]).wait_recv()
        spread_slot(origin)

    push(
        "section",
        1 - core,
        smalls.at[1 - core],
        smalls.at[1 - core],
        small_core_send,
        small_core_recv,
    ).wait_recv()
    gain = jnp.concatenate([smalls[0, origin, 5:6, :depth] for origin in range(count)], axis=1)
    normed[rank] = norm_rows(hidden[core].astype(F32), gain).astype(BF16)

    def block_copy(block, sign):
        return push(
            "seq",
            rank + sign,
            normed.at[block],
            normed.at[block],
            (right_send if sign > 0 else left_send).at[block],
            block_recv.at[block],
        )

    def open_end(sign):
        return rank < count - 1 if sign > 0 else rank > 0

    for sign in (1, -1):

        @pl.when(open_end(sign))
        def _():
            block_copy(rank, sign).start()

    for away in range(1, count):
        for sign in (1, -1):
            block = rank - sign * away

            @pl.when(block >= 0 if sign > 0 else block < count)
            def _():
                block_copy(block, sign).wait_recv()

                @pl.when(open_end(sign))
                def _():
                    block_copy(block, sign).start()

    for origin in range(count):
        for step in range(1, copies):
            share = lax.rem(stream + step, copies)
            place = columns.at[core, slot(origin, share)]
            push(
                "dp", share, place, place, copy_send.at[origin, step], copy_recv.at[origin, share]
            ).wait_recv()
            push(
                "section",
                1 - core,
                place,
                place,
                core_send.at[origin, share],
                core_recv.at[origin, share],
            ).start()
    for origin in range(count):
        for share in range(copies):
            theirs = columns.at[1 - core, slot(origin, share)]
            copy = push(
                "section",
                1 - core,
                theirs,
                theirs,
                core_send.at[origin, share],
                core_recv.at[origin, share],
            )
            copy.wait_recv()
            copy.wait_send()
        for step in range(1, copies):
            place = columns.at[core, slot(origin, stream)]
            push(
                "dp", stream, place, place, copy_send.at[origin, step], copy_recv.at[origin, stream]
            ).wait_send()
    own.wait()
    rows_copy = push(
        "section", 1 - core, out_weight.at[0], rows_out.at[1 - core], out_send, out_recv
    )
    rows_copy.wait_recv()
    rows_copy.wait_send()
    push(
        "section", 1 - core, smalls.at[core], smalls.at[core], small_core_send, small_core_recv
    ).wait_send()
    for step in range(1, count):
        to = lax.rem(rank + step, count)
        place = smalls.at[core, rank]
        push("seq", to, place, place, small_send.at[step], small_recv.at[rank]).wait_send()
        split_copy(step).wait_send()
    for block in range(count):

        @pl.when((block <= rank) & (rank < count - 1))
        def _():
            block_copy(block, 1).wait_send()

        @pl.when((block >= rank) & (rank > 0))
        def _():
            block_copy(block, -1).wait_send()


def axis_sizes():
    return {axis: lax.axis_size(axis) for axis in ("section", "seq", "dp")}


def start(small, hidden, bundle, out_weight):
    sizes = axis_sizes()
    count, copies = sizes["seq"], sizes["dp"]
    depth, inner, width = bundle.shape[1] * copies, out_weight.shape[1], out_weight.shape[2]
    dma = pltpu.SemaphoreType.DMA
    return pl.pallas_call(
        functools.partial(start_kernel, sizes),
        out_shape=[
            jax.ShapeDtypeStruct((count,) + hidden.shape[1:], BF16),
            jax.ShapeDtypeStruct((2, count * depth, 2 * inner + 3 * STATE), BF16),
            jax.ShapeDtypeStruct((2, inner, width), BF16),
            jax.ShapeDtypeStruct((2, count) + small.shape, F32),
        ],
        in_specs=[IN_VMEM, IN_VMEM, IN_HBM, IN_VMEM],
        out_specs=[IN_VMEM, IN_HBM, IN_VMEM, IN_VMEM],
        scratch_shapes=[
            dma,
            dma((count,)),
            dma((count,)),
            dma((count, copies)),
            dma((count, copies)),
            dma((count, copies)),
            dma((count, copies)),
            dma,
            dma,
            dma((count,)),
            dma((count,)),
            dma,
            dma,
            dma((count,)),
            dma((count,)),
            dma((count,)),
        ],
        compiler_params=pltpu.CompilerParams(
            collective_id=5, has_side_effects=True, vmem_limit_bytes=LINE_VMEM
        ),
        name="start",
    )(small, hidden, bundle, out_weight)


def small_rows(conv_weight, conv_bias, norm_gain):
    part = conv_bias.shape[1]
    pad = -part % 128
    rows = jnp.concatenate([conv_weight[0], conv_bias], axis=0).astype(F32)
    rows = jnp.pad(rows, ((0, 0), (0, pad)))
    gain = jnp.pad(norm_gain.astype(F32), ((0, 0), (0, part + pad - norm_gain.shape[1])))
    return jnp.concatenate([rows, gain, jnp.zeros((2, part + pad), F32)], axis=0)


def step_columns(rows, whole_inner):
    rows = rows[:, 2 * whole_inner :]
    return jnp.pad(rows, ((0, 0), (0, 3 * STATE - rows.shape[1])))


def layer_facts(smalls, step_bias, decay_log, skip_gain, gate_gain, part, depth):
    count = lax.axis_size("seq")
    rank = lax.axis_index("seq")
    inner = gate_gain.shape[1]
    heads = step_bias.shape[1]
    own = jnp.concatenate([step_bias, decay_log, skip_gain], axis=0)
    own = jnp.pad(own, ((0, 5), (0, 128 - heads)))
    own = both_layers(own.astype(F32))
    gate = both_layers(jnp.broadcast_to(gate_gain, (8, inner)).astype(F32))
    facts = []
    for layer in range(2):
        rows = smalls[layer]
        taps = rows[:, :, :part].transpose(1, 0, 2).reshape(8, count * part)
        gain = jnp.broadcast_to(rows[:, 5, :depth].reshape(1, -1), (8, count * depth))
        facts.append(
            (
                lax.dynamic_slice_in_dim(taps, rank * inner, inner, 1),
                taps[:, count * inner :],
                own[layer],
                gate[layer],
                gain,
            )
        )
    return facts


def column_bundle(in_weight, inner):
    count, copies = lax.axis_size("seq"), lax.axis_size("dp")
    part = in_weight.shape[1] // copies
    rows = lax.dynamic_slice_in_dim(in_weight[0], lax.axis_index("dp") * part, part, 0)
    kinds = [
        rows[:, kind * count * inner : (kind + 1) * count * inner]
        .reshape(part, count, inner)
        .transpose(1, 0, 2)
        for kind in range(2)
    ]
    rest = step_columns(rows, count * inner)
    kinds.append(jnp.broadcast_to(rest[None], (count,) + rest.shape))
    return jnp.concatenate(kinds, axis=2)


def columns_by_collectives(in_weight, inner):
    count = lax.axis_size("seq")
    depth = in_weight.shape[1]
    rows = in_weight[0]
    kinds = []
    for kind in range(2):
        part = rows[:, kind * count * inner : (kind + 1) * count * inner]
        part = part.reshape(depth, count, inner).transpose(1, 0, 2)
        part = lax.all_to_all(part, "seq", split_axis=0, concat_axis=0, tiled=True)
        kinds.append(both_layers(part.reshape(count * depth, inner)))
    step_weight = step_columns(rows, count * inner)
    kinds.append(both_layers(lax.all_gather(step_weight, "seq", axis=0, tiled=True)))
    return [[(kind[layer], whole(kind[layer])) for kind in kinds] for layer in range(2)]


class Flow:
    def __init__(self, sizes, ranks, left_in, right_in, left_out, right_out, final, out_final, scratch, sems):
        self.left_in, self.right_in, self.left_out, self.right_out = (
            left_in,
            right_in,
            left_out,
            right_out,
        )
        self.final, self.out_final = final, out_final
        self.give, self.got, self.parts, self.sums = scratch
        (
            self.core_send,
            self.core_recv,
            self.part_send,
            self.part_recv,
            self.z_send,
            self.z_recv,
            self.give_send,
            self.give_recv,
        ) = sems
        self.count, self.copies = sizes["seq"], sizes["dp"]
        self.core, self.rank, self.stream = ranks["section"], ranks["seq"], ranks["dp"]
        self.units, half, self.depth = self.got.shape
        self.halves = (half, left_out.shape[1])

    def multiply(self, unit, kind, core, keep):
        depth = self.depth
        if kind == 0:
            strip = self.halves[0] // 2
            base = core * (self.right_in.shape[1] - self.halves[0])
            source, right = self.right_in, self.left_in
            block = unit
        else:
            strip = self.halves[1] // 2
            base = 0
            source, right = self.left_out, self.right_out
            block = 2 * (unit - self.count) + core
        right = right[:, pl.ds(pl.multiple_of(block * depth, depth), depth)]

        def body(index, _):
            low = pl.multiple_of(base + index * strip, 128)
            keep(pl.ds(pl.multiple_of(index * strip, strip), strip), mm_tn(source[:, pl.ds(low, strip)], right))
            return 0

        lax.fori_loop(0, 2, body, 0)

    def core_copy(self, unit, kind):
        rows = pl.ds(0, self.halves[kind])
        return push(
            "section",
            1 - self.core,
            self.give.at[unit, rows],
            self.got.at[unit, rows],
            self.core_send.at[unit],
            self.core_recv.at[unit],
        )

    def part_rows(self, member, kind):
        share = self.halves[kind] // self.copies
        return pl.ds(pl.multiple_of(member * share, share), share)

    def bits(self, unit):
        first = 1 + lax.rem(unit, 2)
        return first, 3 - first

    def flip(self, bit):
        low = lax.rem(lax.div(self.stream, bit), 2)
        return self.stream + bit - 2 * bit * low

    def step_copy(self, unit, step, kind):
        first, second = self.bits(unit)
        partner, opposite = self.flip(first), self.flip(second)
        member = (partner, partner + opposite - self.stream, opposite)[step]
        return push(
            "dp",
            opposite if step == 2 else partner,
            self.got.at[unit, self.part_rows(member, kind)],
            self.parts.at[unit, step, pl.ds(0, self.halves[kind] // self.copies)],
            self.part_send.at[unit, step],
            self.part_recv.at[unit, step],
        )

    def z_copy(self, unit):
        return push(
            "seq",
            unit,
            self.sums.at[unit],
            self.final.at[self.core, self.rank],
            self.z_send.at[unit],
            self.z_recv.at[self.rank],
        )

    def first(self, unit, kind):
        def keep(rows, value):
            self.give[unit, rows, :] = value.astype(BF16)

        self.multiply(unit, kind, 1 - self.core, keep)
        self.core_copy(unit, kind).start()

    def second(self, unit, kind):
        self.core_copy(unit, kind).wait_recv()

        def keep(rows, value):
            self.got[unit, rows, :] = (value + self.got[unit, rows, :].astype(F32)).astype(BF16)

        self.multiply(unit, kind, self.core, keep)
        self.step_copy(unit, 0, kind).start()
        self.step_copy(unit, 1, kind).start()

    def add_part(self, unit, step, member, kind):
        self.step_copy(unit, step, kind).wait_recv()
        total = self.got[unit, self.part_rows(member, kind), :].astype(F32)
        part = self.parts[unit, step, : self.halves[kind] // self.copies, :]
        return (total + part.astype(F32)).astype(BF16)

    def third(self, unit, kind):
        opposite = self.flip(self.bits(unit)[1])
        self.got[unit, self.part_rows(opposite, kind), :] = self.add_part(unit, 1, opposite, kind)
        self.step_copy(unit, 2, kind).start()
        self.got[unit, self.part_rows(self.stream, kind), :] = self.add_part(
            unit, 0, self.stream, kind
        )

    def fourth(self, unit, kind):
        total = self.add_part(unit, 2, self.stream, kind)
        if kind:
            self.out_final[self.core, unit - self.count] = total
        else:

            @pl.when(unit == self.rank)
            def _():
                self.final[self.core, self.rank] = total

            @pl.when(unit != self.rank)
            def _():
                self.sums[unit] = total
                self.z_copy(unit).start()

    LAGS = (0, 1, 5, 9)

    def turn(self, turn, pace):
        for stage, lag in zip((self.first, self.second, self.third, self.fourth), self.LAGS):
            at = turn - lag

            for kind, (low, high) in enumerate(((0, self.count), (self.count, self.units))):

                @pl.when((at >= low * pace) & (at < high * pace) & (lax.rem(at, pace) == 0))
                def _():
                    stage(lax.div(at, pace), kind)

    def turns(self, pace):
        return (self.units - 1) * pace + self.LAGS[3] + 1

    def ready(self, pace):
        last = self.LAGS[3]
        return (self.count - 1) * pace + last + 2, (self.units - 1) * pace + last + 1

    def finals_here(self, kind, layer):
        if kind == 0:
            for step in range(1, self.count):
                origin = lax.rem(self.rank + step, self.count)
                place = self.final.at[self.core, origin]
                push(
                    "seq", origin, place, place, self.z_send.at[origin], self.z_recv.at[origin]
                ).wait_recv()

        @pl.when(self.core != layer)
        def _():
            self.give_copy(kind).start()

    def give_copy(self, kind):
        final = (self.final, self.out_final)[kind]
        place = final.at[self.core]
        return push(
            "section", 1 - self.core, place, place, self.give_send.at[kind], self.give_recv.at[kind]
        )

    def finals_given(self, kind, layer):
        final = (self.final, self.out_final)[kind]

        @pl.when(self.core == layer)
        def _():
            place = final.at[1 - self.core]
            push(
                "section", 1 - self.core, place, place, self.give_send.at[kind], self.give_recv.at[kind]
            ).wait_recv()

        @pl.when(self.core != layer)
        def _():
            self.give_copy(kind).wait_send()

    def settle(self):
        for kind, (low, high) in enumerate(((0, self.count), (self.count, self.units))):

            def body(unit, _):
                self.core_copy(unit, kind).wait_send()
                for step in range(3):
                    self.step_copy(unit, step, kind).wait_send()
                if kind == 0:

                    @pl.when(unit != self.rank)
                    def _():
                        self.z_copy(unit).wait_send()

                return 0

            lax.fori_loop(low, high, body, 0)


class Square:
    def __init__(self, member, sources, slots, sems):
        self.member, self.sources, self.slots = member, sources, slots
        self.own_sem, self.send, self.recv = sems

    def flip(self, bit):
        return self.member + bit - 2 * bit * lax.rem(lax.div(self.member, bit), 2)

    def own_copy(self, kind):
        return pltpu.make_async_copy(
            self.sources[kind], self.slots[kind].at[self.member], self.own_sem.at[kind]
        )

    def near_copy(self, kind, way):
        return push(
            "dp",
            self.flip(1 + way),
            self.sources[kind],
            self.slots[kind].at[self.member],
            self.send.at[kind, way],
            self.recv.at[kind, way],
        )

    def far_copy(self, kind, way):
        place = self.slots[kind].at[self.flip(1 + way), way]
        return push(
            "dp", self.flip(2 - way), place, place, self.send.at[kind, 2 + way], self.recv.at[kind, 2 + way]
        )

    def begin(self, kind):
        self.own_copy(kind).start()
        for way in range(2):
            self.near_copy(kind, way).start()

    def middle(self, kind):
        for way in range(2):
            self.near_copy(kind, way).wait_recv()
            self.far_copy(kind, way).start()

    def end(self, kind):
        for way in range(2):
            self.far_copy(kind, way).wait_recv()
        for way in range(2):
            self.near_copy(kind, way).wait_send()
            self.far_copy(kind, way).wait_send()
        self.own_copy(kind).wait()


def square_sems():
    dma = pltpu.SemaphoreType.DMA
    return [dma((2,)), dma((2, 4)), dma((2, 4))]


def flow_shapes(sizes, depth, inner, width, wide):
    count, copies = sizes["seq"], sizes["dp"]
    units = count + width // depth // 2
    half = -(-wide // 1024) * 512
    dma = pltpu.SemaphoreType.DMA
    scratch = [
        pltpu.VMEM((units, half, depth), BF16),
        pltpu.VMEM((units, half, depth), BF16),
        pltpu.VMEM((units, 3, half // copies, depth), BF16),
        pltpu.VMEM((count, half // copies, depth), BF16),
    ]
    sems = [
        dma((units,)),
        dma((units,)),
        dma((units, 3)),
        dma((units, 3)),
        dma((sizes["seq"],)),
        dma((sizes["seq"],)),
        dma((2,)),
        dma((2,)),
    ]
    finals = [
        jax.ShapeDtypeStruct((2, count, half // copies, depth), BF16),
        jax.ShapeDtypeStruct((2, units - count, inner // copies, depth), BF16),
    ]
    return scratch, sems, finals


def sum_backward_kernel(
    sizes,
    with_flow,
    whole_inner,
    part,
    stream,
    gain,
    outer,
    product,
    *rest,
):
    ranks = {axis: lax.axis_index(axis) for axis in sizes}
    rank, count = ranks["seq"], sizes["seq"]
    if with_flow:
        factors, rest = rest[:4], rest[4:]
        finals, rest = rest[4:6], rest[:4] + rest[6:]
    spread, means, grad, gain_grad, inbox, columns, *rest = rest
    if with_flow:
        scratch, rest = rest[:4], rest[4:]
    row_send, row_recv, *sems = rest
    greet_all(sizes if with_flow else {"seq": count}, ranks)
    line = Line(count, rank, part, inbox, spread, sems[:5])
    flow = None
    if with_flow:
        flow = Flow(sizes, ranks, *factors, *finals, scratch, sems[5:])
    gain_grad[...] = jnp.zeros_like(gain_grad)
    share = (count, rank, means.at[rank], means, row_send, row_recv)

    def own_piece(piece, total):
        rows = pl.ds(pl.multiple_of(piece * PIECE, PIECE), PIECE)
        back, gain_part = norm_back(stream[rows, :].astype(F32), gain[0:1, :], total)
        gain_grad[0:1, :] += gain_part
        whole = outer[rows, :].astype(F32) + back
        grad[rows, :] = whole
        low = whole.astype(BF16)
        spread[rank, rows, :] = low
        along_rows = jnp.sum(low.astype(F32) * product[rows, :], axis=1, keepdims=True)
        columns[rows, :] = jnp.broadcast_to(along_rows / whole_inner, (PIECE, 128))

    def after_own():
        means[rank] = jnp.transpose(columns[...])[0:8, :]
        share_with_all(*share)

    line.run(own_piece, None, after_own, flow)
    if with_flow:
        flow.finals_here(1)
    share_wait_recv(*share)
    share_wait_send(*share)
    if with_flow:
        flow.finals_given(1)
        flow.settle()


def sum_backward(part, stream, gain, outer, product, whole_inner, grads_of):
    sizes = axis_sizes()
    count = sizes["seq"]
    length, width = part.shape
    pieces = SPAN // PIECE
    factors, scratch, sems, finals = [], [], [], []
    if grads_of is not None:
        factors = list(grads_of)
        scratch, sems, finals = flow_shapes(
            sizes, width // count, factors[2].shape[1], width, factors[1].shape[1]
        )
    return line_call(
        functools.partial(sum_backward_kernel, sizes, grads_of is not None, whole_inner),
        "sum_backward",
        7,
        [part, stream, gain, outer, product] + factors,
        [
            jax.ShapeDtypeStruct((count, SPAN, width), BF16),
            jax.ShapeDtypeStruct((count, 8, SPAN), F32),
            jax.ShapeDtypeStruct((SPAN, width), F32),
            jax.ShapeDtypeStruct((8, width), F32),
        ]
        + finals,
        [
            pltpu.VMEM((count + 1, SPAN, width), BF16),
            pltpu.VMEM((SPAN, 128), F32),
        ]
        + scratch
        + [pltpu.SemaphoreType.DMA((count,)), pltpu.SemaphoreType.DMA((count,))]
        + line_sems(count, pieces)
        + sems,
    )


SMALL_COLUMNS = 1280


def unpack_kernel(inner, first, second, result, held, rest, sems):
    origin = pl.program_id(0)
    count = pl.num_programs(0)
    copies, _, _, share, depth = first.shape
    mine = lax.axis_index("section") == 0
    bounds = ((0, inner), (inner, 2 * inner), (2 * inner, 2 * inner + 3 * STATE))

    @pl.when(origin == 0)
    def _():
        rest[...] = jnp.zeros_like(rest)

    for core in range(2):
        for member in range(copies):
            rows = jnp.where(mine, first[member, core, 0], second[member, core, 0]).astype(F32)
            half = copies * share
            start = core * (bounds[2][1] - half) + member * share
            for kind, (low, high) in enumerate(bounds):
                top, end = max(start, low, core * half), min(start + share, high)
                if top < end:
                    piece = rows[top - start : end - start]
                    if kind < 2:
                        held[origin, kind, top - low : end - low, :] = piece
                    else:
                        rest[top - low : end - low, :] += piece

    def copy(at, kind):
        low = pl.multiple_of((kind * count + at) * inner, 8)
        return pltpu.make_async_copy(
            held.at[at, kind], result.at[pl.ds(low, inner)], sems.at[at, kind]
        )

    for kind in range(2):
        copy(origin, kind).start()

    @pl.when(origin == count - 1)
    def _():
        low = 2 * held.shape[0] * inner
        left = result.shape[0] - low
        tail = pltpu.make_async_copy(
            rest.at[pl.ds(0, left)], result.at[pl.ds(low, left)], sems.at[held.shape[0], 0]
        )
        tail.start()
        for at in range(held.shape[0]):
            for kind in range(2):
                copy(at, kind).wait()
        tail.wait()


def unpack(first, second, inner, width):
    copies, _, count, share, depth = first.shape
    block = pl.BlockSpec((copies, 2, 1, share, depth), lambda origin: (0, 0, origin, 0, 0))
    return pl.pallas_call(
        functools.partial(unpack_kernel, inner),
        grid=(count,),
        in_specs=[block, block],
        out_specs=IN_HBM,
        out_shape=jax.ShapeDtypeStruct((width, depth), F32),
        scratch_shapes=[
            pltpu.VMEM((count, 2, inner, depth), F32),
            pltpu.VMEM((3 * STATE, depth), F32),
            pltpu.SemaphoreType.DMA((count + 1, 2)),
        ],
        compiler_params=pltpu.CompilerParams(vmem_limit_bytes=VMEM_LIMIT),
        name="unpack",
    )(first, second).T


def unpack_rows_kernel(first, second, result):
    mine = lax.axis_index("section") == 0
    _, cores, blocks, _, depth = first.shape
    for core in range(cores):
        for block in range(blocks):
            low = (block * cores + core) * depth
            rows = jnp.where(mine, first[0, core, block], second[0, core, block])
            result[:, low : low + depth] = rows.astype(F32)


def unpack_rows(first, second):
    copies, cores, blocks, share, depth = first.shape
    piece = pl.BlockSpec((1,) + first.shape[1:], lambda member: (member, 0, 0, 0, 0))
    width = cores * blocks * depth
    return pl.pallas_call(
        unpack_rows_kernel,
        grid=(copies,),
        in_specs=[piece, piece],
        out_specs=pl.BlockSpec((share, width), lambda member: (member, 0)),
        out_shape=jax.ShapeDtypeStruct((copies * share, width), F32),
        compiler_params=pltpu.CompilerParams(vmem_limit_bytes=VMEM_LIMIT),
        name="unpack_rows",
    )(first, second)


def grads_by_collectives(in_parts, out_part, inner):
    core = lax.axis_index("section")
    count = lax.axis_size("seq")

    def to_core(pair):
        theirs = other_core(jnp.where(core == 0, pair[1], pair[0]).astype(BF16))
        return (jnp.where(core == 0, pair[0], pair[1]) + theirs.astype(F32)).astype(BF16)

    gate, x, rest = (to_core(pair) for pair in in_parts)
    out = to_core(out_part)
    depth = gate.shape[0] // count

    def rows_of(part):
        part = part.reshape(count, depth, -1)
        part = lax.all_to_all(part, "seq", split_axis=0, concat_axis=0, tiled=True)
        return lax.psum(part, "dp").astype(F32)

    gate, x, rest = rows_of(gate), rows_of(x), rows_of(rest)
    columns = [part.transpose(1, 0, 2).reshape(depth, -1) for part in (gate, x)]
    return jnp.concatenate(columns + [jnp.sum(rest, axis=0)], axis=1), lax.psum(out, "dp").astype(F32)


def local(
    hidden_in,
    doc_starts,
    cotangent,
    norm_gain,
    in_weight,
    conv_weight,
    conv_bias,
    step_bias,
    decay_log,
    skip_gain,
    gate_gain,
    out_weight,
):
    sizes = axis_sizes()
    core = lax.axis_index("section")
    rank = lax.axis_index("seq")
    count, copies = sizes["seq"], sizes["dp"]
    inner = out_weight.shape[1]
    heads = step_bias.shape[1]
    whole_inner = inner * count
    depth = in_weight.shape[1]
    part = conv_bias.shape[1]
    tokens = hidden_in.shape[1]
    regular = inner % depth == 0 and depth % 128 == 0 and copies == 4 and count % 2 == 0

    gather = lambda array: lax.all_gather(array, "seq", axis=0, tiled=True)
    stream = lax.dynamic_index_in_dim(hidden_in, core, 0, keepdims=False)
    outer = lax.dynamic_index_in_dim(cotangent, core, 0, keepdims=False)
    starts = lax.dynamic_index_in_dim(doc_starts, core, 0, keepdims=False)
    small = small_rows(conv_weight, conv_bias, norm_gain)
    if regular:
        normed_0, columns, out_rows, smalls = start(
            small, hidden_in, column_bundle(in_weight, inner), out_weight
        )
        normed_0 = normed_0.reshape(count * tokens, -1)
        both_columns = columns
        columns = [[(columns, of_layer(columns, layer))] for layer in range(2)]
        out_rows = [(out_rows, of_layer(out_rows, layer)) for layer in range(2)]
    else:
        smalls = lax.all_gather(lax.all_gather(small, "seq", axis=0), "section", axis=0)
        columns = columns_by_collectives(in_weight, inner)
        out_rows = [(array, whole(array)) for array in both_layers(out_weight[0])]
    facts = layer_facts(smalls, step_bias, decay_log, skip_gain, gate_gain, part, depth)
    gains = [fact[4] for fact in facts]
    if not regular:
        normed_0 = gather(norm_rows(stream.astype(F32), gains[0][0:1]).astype(BF16))
    layers = [(columns[layer],) + facts[layer][:4] + (out_rows[layer],) for layer in range(2)]
    if regular:
        fused_layers = [(both_columns,) + layers[layer][1:] for layer in range(2)]

    outer_after, normed_0 = lax.optimization_barrier((outer, normed_0))
    dh_whole = gather(outer_after)
    fwd_0 = run_forward(starts, normed_0, layers[0])
    normed_1, scales_0, hidden_1, product_0 = sum_forward(
        fwd_0[6], fwd_0[7], stream, gains[1], whole_inner
    )
    normed_1 = normed_1.reshape(normed_0.shape)
    fwd_1 = run_forward(starts, normed_1, layers[1], dh_whole)
    scales_1, means_1 = sum_stats(fwd_1[7], whole_inner)

    if regular:
        inputs = (hidden_1, gains[1], outer, product_0)
        fused_1 = (1, whole_inner, normed_1, inputs, ())
        input_grad_1, gain_grad_1, *sums_1 = run_backward(
            starts, dh_whole, scales_1, means_1, fused_layers[1], fwd_1[:6], fused_1
        )
        *sums_1, means_0, dh_0, final_1, out_final_1 = sums_1
    else:
        back_1 = run_backward(starts, dh_whole, scales_1, means_1, layers[1], fwd_1[:6])
        kinds = len(columns[0])
        gated_1, dnormed_1 = back_1[kinds : kinds + 2]
        dh_0, means_0, input_grad_1, gain_grad_1 = sum_backward(
            dnormed_1, hidden_1, gains[1], outer, product_0, whole_inner, None
        )
    own_dh_0 = lax.dynamic_index_in_dim(dh_0, rank, 0, keepdims=False)
    part_1, dh_0 = lax.optimization_barrier((fwd_1[6], dh_0))
    product_1 = lax.psum_scatter(part_1, "seq", scatter_dimension=0, tiled=True)
    own_scale = lax.dynamic_index_in_dim(scales_1, rank, 0, keepdims=False)[0]
    hidden_2 = (hidden_1.astype(F32) + product_1.astype(F32) * own_scale[:, None]).astype(BF16)
    dh_0 = dh_0.reshape(dh_whole.shape)
    if regular:
        inputs = (stream, gains[0], own_dh_0, *sums_1, gain_grad_1)
        input_grad_0, smalls, halves_0, halves_out_0, halves_1, halves_out_1 = run_backward(
            starts, dh_0, scales_0, means_0, fused_layers[0], fwd_0[:6],
            (0, whole_inner, normed_0, inputs, (final_1, out_final_1)),
        )
        grad_in = unpack(halves_0, halves_1, inner, in_weight.shape[2])
        grad_out = unpack_rows(halves_out_0, halves_out_1)
    else:
        back_0 = run_backward(starts, dh_0, scales_0, means_0, layers[0], fwd_0[:6])
        gated_0, dnormed_0 = back_0[kinds : kinds + 2]
        input_grad_0, gain_grad_0 = sum_plain(dnormed_0, stream, gains[0], own_dh_0)

        def packed(back):
            gx, gbc, gheads = back[kinds + 2 : kinds + 5]
            rest = jnp.pad(gheads[:2], ((0, 0), (0, 128)))
            rest = jnp.concatenate([gbc[:5], rest, gbc[7:]], axis=0)
            return jnp.concatenate([gx, rest, jnp.zeros((8, 256), F32)], axis=1)

        small_grads = jnp.stack([packed(back_0), packed(back_1)])
        pairs = [
            (mm_tn(normed_0, back_0[kind]), mm_tn(normed_1, back_1[kind])) for kind in range(kinds)
        ]
        grad_in, grad_out = grads_by_collectives(
            pairs, (mm_tn(gated_0, dh_0), mm_tn(gated_1, dh_whole)), inner
        )
        gain_rows = jnp.stack([gain_grad_0[0], gain_grad_1[0]]).reshape(2, -1, 256)
        small_grads = small_grads.at[:, : gain_rows.shape[1], inner + 256 :].set(gain_rows)
        smalls = lax.all_gather(lax.psum(small_grads, ("section", "dp")), "seq", axis=0)
    grad_in = grad_in[:, : in_weight.shape[2]]

    mine = lax.dynamic_index_in_dim(smalls, core, 1, keepdims=False)
    x_part = mine[:, :5, :inner].transpose(1, 0, 2).reshape(5, whole_inner)
    bc_part = jnp.sum(mine[:, :5, inner : inner + 256], axis=0)
    channels = lax.dynamic_slice_in_dim(
        jnp.concatenate([x_part, bc_part], axis=1), rank * part, part, 1
    )
    gain_rows = norm_gain.shape[1] * count // 256
    norm_grad = jnp.sum(mine[:, :gain_rows, inner + 256 :], axis=0).reshape(-1)
    norm_grad = lax.dynamic_slice_in_dim(norm_grad, rank * norm_gain.shape[1], norm_gain.shape[1], 0)
    own = lax.dynamic_index_in_dim(mine, rank, 0, keepdims=False)

    def by_layer(first, second):
        kept = jnp.where(core == 0, first, second)
        theirs = other_core(jnp.where(core == 0, second, first))
        return jnp.stack([jnp.where(core == 0, kept, theirs), jnp.where(core == 0, theirs, kept)])

    return (
        by_layer(hidden_1, hidden_2)[None],
        by_layer(input_grad_0, input_grad_1)[None],
        norm_grad[None],
        grad_in[None],
        channels[None, :TAPS],
        channels[TAPS:],
        own[5:6, inner : inner + heads],
        own[6:7, inner : inner + heads],
        jnp.sum(own[5, :inner].reshape(1, heads, HEAD), axis=2),
        own[6:7, :inner],
        grad_out[None],
    )


def solution(mesh):
    return jax.shard_map(
        local,
        mesh=mesh,
        in_specs=(
            P("dp", "seq", None),
            P("dp", None),
            P("dp", "seq", None),
            P("section", "seq"),
            P("section", "seq", None),
            P("section", None, "seq"),
            P("section", "seq"),
            P("section", "seq"),
            P("section", "seq"),
            P("section", "seq"),
            P("section", "seq"),
            P("section", "seq", None),
        ),
        out_specs=(
            P("section", "dp", "seq", None),
            P("section", "dp", "seq", None),
            P("section", "seq"),
            P("section", "seq", None),
            P("section", None, "seq"),
            P("section", "seq"),
            P("section", "seq"),
            P("section", "seq"),
            P("section", "seq"),
            P("section", "seq"),
            P("section", "seq", None),
        ),
        check_vma=False,
    )
```

```python
import functools

import jax
import jax.numpy as jnp
from jax import lax
from jax.experimental import pallas as pl
from jax.experimental.pallas import tpu as pltpu
from jax.sharding import PartitionSpec as P

SPAN = 256
HEAD = 64
STATE = 128
TAPS = 4
EPSILON = 1e-05
HIGHEST = lax.Precision.HIGHEST
F32 = jnp.float32
BF16 = jnp.bfloat16
FAR = -1e30


def mm(a, b):
    return jnp.dot(a, b, preferred_element_type=F32)


def mm_nt(a, b):
    return lax.dot_general(a, b, (((1,), (1,)), ((), ())), preferred_element_type=F32)


def mm_tn(a, b):
    return lax.dot_general(a, b, (((0,), (0,)), ((), ())), preferred_element_type=F32)


def exact(a, b):
    return lax.dot_general(
        a, b, (((1,), (0,)), ((), ())), precision=HIGHEST, preferred_element_type=F32
    )


def doc_of(starts_ref, position):
    total = jnp.zeros(position.shape, jnp.int32)
    for entry in range(starts_ref.shape[0]):
        total = total + (starts_ref[entry] <= position).astype(jnp.int32)
    return total


def tiles_of(width):
    return [(low, min(low + 128, width)) for low in range(0, width, 128)]


def spread_pair(columns, tile, width):
    rows = columns.shape[0]
    first = jnp.broadcast_to(columns[:, 2 * tile : 2 * tile + 1], (rows, width))
    if width <= HEAD:
        return first
    second = jnp.broadcast_to(columns[:, 2 * tile + 1 : 2 * tile + 2], (rows, width))
    lane = lax.broadcasted_iota(jnp.int32, (rows, width), 1)
    return jnp.where(lane < HEAD, first, second)


def block_facts(starts_ref, block, length):
    base = block * SPAN
    column = base + lax.broadcasted_iota(jnp.int32, (SPAN, 128), 0)
    doc_col = doc_of(starts_ref, column)
    before = []
    for lag in range(1, TAPS):
        same = (doc_of(starts_ref, column - lag) == doc_col) & (column >= lag)
        before.append(same.astype(F32))
    row = base + lax.broadcasted_iota(jnp.int32, (8, SPAN), 1)
    doc_row = doc_of(starts_ref, row)
    same_square = doc_col[:, 0:1] == doc_row[0:1, :]
    edge_before = jnp.full((8, 128), base - 1, jnp.int32)
    last_doc_before = doc_of(starts_ref, edge_before)[0:1, :]
    last_doc = doc_of(starts_ref, jnp.full((8, 128), base + SPAN - 1, jnp.int32))[0:1, :]
    carried = ((doc_col == last_doc_before) & (base > 0)).astype(F32)
    to_last = (doc_col == last_doc).astype(F32)
    return doc_col, column, before, same_square, carried, to_last


def taps_sum(ext_ref, low, high, before, kernel, bias):
    summed = ext_ref[pl.ds(8, SPAN), low:high] * kernel[TAPS - 1 : TAPS, low:high] + bias[0:1, low:high]
    for lag in range(1, TAPS):
        summed = summed + (
            ext_ref[pl.ds(8 - lag, SPAN), low:high]
            * before[lag - 1][:, : high - low]
            * kernel[TAPS - 1 - lag : TAPS - lag, low:high]
        )
    return summed


def sigmoid(value):
    return 1.0 / (1.0 + jnp.exp(-value))


def softplus(value):
    small = jnp.exp(-jnp.abs(value))
    series = small * (1.0 - small * (0.5 - small * (1.0 / 3.0)))
    return jnp.maximum(value, 0.0) + jnp.where(small < 0.01, series, jnp.log(1.0 + small))


def lower_ones():
    row = lax.broadcasted_iota(jnp.int32, (SPAN, SPAN), 0)
    col = lax.broadcasted_iota(jnp.int32, (SPAN, SPAN), 1)
    return row, col


def split_weights(inner, refs):
    if refs[0].shape[1] > inner:
        parts = [(0, inner), (inner, 2 * inner), (2 * inner, 2 * inner + 3 * STATE)]
        return [refs[0].at[:, low:high] for low, high in parts] + [refs[1:]]
    return [refs[0], refs[1], refs[2], refs[3:]]


def own_heads(columns, heads, sign):
    shift = lax.rem(128 + sign * heads * lax.axis_index("seq"), 128)
    return pltpu.roll(columns, shift, 1)


TOTAL, DELTA, GROWN, ENDING, BEFORE = 0, 1, 2, 3, 4


def forward_kernel(
    with_back,
    length,
    starts_ref,
    normed_ref,
    kx_ref,
    kbc_ref,
    heads_ref,
    gain_ref,
    wo_ref,
    *rest,
):
    inner = kx_ref.shape[1]
    wg_ref, wx_ref, wbc_ref, rest = split_weights(inner, rest)
    if with_back:
        dh_ref, rest = rest[0], rest[1:]
    (
        gate_ref,
        x_ref,
        bc_ref,
        dt_ref,
        scan_ref,
        state_ref,
        part_ref,
        stat_ref,
        ext_x,
        ext_bc,
        memory,
        gu_ref,
    ) = rest
    block = pl.program_id(0)

    @pl.when(block == 0)
    def _():
        ext_x[...] = jnp.zeros_like(ext_x)
        ext_bc[...] = jnp.zeros_like(ext_bc)
        memory[...] = jnp.zeros_like(memory)

    @pl.when(block > 0)
    def _():
        ext_x[0:8, :] = ext_x[SPAN : SPAN + 8, :]
        ext_bc[0:8, :] = ext_bc[SPAN : SPAN + 8, :]

    normed = normed_ref[...]
    bcdt = mm(normed, wbc_ref[...]).astype(BF16)
    bc_ref[...] = bcdt[:, : 2 * STATE]
    ext_bc[8 : SPAN + 8, :] = bcdt[:, : 2 * STATE].astype(F32)
    dt_low = own_heads(bcdt[:, 2 * STATE :].astype(F32), inner // HEAD, -1)
    dt_ref[...] = dt_low
    x_low = mm(normed, wx_ref[...]).astype(BF16)
    x_ref[...] = x_low
    ext_x[8 : SPAN + 8, :] = x_low.astype(F32)
    gate_low = mm(normed, wg_ref[...]).astype(BF16)
    gate_ref[...] = gate_low

    _, _, before, same_square, carried, to_last = block_facts(starts_ref, block, length)
    row, col = lower_ones()
    lower = (row >= col).astype(F32)
    keep = jnp.where(same_square & (row >= col), 0.0, FAR)

    delta = softplus(dt_low + heads_ref[0:1, :])
    rate = -jnp.exp(heads_ref[1:2, :]) * delta
    total = exact(lower, rate)
    total_rows = jnp.transpose(total)
    grown = carried * jnp.exp(total)
    last_total = total[SPAN - 1 : SPAN, :]
    ending = to_last * jnp.exp(last_total - total)
    carry_last = grown[SPAN - 1 : SPAN, :]

    kbc = kbc_ref[...]
    b_conv = taps_sum(ext_bc, 0, STATE, before, kbc, kbc[TAPS : TAPS + 1])
    c_conv = taps_sum(ext_bc, STATE, 2 * STATE, before, kbc, kbc[TAPS : TAPS + 1])
    b_low = (b_conv * sigmoid(b_conv)).astype(BF16)
    c_low = (c_conv * sigmoid(c_conv)).astype(BF16)
    scores = mm_nt(c_low, b_low)
    b_flip = jnp.transpose(b_low.astype(F32)).astype(BF16)

    state_ref[0] = memory[...].astype(BF16)
    kx = kx_ref[...]
    squares = jnp.zeros((SPAN, 128), F32)
    for tile, (low, high) in enumerate(tiles_of(inner)):
        width = high - low
        lane = lax.broadcasted_iota(jnp.int32, (SPAN, width), 1)
        conv = taps_sum(ext_x, low, high, before, kx, kx[TAPS : TAPS + 1])
        values = conv * sigmoid(conv)
        weighted = spread_pair(delta, tile, width) * values
        w_low = weighted.astype(BF16)
        mixed = None
        for half in range(width // HEAD):
            head = 2 * tile + half
            decay = jnp.exp(total[:, head : head + 1] - total_rows[head : head + 1, :] + keep)
            part = mm((scores * decay).astype(BF16), w_low)
            mixed = part if mixed is None else jnp.where(lane < HEAD, mixed, part)
        mem = memory[:, low:high]
        mixed = mixed + mm(c_low, mem.astype(BF16)) * spread_pair(grown, tile, width)
        scan_ref[:, low:high] = mixed
        fresh = mm(b_flip, (weighted * spread_pair(ending, tile, width)).astype(BF16))
        memory[:, low:high] = mem * spread_pair(carry_last, tile, width) + fresh
        mixed = (
            (mixed + spread_pair(heads_ref[2:3, :], tile, width) * values).astype(BF16).astype(F32)
        )
        gate = gate_ref[:, low:high].astype(F32)
        g = mixed * (gate * sigmoid(gate))
        if width == 128:
            squares = squares + g * g
        else:
            squares = squares + jnp.concatenate([g * g, jnp.zeros((SPAN, 128 - width), F32)], axis=1)
        gu_ref[:, low:high] = (g * gain_ref[0:1, low:high]).astype(BF16)

    stats = jnp.sum(squares, axis=1, keepdims=True)
    gu = gu_ref[...]
    part_ref[...] = mm(gu, wo_ref[...]).astype(part_ref.dtype)
    if with_back:
        dgated = mm_nt(dh_ref[...], wo_ref[...])
        along = jnp.sum(dgated * gu.astype(F32), axis=1, keepdims=True)
        lane = lax.broadcasted_iota(jnp.int32, (SPAN, 128), 1)
        both = jnp.where(lane == 0, stats, jnp.where(lane == 1, along, 0.0))
    else:
        both = jnp.broadcast_to(stats, (SPAN, 128))
    stat_ref[...] = jnp.transpose(both)[0:8, :]


BACKWARD_STEPS = 5
AFTER, SCALE, MEAN, DTOTAL, DDELTA = 7, 10, 11, 12, 13


def backward_steps(
    step, is_last, block, length, starts_ref, dh, stat_refs, small_refs, weight_refs, wo_ref,
    saved_refs, grad_refs, sum_refs, scratch, finish,
):
    scale_ref, mean_ref = stat_refs
    kx_ref, kbc_ref, heads_ref, gain_ref = small_refs
    gate_ref, x_ref, xh_ref, bc_ref, bch_ref, dt_ref, scan_ref, state_ref = saved_refs
    dgate_ref, dx_ref, dbc_ref, gated_ref = grad_refs
    gx_ref, gbc_ref, gheads_ref = sum_refs
    (
        ext_x, ext_bc, ext_dx, ext_dbc, dmemory, columns, total_rows, squares, dgated_ref, pair_ref,
        c_flip_ref, dpair_ref, dlast_ref,
    ) = scratch
    inner = kx_ref.shape[1]

    @pl.when((step == 0) & is_last)
    def _():
        ext_dx[...] = jnp.zeros_like(ext_dx)
        ext_dbc[...] = jnp.zeros_like(ext_dbc)
        dmemory[...] = jnp.zeros_like(dmemory)
        gx_ref[...] = jnp.zeros_like(gx_ref)
        gbc_ref[...] = jnp.zeros_like(gbc_ref)
        gheads_ref[...] = jnp.zeros_like(gheads_ref)

    @pl.when((step == 0) & jnp.logical_not(is_last))
    def _():
        ext_dx[SPAN : SPAN + 8, :] = ext_dx[0:8, :]
        ext_dbc[SPAN : SPAN + 8, :] = ext_dbc[0:8, :]

    def convs(before):
        kbc = kbc_ref[...]
        return [
            taps_sum(ext_bc, low, low + STATE, before, kbc, kbc[TAPS : TAPS + 1])
            for low in (0, STATE)
        ]

    def before_rows():
        return [columns[BEFORE + lag] for lag in range(TAPS - 1)]

    @pl.when(step == 0)
    def _():
        ext_x[0:8, :] = xh_ref[8:16, :].astype(F32)
        ext_x[8 : SPAN + 8, :] = x_ref[...].astype(F32)
        ext_bc[0:8, :] = bch_ref[8:16, :].astype(F32)
        ext_bc[8 : SPAN + 8, :] = bc_ref[...].astype(F32)
        doc_col, column, before, same_square, carried, to_last = block_facts(
            starts_ref, block, length
        )
        for lag in range(1, TAPS):
            same = (doc_of(starts_ref, column + lag) == doc_col) & (column + lag < length)
            columns[AFTER + lag - 1] = same.astype(F32)
            columns[BEFORE + lag - 1] = before[lag - 1]
        row, col = lower_ones()
        squares[0] = jnp.where(same_square & (row <= col), 0.0, FAR)
        delta = softplus(dt_ref[...] + heads_ref[0:1, :])
        total = exact((row >= col).astype(F32), -jnp.exp(heads_ref[1:2, :]) * delta)
        total_rows[...] = jnp.transpose(total)
        columns[TOTAL] = total
        columns[DELTA] = delta
        columns[GROWN] = carried * jnp.exp(total)
        columns[ENDING] = to_last * jnp.exp(total[SPAN - 1 : SPAN, :] - total)
        columns[SCALE] = row_to_columns(scale_ref[0, 0:1, :])
        columns[MEAN] = row_to_columns(mean_ref[0, 0:1, :])
        columns[DTOTAL] = jnp.zeros((SPAN, 128), F32)
        columns[DDELTA] = jnp.zeros((SPAN, 128), F32)
        dlast_ref[...] = jnp.zeros_like(dlast_ref)
        b_conv, c_conv = convs(before)
        b_low = (b_conv * sigmoid(b_conv)).astype(BF16)
        c_low = (c_conv * sigmoid(c_conv)).astype(BF16)
        pair_ref[0] = b_low
        pair_ref[1] = c_low
        squares[1] = mm_nt(b_low, c_low)
        squares[2] = jnp.zeros((SPAN, SPAN), F32)
        c_flip_ref[...] = jnp.transpose(c_low.astype(F32)).astype(BF16)
        dpair_ref[...] = jnp.zeros_like(dpair_ref)
        dgated_ref[...] = mm_nt(dh[...], wo_ref[...])

    def one_tile(tile, low, high):
        width = high - low
        before = before_rows()
        after = [columns[AFTER + lag] for lag in range(TAPS - 1)]
        total, delta, grown, ending = (columns[at] for at in (TOTAL, DELTA, GROWN, ENDING))
        keep, scores = squares[0], squares[1]
        carry_last = grown[SPAN - 1 : SPAN, :]
        b_low = pair_ref[0]
        kx = kx_ref[...]
        lane = lax.broadcasted_iota(jnp.int32, (SPAN, width), 1)
        picker = (
            lax.broadcasted_iota(jnp.int32, (width, 128), 1)
            == 2 * tile + lax.broadcasted_iota(jnp.int32, (width, 128), 0) // HEAD
        ).astype(F32)
        skip = spread_pair(heads_ref[2:3, :], tile, width)
        conv = taps_sum(ext_x, low, high, before, kx, kx[TAPS : TAPS + 1])
        sig = sigmoid(conv)
        values = conv * sig
        delta_t = spread_pair(delta, tile, width)
        weighted = delta_t * values
        w_low = weighted.astype(BF16)
        scanned = scan_ref[:, low:high]
        mixed = (scanned + skip * values).astype(BF16).astype(F32)
        gate = gate_ref[:, low:high].astype(F32)
        gate_sig = sigmoid(gate)
        silu = gate * gate_sig
        scale = columns[SCALE, :, :width]
        n = mixed * silu * scale
        gain = gain_ref[0:1, low:high]
        dgated_t = dgated_ref[:, low:high]
        gated_ref[:, low:high] = (n * gain).astype(BF16)
        dg = scale * (dgated_t * gain - n * columns[MEAN, :, :width])
        dgate_ref[:, low:high] = (
            dg * mixed * (gate_sig * (1.0 + gate * (1.0 - gate_sig)))
        ).astype(BF16)
        dy_low = (dg * silu).astype(BF16)
        dy = dy_low.astype(F32)
        grad_w = None
        for half in range(width // HEAD):
            head = 2 * tile + half
            decay = jnp.exp(total_rows[head : head + 1, :] - total[:, head : head + 1] + keep)
            mine = (lane // HEAD) == half
            pairs = mm_nt(jnp.where(mine, w_low, jnp.zeros_like(w_low)), dy_low)
            squares[2] += decay * pairs
            part = mm((scores * decay).astype(BF16), dy_low)
            grad_w = part if grad_w is None else jnp.where(lane < HEAD, grad_w, part)
        dmem = dmemory[:, low:high]
        dmem_low = dmem.astype(BF16)
        mem_low = state_ref[0, :, low:high]
        ending_t = spread_pair(ending, tile, width)
        from_state = mm(b_low, dmem_low) * ending_t
        grad_w = grad_w + from_state
        dpair_ref[0] += mm_nt((weighted * ending_t).astype(BF16), dmem_low)
        dy_grown = (dy * spread_pair(grown, tile, width)).astype(BF16)
        dpair_ref[1] += mm_nt(dy_grown, mem_low)
        carry_t = spread_pair(carry_last, tile, width)
        w_round = w_low.astype(F32)
        at_last = jnp.sum(w_round * from_state, axis=0, keepdims=True) + jnp.sum(
            dmem * mem_low.astype(F32) * carry_t, axis=0, keepdims=True
        )
        dlast_ref[...] += exact(jnp.broadcast_to(at_last, (8, width)), picker)
        dmemory[:, low:high] = dmem * carry_t + mm(c_flip_ref[...], dy_grown)
        columns[DTOTAL] += exact(dy * scanned - w_round * grad_w, picker)
        columns[DDELTA] += exact(values * grad_w, picker)
        dconv = (delta_t * grad_w + skip * dy) * (sig * (1.0 + conv * (1.0 - sig)))
        ext_dx[0:SPAN, low:high] = dconv
        sums = [jnp.sum(dconv * ext_x[pl.ds(8, SPAN), low:high], axis=0, keepdims=True)]
        for lag in range(1, TAPS):
            masked = dconv * before[lag - 1][:, :width]
            sums.append(
                jnp.sum(masked * ext_x[pl.ds(8 - lag, SPAN), low:high], axis=0, keepdims=True)
            )
        sums = sums[::-1] + [
            jnp.sum(dconv, axis=0, keepdims=True),
            jnp.sum(dy * values, axis=0, keepdims=True),
            jnp.sum(dgated_t * n, axis=0, keepdims=True),
            jnp.zeros((1, width), F32),
        ]
        gx_ref[:, low:high] += jnp.concatenate(sums, axis=0)
        back = ext_dx[0:SPAN, low:high] * kx[TAPS - 1 : TAPS, low:high]
        for lag in range(1, TAPS):
            back = back + (
                ext_dx[pl.ds(lag, SPAN), low:high]
                * after[lag - 1][:, :width]
                * kx[TAPS - 1 - lag : TAPS - lag, low:high]
            )
        dx_ref[:, low:high] = back.astype(BF16)

    tiles = list(enumerate(tiles_of(inner)))
    cut = -(-len(tiles) // (BACKWARD_STEPS - 2))
    for at in range(BACKWARD_STEPS - 2):
        group = tiles[at * cut : (at + 1) * cut]
        if group:

            @pl.when(step == at + 1)
            def _():
                for tile, (low, high) in group:
                    one_tile(tile, low, high)

    @pl.when(step == BACKWARD_STEPS - 1)
    def _():
        before = before_rows()
        kbc = kbc_ref[...]
        score_grad = squares[2]
        db = dpair_ref[0] + mm(score_grad.astype(BF16), pair_ref[1])
        dc = dpair_ref[1] + mm(jnp.transpose(score_grad).astype(BF16), pair_ref[0])
        for part, (conv, grad) in enumerate(zip(convs(before), (db, dc))):
            low, high = part * STATE, (part + 1) * STATE
            sig = sigmoid(conv)
            dconv = grad * (sig * (1.0 + conv * (1.0 - sig)))
            ext_dbc[0:SPAN, low:high] = dconv
            sums = [jnp.sum(dconv * ext_bc[pl.ds(8, SPAN), low:high], axis=0, keepdims=True)]
            for lag in range(1, TAPS):
                masked = dconv * before[lag - 1]
                sums.append(
                    jnp.sum(masked * ext_bc[pl.ds(8 - lag, SPAN), low:high], axis=0, keepdims=True)
                )
            sums = sums[::-1] + [jnp.sum(dconv, axis=0, keepdims=True), jnp.zeros((3, STATE), F32)]
            gbc_ref[:, low:high] += jnp.concatenate(sums, axis=0)
            back = dconv * kbc[TAPS - 1 : TAPS, low:high]
            for lag in range(1, TAPS):
                back = back + (
                    ext_dbc[pl.ds(lag, SPAN), low:high]
                    * columns[AFTER + lag - 1]
                    * kbc[TAPS - 1 - lag : TAPS - lag, low:high]
                )
            dbc_ref[:, low:high] = back.astype(BF16)
        row, col = lower_ones()
        slope = -jnp.exp(heads_ref[1:2, :])
        rate = slope * columns[DELTA]
        drate = exact((row <= col).astype(F32), columns[DTOTAL]) + dlast_ref[0:1, :]
        ddt = (columns[DDELTA] + slope * drate) * sigmoid(dt_ref[...] + heads_ref[0:1, :])
        lane = lax.broadcasted_iota(jnp.int32, (SPAN, 128), 1)
        own_ddt = jnp.where(lane < inner // HEAD, ddt, 0.0)
        dbc_ref[:, 2 * STATE :] = own_heads(own_ddt, inner // HEAD, 1).astype(BF16)
        gheads_ref[...] += jnp.concatenate(
            [
                jnp.sum(ddt, axis=0, keepdims=True),
                jnp.sum(drate * rate, axis=0, keepdims=True),
                jnp.zeros((6, 128), F32),
            ],
            axis=0,
        )
        finish(
            mm_nt(dgate_ref[...], weight_refs[0][...])
            + mm_nt(dx_ref[...], weight_refs[1][...])
            + mm_nt(dbc_ref[...], weight_refs[2][...])
        )


def backward_scratch(inner):
    return [
        pltpu.VMEM((SPAN + 8, inner), F32),
        pltpu.VMEM((SPAN + 8, 2 * STATE), F32),
        pltpu.VMEM((SPAN + 8, inner), F32),
        pltpu.VMEM((SPAN + 8, 2 * STATE), F32),
        pltpu.VMEM((STATE, inner), F32),
        pltpu.VMEM((14, SPAN, 128), F32),
        pltpu.VMEM((128, SPAN), F32),
        pltpu.VMEM((3, SPAN, SPAN), F32),
        pltpu.VMEM((SPAN, inner), F32),
        pltpu.VMEM((2, SPAN, STATE), BF16),
        pltpu.VMEM((STATE, SPAN), BF16),
        pltpu.VMEM((2, SPAN, STATE), F32),
        pltpu.VMEM((8, 128), F32),
    ]


def plain_backward_kernel(length, starts_ref, dh_ref, scale_ref, mean_ref, *rest):
    small, wo_ref, saved, rest = rest[:4], rest[4], rest[5:13], rest[13:]
    inner = small[0].shape[1]
    *weights, rest = split_weights(inner, rest)
    *grads, rest = split_weights(inner, rest)
    gated_ref, dnormed_ref, *rest = rest
    sums, scratch = rest[:3], rest[3:]
    turn = pl.program_id(0)

    def finish(total):
        dnormed_ref[...] = total.astype(dnormed_ref.dtype)

    for step in range(BACKWARD_STEPS):
        backward_steps(
            step, turn == 0, pl.num_programs(0) - 1 - turn, length, starts_ref, dh_ref,
            (scale_ref, mean_ref), small, weights, wo_ref, saved, grads + [gated_ref], sums, scratch,
            finish,
        )


def fused_backward_kernel(sizes, whole_inner, length, outer_layer, starts_ref, dh, scale_ref, mean_ref, *rest):
    small, wo_ref, saved, rest = rest[:4], rest[4], rest[5:13], rest[13:]
    columns, normed, stream, gain, rest = *rest[:4], rest[4:]
    if outer_layer:
        outer, product, rest = rest[0], rest[1], rest[2:]
        grad, gain_out, gx, gbc, gheads, means, gathered, finals, rest = *rest[:7], rest[7:9], rest[9:]
    else:
        other_sums, rest = rest[:4], rest[4:]
        carried, rest = rest[:2], rest[2:]
        grad, smalls_out, slots, rest = *rest[:2], rest[2:4], rest[4:]
    scratch, rest = rest[:13], rest[13:]
    weight, dproj, gated, part, inbox, load_sems, rest = *rest[:6], rest[6:]
    flow_scratch, flow_finals, rest = rest[:4], rest[4:6], rest[6:]
    ranks = {axis: lax.axis_index(axis) for axis in sizes}
    core, rank, member = ranks["section"], ranks["seq"], ranks["dp"]
    count, copies = sizes["seq"], sizes["dp"]
    if outer_layer:
        spread, mean_rows, tokens, rest = *rest[:3], rest[3:]
        row_send, row_recv, out_sems, rest = *rest[:3], rest[3:]
        line_refs, rest = rest[:5], rest[5:]
        flow_sems = rest
    else:
        gx, gbc, gheads, gain_out, rest = *rest[:4], rest[4:]
        packed, theirs, dp_sum, dp_slots, z_slots, rest = *rest[:5], rest[5:]
        small_sems, rest = rest[:6], rest[6:]
        squares_0, squares_1, rest = rest[:3], rest[3:6], rest[6:]
        line_refs, flow_sems = tuple(rest[:2]) + (None,) * 3, rest[2:]
        spread = None
    turn = pl.program_id(0)
    blocks = length // SPAN
    steps = blocks * BACKWARD_STEPS
    block = blocks - 1 - lax.div(turn, BACKWARD_STEPS)
    inner = small[0].shape[1]
    parts = ((0, inner), (inner, 2 * inner), (2 * inner, 2 * inner + 3 * STATE))
    width = dh.shape[1]
    line = Line(
        count,
        rank,
        part,
        inbox,
        spread,
        line_refs,
        (lambda at: (blocks - at) * BACKWARD_STEPS) if outer_layer else (lambda at: steps),
    )
    left_in = weight.at[0:length, 0:width]
    flow = Flow(
        sizes, ranks, left_in, dproj, gated, dh, *flow_finals, flow_scratch, flow_sems
    )
    weight_load = pltpu.make_async_copy(
        columns.at[1 if outer_layer else 0], weight, load_sems.at[0]
    )
    normed_load = pltpu.make_async_copy(normed, left_in, load_sems.at[1])

    @pl.when(turn == 0)
    def _():
        greet_all(sizes, ranks)
        weight_load.start()
        gain_out[...] = jnp.zeros_like(gain_out)

    @pl.when(turn == BACKWARD_STEPS - 1)
    def _():
        weight_load.wait()

    if not outer_layer:
        square = Square(member, carried, slots, squares_1)
        for when, stage in (
            (0, square.begin),
            (steps // 2, square.middle),
            (steps - 1, square.end),
        ):

            @pl.when((turn == when) & (core == 1))
            def _():
                stage(0)
                stage(1)

    @pl.when(turn < steps)
    def _():
        rows = pl.ds(pl.multiple_of(block * SPAN, SPAN), SPAN)

        def finish(total):
            part[rows, :] = total.astype(part.dtype)

        backward_steps(
            lax.rem(turn, BACKWARD_STEPS),
            turn < BACKWARD_STEPS,
            block,
            length,
            starts_ref,
            dh.at[rows],
            (scale_ref, mean_ref),
            small,
            [weight.at[:, low:high] for low, high in parts],
            wo_ref,
            saved,
            [dproj.at[rows, low:high] for low, high in parts] + [gated.at[rows]],
            (gx, gbc, gheads),
            scratch,
            finish,
        )

    def own_piece(piece, total):
        rows = pl.ds(pl.multiple_of(piece * PIECE, PIECE), PIECE)
        back, gain_part = norm_back(stream[rows, :].astype(F32), gain[0:1, :], total)
        gain_out[0:1, :] += gain_part
        if outer_layer:
            above = outer[rows, :]
        else:
            start = pl.multiple_of(rank * SPAN + piece * PIECE, PIECE)
            above = dh[pl.ds(start, PIECE), :]
        whole_grad = above.astype(F32) + back
        grad[rows, :] = whole_grad
        if outer_layer:
            low = whole_grad.astype(BF16)
            spread[rank, rows, :] = low
            along_rows = jnp.sum(low.astype(F32) * product[rows, :], axis=1, keepdims=True)
            tokens[rows, :] = jnp.broadcast_to(along_rows / whole_inner, (PIECE, 128))

    if outer_layer:
        share = (count, rank, mean_rows.at[rank], mean_rows, row_send, row_recv)

        def after_own():
            mean_rows[rank] = jnp.transpose(tokens[...])[0:8, :]
            share_with_all(*share)

    else:
        s_core_send, s_core_recv, s_dp_send, s_dp_recv, s_z_send, s_z_recv = small_sems

        def s_core_copy():
            return push("section", 1 - core, packed, theirs, s_core_send, s_core_recv)

        def s_dp_copy(step):
            to = lax.rem(member + step, copies)
            return push(
                "dp", to, dp_sum, dp_slots.at[member], s_dp_send.at[step], s_dp_recv.at[member]
            )

        def s_z_copy(step):
            to = lax.rem(rank + step, count)
            return push(
                "seq", to, z_slots.at[rank], z_slots.at[rank], s_z_send.at[step], s_z_recv.at[rank]
            )

        def after_own():
            wide = SMALL_COLUMNS - 256
            mine = (gx, gbc, gheads, gain_out)
            packed[...] = jnp.zeros_like(packed)
            for layer, (x_sum, bc_sum, head_sum, gain_sum) in enumerate((mine, other_sums)):
                packed[layer, :, :inner] = x_sum[...]
                packed[layer, 0:5, inner:wide] = bc_sum[0:5, :]
                packed[layer, 5:7, inner : inner + 128] = head_sum[0:2, :]
                for row in range(width // 256):
                    packed[layer, row : row + 1, wide:] = gain_sum[0:1, row * 256 : (row + 1) * 256]
            s_core_copy().start()

    def serve(at, _):
        line.turn(at, own_piece, None, after_own)
        return 0

    square_here = None if outer_layer else Square(member, flow_finals, slots, squares_0)
    ready = flow.ready(2)

    def serve_both(at, _):
        line.turn(at, own_piece, None, after_own)
        flow.turn(at - steps, 2)
        for kind in range(2):

            @pl.when(at - steps == ready[kind])
            def _():
                flow.finals_here(kind, 1 if outer_layer else 0)

            if not outer_layer:

                @pl.when(at - steps == ready[kind] + 1)
                def _():
                    flow.finals_given(kind, 0)

                    @pl.when(core == 0)
                    def _():
                        square_here.begin(kind)

        return 0

    if outer_layer:

        @pl.when(turn < steps)
        def _():
            serve(turn, 0)

    @pl.when(turn == steps)
    def _():
        normed_load.start()
        normed_load.wait()
        lax.fori_loop(steps, steps + max(line.turns(), ready[1] + 2), serve_both, 0)
        if outer_layer:
            copies_out = [
                pltpu.make_async_copy(spread.at[at], gathered.at[at], out_sems.at[at])
                for at in range(count)
            ]
            for copy in copies_out:
                copy.start()
            share_wait_recv(*share)
            means[...] = mean_rows[...]
            share_wait_send(*share)
            flow.finals_given(0, 1)
            flow.finals_given(1, 1)
            for at in range(2):
                final_copy = pltpu.make_async_copy(
                    flow_finals[at], finals[at], out_sems.at[count + at]
                )
                final_copy.start()
                final_copy.wait()
            flow.settle()
            line.settle()
            for copy in copies_out:
                copy.wait()
        else:
            s_core_copy().wait_recv()
            dp_sum[...] = packed[...] + theirs[...]
            for step in range(1, copies):
                s_dp_copy(step).start()

            @pl.when(core == 0)
            def _():
                square_here.middle(0)
                square_here.middle(1)

            total = dp_sum[...]
            for step in range(1, copies):
                origin = lax.rem(member + step, copies)
                place = dp_slots.at[origin]
                push(
                    "dp", origin, place, place, s_dp_send.at[step], s_dp_recv.at[origin]
                ).wait_recv()
                total = total + dp_slots[origin]
            z_slots[rank] = total
            for step in range(1, count):
                s_z_copy(step).start()
            @pl.when(core == 0)
            def _():
                square_here.end(0)
                square_here.end(1)

            for step in range(1, count):
                origin = lax.rem(rank + step, count)
                place = z_slots.at[origin]
                push("seq", origin, place, place, s_z_send.at[step], s_z_recv.at[origin]).wait_recv()
            smalls_out[...] = z_slots[...]

            s_core_copy().wait_send()
            for step in range(1, copies):
                s_dp_copy(step).wait_send()
            for step in range(1, count):
                s_z_copy(step).wait_send()
            flow.settle()
            line.settle()


def whole(array):
    return pl.BlockSpec(array.shape, lambda i: (0,) * array.ndim, pipeline_mode=pl.Buffered(1))


def of_layer(array, layer):
    return pl.BlockSpec(
        (None,) + array.shape[1:],
        lambda i: (layer,) + (0,) * (array.ndim - 1),
        pipeline_mode=pl.Buffered(1),
    )


def cost(length, width, inner, passes):
    flops = 2 * length * width * (3 * inner + 384) * passes
    return pl.CostEstimate(flops=flops, bytes_accessed=length * width * 16, transcendentals=0)


VMEM_LIMIT = 48 * 2**20


def part_kind(length, width):
    return F32 if length * width * 4 <= 8 * 2**20 else BF16


def run_forward(starts, normed, weights, dh=None):
    columns, kx, kbc, heads, gain, wo = weights
    length, width = normed.shape
    inner = kx.shape[1]
    blocks = length // SPAN
    rows = lambda cols: pl.BlockSpec((SPAN, cols), lambda i: (i, 0))
    small = [kx, kbc, heads, gain]
    given = [wo] + list(columns)
    operands = [starts, normed] + small + [array for array, _ in given]
    in_specs = [pl.BlockSpec(memory_space=pltpu.SMEM), rows(width)]
    in_specs += [whole(array) for array in small] + [spec for _, spec in given]
    if dh is not None:
        operands.append(dh)
        in_specs.append(rows(width))
    out_shape = [
        jax.ShapeDtypeStruct((length, inner), BF16),
        jax.ShapeDtypeStruct((length, inner), BF16),
        jax.ShapeDtypeStruct((length, 2 * STATE), BF16),
        jax.ShapeDtypeStruct((length, 128), F32),
        jax.ShapeDtypeStruct((length, inner), F32),
        jax.ShapeDtypeStruct((blocks, STATE, inner), BF16),
        jax.ShapeDtypeStruct((length, width), BF16 if dh is not None else part_kind(length, width)),
        jax.ShapeDtypeStruct((8, length), F32),
    ]
    out_specs = [
        rows(inner),
        rows(inner),
        rows(2 * STATE),
        rows(128),
        rows(inner),
        pl.BlockSpec((1, STATE, inner), lambda i: (i, 0, 0)),
        rows(width),
        pl.BlockSpec((8, SPAN), lambda i: (0, i)),
    ]
    return pl.pallas_call(
        functools.partial(forward_kernel, dh is not None, length),
        grid=(blocks,),
        in_specs=in_specs,
        out_specs=out_specs,
        out_shape=out_shape,
        scratch_shapes=[
            pltpu.VMEM((SPAN + 8, inner), F32),
            pltpu.VMEM((SPAN + 8, 2 * STATE), F32),
            pltpu.VMEM((STATE, inner), F32),
            pltpu.VMEM((SPAN, inner), BF16),
        ],
        compiler_params=pltpu.CompilerParams(
            dimension_semantics=("arbitrary",), vmem_limit_bytes=BACK_VMEM
        ),
        cost_estimate=cost(length, width, inner, 1),
        name="layer_forward",
    )(*operands)


def run_backward(starts, dh, scales, means, weights, saved, fused=None):
    columns, kx, kbc, heads, gain, wo = weights
    gate, x, bc, dt, scanned, states = saved
    length, width = dh.shape
    inner = kx.shape[1]
    blocks = length // SPAN
    if fused is None:
        block = lambda i: blocks - 1 - i
    else:
        block = lambda i: blocks - 1 - jnp.minimum(lax.div(i, BACKWARD_STEPS), blocks - 1)
    rows = lambda cols: pl.BlockSpec((SPAN, cols), lambda i: (block(i), 0))
    halo = lambda cols: pl.BlockSpec(
        (16, cols), lambda i: (jnp.maximum(block(i) * (SPAN // 16) - 1, 0), 0)
    )
    fixed = lambda shape: pl.BlockSpec(shape, lambda i: (0,) * len(shape))
    stat = pl.BlockSpec((1, 8, SPAN), lambda i: (block(i), 0, 0))
    small = [kx, kbc, heads, gain]
    operands = [starts, dh, scales, means] + small + [wo[0]]
    in_specs = [pl.BlockSpec(memory_space=pltpu.SMEM), whole(dh) if fused else rows(width), stat, stat]
    in_specs += [whole(array) for array in small] + [wo[1]]
    operands += [gate, x, x, bc, bc, dt, scanned, states]
    in_specs += [
        rows(inner),
        rows(inner),
        halo(inner),
        rows(2 * STATE),
        halo(2 * STATE),
        rows(128),
        rows(inner),
        pl.BlockSpec((1, STATE, inner), lambda i: (block(i), 0, 0)),
    ]
    sums = [
        jax.ShapeDtypeStruct((8, inner), F32),
        jax.ShapeDtypeStruct((8, 2 * STATE), F32),
        jax.ShapeDtypeStruct((8, 128), F32),
    ]
    scratch = backward_scratch(inner)
    if fused is None:
        operands += [array for array, _ in columns]
        in_specs += [spec for _, spec in columns]
        widths = [2 * inner + 3 * STATE] if len(columns) == 1 else [inner, inner, 3 * STATE]
        out_shape = [jax.ShapeDtypeStruct((length, cols), BF16) for cols in widths] + [
            jax.ShapeDtypeStruct((length, inner), BF16),
            jax.ShapeDtypeStruct((length, width), part_kind(length, width)),
        ]
        out_specs = [rows(cols) for cols in widths] + [rows(inner), rows(width)]
        out_shape += sums
        out_specs += [fixed(array.shape) for array in sums]
        kernel, grid, settings = functools.partial(plain_backward_kernel, length), blocks, {}
    else:
        sizes = axis_sizes()
        count, copies = sizes["seq"], sizes["dp"]
        layer, whole_inner, normed, inputs, carried = fused
        wide = columns.shape[2]
        dma = pltpu.SemaphoreType.DMA
        operands += [columns, normed] + list(inputs) + list(carried)
        in_specs += [IN_HBM, IN_HBM] + [whole(array) for array in list(inputs) + list(carried)]
        flow_scratch, flow_sems, finals = flow_shapes(sizes, width // count, inner, width, wide)
        scratch += [
            pltpu.VMEM((width, wide), BF16),
            pltpu.VMEM((length, wide), BF16),
            pltpu.VMEM((length, inner), BF16),
            pltpu.VMEM((length, width), BF16),
            pltpu.VMEM((count + 1, SPAN, width), BF16),
            dma((2,)),
        ]
        scratch += flow_scratch + [pltpu.VMEM(f.shape, f.dtype) for f in finals]
        out_shape = [jax.ShapeDtypeStruct((SPAN, width), F32)]
        if layer:
            out_shape += [jax.ShapeDtypeStruct((8, width), F32)] + sums
            out_shape += [jax.ShapeDtypeStruct((count, 8, SPAN), F32)]
            out_specs = [fixed(array.shape) for array in out_shape]
            out_shape += [jax.ShapeDtypeStruct((count, SPAN, width), BF16)] + finals
            out_specs += [IN_HBM] * 3
            scratch += [
                pltpu.VMEM((count, SPAN, width), BF16),
                pltpu.VMEM((count, 8, SPAN), F32),
                pltpu.VMEM((SPAN, 128), F32),
                dma((count,)),
                dma((count,)),
                dma((count + 2,)),
            ]
            scratch += line_sems(count, SPAN // PIECE)
        else:
            out_shape += [jax.ShapeDtypeStruct((count, 2, 8, SMALL_COLUMNS), F32)]
            out_specs = [fixed(array.shape) for array in out_shape]
            slots = [jax.ShapeDtypeStruct((copies,) + f.shape, f.dtype) for f in finals]
            out_shape += slots
            out_specs += [IN_HBM] * 2
            scratch += [pltpu.VMEM(array.shape, F32) for array in sums] + [pltpu.VMEM((8, width), F32)]
            scratch += [pltpu.VMEM((2, 8, SMALL_COLUMNS), F32)] * 3
            scratch += [pltpu.VMEM((size, 2, 8, SMALL_COLUMNS), F32) for size in (copies, count)]
            scratch += [dma, dma, dma((copies,)), dma((copies,)), dma((count,)), dma((count,))]
            scratch += square_sems() + square_sems() + line_sems(count, SPAN // PIECE)[:2]
        scratch += flow_sems
        kernel = functools.partial(fused_backward_kernel, sizes, whole_inner, length, bool(layer))
        grid = blocks * BACKWARD_STEPS + 1
        settings = {"collective_id": 2 + layer, "has_side_effects": True}
    return pl.pallas_call(
        kernel,
        grid=(grid,),
        in_specs=in_specs,
        out_specs=out_specs,
        out_shape=out_shape,
        scratch_shapes=scratch,
        compiler_params=pltpu.CompilerParams(
            dimension_semantics=("arbitrary",), vmem_limit_bytes=BACK_VMEM, **settings
        ),
        cost_estimate=cost(length, width, inner, 2),
        name="layer_backward",
    )(*operands)


BACK_VMEM = 63 * 2**20


def norm_rows(rows_in, gain_vec):
    return (
        rows_in
        * lax.rsqrt(jnp.mean(rows_in * rows_in, axis=-1, keepdims=True) + EPSILON)
        * gain_vec
    )


def norm_back(rows_in, gain_vec, grad):
    inverse = lax.rsqrt(jnp.mean(rows_in * rows_in, axis=-1, keepdims=True) + EPSILON)
    unit = rows_in * inverse
    scaled = grad * gain_vec
    back = inverse * (scaled - unit * jnp.mean(scaled * unit, axis=-1, keepdims=True))
    return back, jnp.sum(grad * unit, axis=0, keepdims=True)


MESH = pl.DeviceIdType.MESH
PIECE = 16
HOP = 2


def along(axis, index):
    return {axis: index}


def greet(axis, count, rank):
    barrier = pltpu.get_barrier_semaphore()
    for step in range(1, count):
        pl.semaphore_signal(
            barrier, inc=1, device_id=along(axis, lax.rem(rank + step, count)), device_id_type=MESH
        )
    pl.semaphore_wait(barrier, count - 1)


def send_to(axis, index, source, target, send_sem, recv_sem):
    return pltpu.make_async_remote_copy(
        src_ref=source,
        dst_ref=target,
        send_sem=send_sem,
        recv_sem=recv_sem,
        device_id=along(axis, index),
        device_id_type=MESH,
    )


def share_with_all(count, rank, source, slots, send_sems, recv_sems):
    for step in range(1, count):
        to = lax.rem(rank + step, count)
        send_to("seq", to, source, slots.at[rank], send_sems.at[step], recv_sems.at[rank]).start()


def share_wait_recv(count, rank, source, slots, send_sems, recv_sems):
    for step in range(1, count):
        origin = lax.rem(rank + step, count)
        send_to(
            "seq", origin, source, slots.at[origin], send_sems.at[step], recv_sems.at[origin]
        ).wait_recv()


def share_wait_send(count, rank, source, slots, send_sems, recv_sems):
    for step in range(1, count):
        to = lax.rem(rank + step, count)
        send_to("seq", to, source, slots.at[rank], send_sems.at[step], recv_sems.at[rank]).wait_send()


class Line:
    def __init__(self, count, rank, part, inbox, spread, sems, born=lambda block: 0):
        self.count, self.rank = count, rank
        self.part, self.inbox, self.spread = part, inbox, spread
        self.sum_send, self.sum_recv, self.out_right, self.out_left, self.out_recv = sems
        self.born = born
        self.pieces = SPAN // PIECE

    def sum_copy(self, slot, target_slot, to, piece):
        rows = pl.ds(piece * PIECE, PIECE)
        return send_to(
            "seq",
            to,
            self.inbox.at[slot, rows],
            self.inbox.at[target_slot, rows],
            self.sum_send.at[slot, piece],
            self.sum_recv.at[target_slot, piece],
        )

    def arrived(self, slot, piece):
        self.sum_copy(slot, slot, self.rank, piece).wait_recv()

    def own_part(self, block, piece):
        start = pl.multiple_of(block * SPAN + piece * PIECE, PIECE)
        return self.part[pl.ds(start, PIECE), :].astype(F32)

    def pass_sum(self, piece, away, sign):
        count, rank = self.count, self.rank
        rows = pl.ds(pl.multiple_of(piece * PIECE, PIECE), PIECE)
        block = rank + sign * away
        first = rank == 0 if sign > 0 else rank == count - 1

        @pl.when(first)
        def _():
            self.inbox[block, rows, :] = self.own_part(block, piece).astype(BF16)

        @pl.when(jnp.logical_not(first))
        def _():
            self.arrived(block, piece)
            total = self.own_part(block, piece) + self.inbox[block, rows, :].astype(F32)
            self.inbox[block, rows, :] = total.astype(BF16)

        target = count if sign < 0 and away == 1 else block
        self.sum_copy(block, target, rank + sign, piece).start()

    def pass_sums(self, turn):
        count, rank, pieces = self.count, self.rank, self.pieces
        for away in range(count - 1, 0, -1):
            for sign in (1, -1):
                block = rank + sign * away
                inside = block < count if sign > 0 else block >= 0
                piece = turn - self.born(block) - HOP * (rank if sign > 0 else count - 1 - rank)

                @pl.when(inside & (piece >= 0) & (piece < pieces))
                def _():
                    self.pass_sum(piece, away, sign)

    def own_lag(self, block):
        return self.born(block) + HOP * jnp.maximum(block, self.count - 1 - block)

    def own_total(self, piece):
        count, rank = self.count, self.rank
        rows = pl.ds(pl.multiple_of(piece * PIECE, PIECE), PIECE)

        @pl.when(rank > 0)
        def _():
            self.arrived(rank, piece)

        @pl.when(rank < count - 1)
        def _():
            self.arrived(count, piece)

        from_left = jnp.where(rank > 0, self.inbox[rank, rows, :].astype(F32), 0.0)
        from_right = jnp.where(rank < count - 1, self.inbox[count, rows, :].astype(F32), 0.0)
        return self.own_part(rank, piece) + from_left + from_right

    def out_copy(self, block, piece, sign):
        rows = pl.ds(pl.multiple_of(piece * PIECE, PIECE), PIECE)
        sems = self.out_right if sign > 0 else self.out_left
        return send_to(
            "seq",
            self.rank + sign,
            self.spread.at[block, rows],
            self.spread.at[block, rows],
            sems.at[block, piece],
            self.out_recv.at[block, piece],
        )

    def start_out(self, block, piece, sign):
        @pl.when(self.rank < self.count - 1 if sign > 0 else self.rank > 0)
        def _():
            self.out_copy(block, piece, sign).start()

    def pass_out(self, turn, away):
        for sign in (1, -1):
            block = self.rank - sign * away
            piece = turn - self.own_lag(block) - HOP * away
            inside = block >= 0 if sign > 0 else block < self.count

            @pl.when(inside & (piece >= 0) & (piece < self.pieces))
            def _():
                self.out_copy(block, piece, sign).wait_recv()
                self.start_out(block, piece, sign)

    def turns(self):
        return self.pieces + HOP * (2 if self.spread is not None else 1) * (self.count - 1)

    def turn(self, turn, own_piece, before_own=None, after_own=None):
        self.pass_sums(turn)
        if self.spread is not None:
            for away in range(1, self.count):
                self.pass_out(turn, away)
        piece = turn - self.own_lag(self.rank)
        if before_own is not None:

            @pl.when(piece == 0)
            def _():
                before_own()

        @pl.when((piece >= 0) & (piece < self.pieces))
        def _():
            own_piece(piece, self.own_total(piece))
            if self.spread is not None:
                self.start_out(self.rank, piece, 1)
                self.start_out(self.rank, piece, -1)

        if after_own is not None:

            @pl.when(piece == self.pieces - 1)
            def _():
                after_own()

    def run(self, own_piece, before_own=None, after_own=None, flow=None, pace=2):
        turns = self.turns()
        if flow is not None:
            turns = max(turns, flow.turns(pace))

        def step(turn, _):
            self.turn(turn, own_piece, before_own, after_own)
            if flow is not None:
                flow.turn(turn, pace)
            return 0

        lax.fori_loop(0, turns, step, 0)
        self.settle()

    def settle(self):
        def body(piece, _):
            for block in range(self.count):
                right = (block > self.rank) & (self.rank < self.count - 1)
                left = (block < self.rank) & (self.rank > 0)

                @pl.when(right | left)
                def _():
                    self.sum_copy(block, block, self.rank, piece).wait_send()

                if self.spread is not None:

                    @pl.when((block <= self.rank) & (self.rank < self.count - 1))
                    def _():
                        self.out_copy(block, piece, 1).wait_send()

                    @pl.when((block >= self.rank) & (self.rank > 0))
                    def _():
                        self.out_copy(block, piece, -1).wait_send()

            return 0

        lax.fori_loop(0, self.pieces, body, 0)


def line_sems(count, pieces):
    return [
        pltpu.SemaphoreType.DMA((count + 1, pieces)),
        pltpu.SemaphoreType.DMA((count + 1, pieces)),
        pltpu.SemaphoreType.DMA((count, pieces)),
        pltpu.SemaphoreType.DMA((count, pieces)),
        pltpu.SemaphoreType.DMA((count, pieces)),
    ]


def row_to_columns(row):
    return jnp.transpose(jnp.broadcast_to(row, (128, SPAN)))


def sum_forward_kernel(
    count,
    whole_inner,
    part,
    stat,
    stream,
    gain,
    spread,
    scales,
    hidden,
    product,
    inbox,
    slots,
    columns,
    stat_send,
    stat_recv,
    *sems,
):
    rank = lax.axis_index("seq")
    greet("seq", count, rank)
    share = (count, rank, stat, slots, stat_send, stat_recv)
    share_with_all(*share)
    line = Line(count, rank, part, inbox, spread, sems)

    def before_own():
        share_wait_recv(*share)
        for block in range(count):
            lanes = slice(block * SPAN, (block + 1) * SPAN)
            total = stat[:, lanes]
            for origin in range(count):
                total = total + jnp.where(origin == rank, 0.0, slots[origin, :, lanes])
            scales[block] = lax.rsqrt(total / whole_inner + EPSILON)
        columns[...] = row_to_columns(scales[rank][0:1, :])

    def own_piece(piece, total):
        rows = pl.ds(pl.multiple_of(piece * PIECE, PIECE), PIECE)
        y = total * columns[rows, 0:1]
        low = (stream[rows, :].astype(F32) + y).astype(BF16)
        hidden[rows, :] = low
        product[rows, :] = y
        spread[rank, rows, :] = norm_rows(low.astype(F32), gain[0:1, :]).astype(BF16)

    line.run(own_piece, before_own)
    share_wait_send(*share)


def sum_plain_kernel(count, part, stream, gain, outer, grad, gain_grad, inbox, *sems):
    rank = lax.axis_index("seq")
    greet("seq", count, rank)
    line = Line(count, rank, part, inbox, None, tuple(sems) + (None,) * 3)
    gain_grad[...] = jnp.zeros_like(gain_grad)

    def own_piece(piece, total):
        rows = pl.ds(pl.multiple_of(piece * PIECE, PIECE), PIECE)
        back, gain_part = norm_back(stream[rows, :].astype(F32), gain[0:1, :], total)
        gain_grad[0:1, :] += gain_part
        grad[rows, :] = outer[rows, :].astype(F32) + back

    line.run(own_piece)


def sum_stats_kernel(count, whole_inner, stat, scales, means, slots, stat_send, stat_recv):
    rank = lax.axis_index("seq")
    greet("seq", count, rank)
    share = (count, rank, stat, slots, stat_send, stat_recv)
    share_with_all(*share)
    share_wait_recv(*share)
    for block in range(count):
        lanes = slice(block * SPAN, (block + 1) * SPAN)
        total = stat[:, lanes]
        for origin in range(count):
            total = total + jnp.where(origin == rank, 0.0, slots[origin, :, lanes])
        scale = lax.rsqrt(total[0:1, :] / whole_inner + EPSILON)
        scales[block] = jnp.broadcast_to(scale, (8, SPAN))
        means[block] = jnp.broadcast_to(total[1:2, :] * scale / whole_inner, (8, SPAN))
    share_wait_send(*share)


IN_VMEM = pl.BlockSpec(memory_space=pltpu.VMEM)


def line_call(kernel, name, collective_id, operands, out_shape, scratch):
    return pl.pallas_call(
        kernel,
        out_shape=out_shape,
        in_specs=[IN_VMEM] * len(operands),
        out_specs=[IN_VMEM] * len(out_shape),
        scratch_shapes=scratch,
        compiler_params=pltpu.CompilerParams(
            collective_id=collective_id, has_side_effects=True, vmem_limit_bytes=LINE_VMEM
        ),
        name=name,
    )(*operands)


LINE_VMEM = 60 * 2**20


def sum_forward(part, stat, stream, gain, whole_inner):
    count = lax.axis_size("seq")
    length, width = part.shape
    pieces = SPAN // PIECE
    return line_call(
        functools.partial(sum_forward_kernel, count, whole_inner),
        "sum_forward",
        1,
        [part, stat, stream, gain],
        [
            jax.ShapeDtypeStruct((count, SPAN, width), BF16),
            jax.ShapeDtypeStruct((count, 8, SPAN), F32),
            jax.ShapeDtypeStruct((SPAN, width), BF16),
            jax.ShapeDtypeStruct((SPAN, width), F32),
        ],
        [
            pltpu.VMEM((count + 1, SPAN, width), BF16),
            pltpu.VMEM((count, 8, length), F32),
            pltpu.VMEM((SPAN, 128), F32),
            pltpu.SemaphoreType.DMA((count,)),
            pltpu.SemaphoreType.DMA((count,)),
        ]
        + line_sems(count, pieces),
    )


def sum_plain(part, stream, gain, outer):
    count = lax.axis_size("seq")
    length, width = part.shape
    pieces = SPAN // PIECE
    return line_call(
        functools.partial(sum_plain_kernel, count),
        "sum_plain",
        8,
        [part, stream, gain, outer],
        [
            jax.ShapeDtypeStruct((SPAN, width), F32),
            jax.ShapeDtypeStruct((8, width), F32),
        ],
        [pltpu.VMEM((count + 1, SPAN, width), BF16)] + line_sems(count, pieces)[:2],
    )


def sum_stats(stat, whole_inner):
    count = lax.axis_size("seq")
    length = stat.shape[1]
    return line_call(
        functools.partial(sum_stats_kernel, count, whole_inner),
        "sum_stats",
        4,
        [stat],
        [
            jax.ShapeDtypeStruct((count, 8, SPAN), F32),
            jax.ShapeDtypeStruct((count, 8, SPAN), F32),
        ],
        [
            pltpu.VMEM((count, 8, length), F32),
            pltpu.SemaphoreType.DMA((count,)),
            pltpu.SemaphoreType.DMA((count,)),
        ],
    )


def other_core(array):
    return lax.ppermute(array, "section", [(0, 1), (1, 0)])


def both_layers(array):
    core = lax.axis_index("section")
    theirs = other_core(array)
    return (
        jnp.where(core == 0, array, theirs),
        jnp.where(core == 0, theirs, array),
    )


IN_HBM = pl.BlockSpec(memory_space=pl.ANY)


def greet_all(sizes, ranks):
    barrier = pltpu.get_barrier_semaphore()
    total = 0
    for axis, size in sizes.items():
        for step in range(1, size):
            to = lax.rem(ranks[axis] + step, size)
            pl.semaphore_signal(barrier, inc=1, device_id={axis: to}, device_id_type=MESH)
            total += 1
    pl.semaphore_wait(barrier, total)


def push(axis, index, source, target, send_sem, recv_sem):
    return pltpu.make_async_remote_copy(
        src_ref=source,
        dst_ref=target,
        send_sem=send_sem,
        recv_sem=recv_sem,
        device_id={axis: index},
        device_id_type=MESH,
    )


def start_kernel(
    sizes,
    small,
    hidden,
    bundle,
    out_weight,
    normed,
    columns,
    rows_out,
    smalls,
    local_sem,
    split_send,
    split_recv,
    copy_send,
    copy_recv,
    core_send,
    core_recv,
    out_send,
    out_recv,
    small_send,
    small_recv,
    small_core_send,
    small_core_recv,
    right_send,
    left_send,
    block_recv,
):
    ranks = {axis: lax.axis_index(axis) for axis in sizes}
    core, rank, stream = ranks["section"], ranks["seq"], ranks["dp"]
    count, copies = sizes["seq"], sizes["dp"]
    part = bundle.shape[1]
    depth = part * copies
    greet_all(sizes, ranks)

    smalls[core, rank] = small[...]
    for step in range(1, count):
        to = lax.rem(rank + step, count)
        place = smalls.at[core, rank]
        push("seq", to, place, place, small_send.at[step], small_recv.at[rank]).start()
    push(
        "section", 1 - core, out_weight.at[0], rows_out.at[core], out_send, out_recv
    ).start()

    def slot(origin, share):
        return pl.ds(pl.multiple_of(origin * depth + share * part, part), part)

    def split_copy(step):
        to = lax.rem(rank + step, count)
        return push(
            "seq",
            to,
            bundle.at[to],
            columns.at[core, slot(rank, stream)],
            split_send.at[step],
            split_recv.at[rank],
        )

    for step in range(count - 1, 0, -1):
        split_copy(step).start()
    own = pltpu.make_async_copy(bundle.at[rank], columns.at[core, slot(rank, stream)], local_sem)
    own.start()

    def flip(bit):
        return stream + bit - 2 * bit * lax.rem(lax.div(stream, bit), 2)

    def near_copy(origin, way, source):
        return push(
            "dp",
            flip(1 + way),
            source,
            columns.at[core, slot(origin, stream)],
            copy_send.at[origin, way],
            copy_recv.at[origin, way],
        )

    def far_copy(origin, way):
        base = origin * depth + flip(1 + way) * part + way * (part // 2)
        place = columns.at[core, pl.ds(pl.multiple_of(base, part // 2), part // 2)]
        return push(
            "dp", flip(2 - way), place, place, copy_send.at[origin, 2 + way], copy_recv.at[origin, 2 + way]
        )

    def share_copy(origin, share):
        place = columns.at[core, slot(origin, share)]
        return push(
            "section", 1 - core, place, place, core_send.at[origin, share], core_recv.at[origin, share]
        )

    def spread_slot(origin, held=None):
        place = columns.at[core, slot(origin, stream)]
        source = place if held is None else held
        for way in range(2):
            near_copy(origin, way, source).start()
        push(
            "section",
            1 - core,
            source,
            place,
            core_send.at[origin, stream],
            core_recv.at[origin, stream],
        ).start()

    spread_slot(rank, bundle.at[rank])
    rows_out[core] = out_weight[0]

    for step in range(1, count):
        origin = lax.rem(rank + step, count)
        place = smalls.at[core, origin]
        push("seq", origin, place, place, small_send.at[step], small_recv.at[origin]).wait_recv()
    push(
        "section", 1 - core, smalls.at[core], smalls.at[core], small_core_send, small_core_recv
    ).start()

    push(
        "section",
        1 - core,
        smalls.at[1 - core],
        smalls.at[1 - core],
        small_core_send,
        small_core_recv,
    ).wait_recv()
    gain = jnp.concatenate([smalls[0, origin, 5:6, :depth] for origin in range(count)], axis=1)
    normed[rank] = norm_rows(hidden[core].astype(F32), gain).astype(BF16)

    def block_copy(block, sign):
        return push(
            "seq",
            rank + sign,
            normed.at[block],
            normed.at[block],
            (right_send if sign > 0 else left_send).at[block],
            block_recv.at[block],
        )

    def open_end(sign):
        return rank < count - 1 if sign > 0 else rank > 0

    for sign in (1, -1):

        @pl.when(open_end(sign))
        def _():
            block_copy(rank, sign).start()

    for step in range(1, count):
        origin = lax.rem(rank + step, count)
        place = columns.at[core, slot(origin, stream)]
        push("seq", origin, place, place, split_send.at[step], split_recv.at[origin]).wait_recv()
        spread_slot(origin)

    for away in range(1, count):
        for sign in (1, -1):
            block = rank - sign * away

            @pl.when(block >= 0 if sign > 0 else block < count)
            def _():
                block_copy(block, sign).wait_recv()

                @pl.when(open_end(sign))
                def _():
                    block_copy(block, sign).start()

        if away == count // 2:
            for origin in range(count):
                for way in range(2):
                    near_copy(origin, way, columns.at[core, slot(origin, stream)]).wait_recv()
                    far_copy(origin, way).start()
                    share_copy(origin, flip(1 + way)).start()

    across = copies - 1 - stream
    for origin in range(count):
        for way in range(2):
            far_copy(origin, way).wait_recv()
        share_copy(origin, across).start()
    for origin in range(count):
        for share in range(copies):
            theirs = columns.at[1 - core, slot(origin, share)]
            copy = push(
                "section",
                1 - core,
                theirs,
                theirs,
                core_send.at[origin, share],
                core_recv.at[origin, share],
            )
            copy.wait_recv()
            copy.wait_send()
        for way in range(2):
            near_copy(origin, way, columns.at[core, slot(origin, stream)]).wait_send()
            far_copy(origin, way).wait_send()
    own.wait()
    rows_copy = push(
        "section", 1 - core, out_weight.at[0], rows_out.at[1 - core], out_send, out_recv
    )
    rows_copy.wait_recv()
    rows_copy.wait_send()
    push(
        "section", 1 - core, smalls.at[core], smalls.at[core], small_core_send, small_core_recv
    ).wait_send()
    for step in range(1, count):
        to = lax.rem(rank + step, count)
        place = smalls.at[core, rank]
        push("seq", to, place, place, small_send.at[step], small_recv.at[rank]).wait_send()
        split_copy(step).wait_send()
    for block in range(count):

        @pl.when((block <= rank) & (rank < count - 1))
        def _():
            block_copy(block, 1).wait_send()

        @pl.when((block >= rank) & (rank > 0))
        def _():
            block_copy(block, -1).wait_send()


def axis_sizes():
    return {axis: lax.axis_size(axis) for axis in ("section", "seq", "dp")}


def start(small, hidden, bundle, out_weight):
    sizes = axis_sizes()
    count, copies = sizes["seq"], sizes["dp"]
    depth, inner, width = bundle.shape[1] * copies, out_weight.shape[1], out_weight.shape[2]
    dma = pltpu.SemaphoreType.DMA
    return pl.pallas_call(
        functools.partial(start_kernel, sizes),
        out_shape=[
            jax.ShapeDtypeStruct((count,) + hidden.shape[1:], BF16),
            jax.ShapeDtypeStruct((2, count * depth, 2 * inner + 3 * STATE), BF16),
            jax.ShapeDtypeStruct((2, inner, width), BF16),
            jax.ShapeDtypeStruct((2, count) + small.shape, F32),
        ],
        in_specs=[IN_VMEM, IN_VMEM, IN_HBM, IN_VMEM],
        out_specs=[IN_VMEM, IN_HBM, IN_VMEM, IN_VMEM],
        scratch_shapes=[
            dma,
            dma((count,)),
            dma((count,)),
            dma((count, copies)),
            dma((count, copies)),
            dma((count, copies)),
            dma((count, copies)),
            dma,
            dma,
            dma((count,)),
            dma((count,)),
            dma,
            dma,
            dma((count,)),
            dma((count,)),
            dma((count,)),
        ],
        compiler_params=pltpu.CompilerParams(
            collective_id=5, has_side_effects=True, vmem_limit_bytes=LINE_VMEM
        ),
        name="start",
    )(small, hidden, bundle, out_weight)


def small_rows(conv_weight, conv_bias, norm_gain):
    part = conv_bias.shape[1]
    pad = -part % 128
    rows = jnp.concatenate([conv_weight[0], conv_bias], axis=0).astype(F32)
    rows = jnp.pad(rows, ((0, 0), (0, pad)))
    gain = jnp.pad(norm_gain.astype(F32), ((0, 0), (0, part + pad - norm_gain.shape[1])))
    return jnp.concatenate([rows, gain, jnp.zeros((2, part + pad), F32)], axis=0)


def step_columns(rows, whole_inner):
    rows = rows[:, 2 * whole_inner :]
    return jnp.pad(rows, ((0, 0), (0, 3 * STATE - rows.shape[1])))


def layer_facts(smalls, step_bias, decay_log, skip_gain, gate_gain, part, depth):
    count = lax.axis_size("seq")
    rank = lax.axis_index("seq")
    inner = gate_gain.shape[1]
    heads = step_bias.shape[1]
    own = jnp.concatenate([step_bias, decay_log, skip_gain], axis=0)
    own = jnp.pad(own, ((0, 5), (0, 128 - heads)))
    own = both_layers(own.astype(F32))
    gate = both_layers(jnp.broadcast_to(gate_gain, (8, inner)).astype(F32))
    facts = []
    for layer in range(2):
        rows = smalls[layer]
        taps = rows[:, :, :part].transpose(1, 0, 2).reshape(8, count * part)
        gain = jnp.broadcast_to(rows[:, 5, :depth].reshape(1, -1), (8, count * depth))
        facts.append(
            (
                lax.dynamic_slice_in_dim(taps, rank * inner, inner, 1),
                taps[:, count * inner :],
                own[layer],
                gate[layer],
                gain,
            )
        )
    return facts


def column_bundle(in_weight, inner):
    count, copies = lax.axis_size("seq"), lax.axis_size("dp")
    part = in_weight.shape[1] // copies
    rows = lax.dynamic_slice_in_dim(in_weight[0], lax.axis_index("dp") * part, part, 0)
    kinds = [
        rows[:, kind * count * inner : (kind + 1) * count * inner]
        .reshape(part, count, inner)
        .transpose(1, 0, 2)
        for kind in range(2)
    ]
    rest = step_columns(rows, count * inner)
    kinds.append(jnp.broadcast_to(rest[None], (count,) + rest.shape))
    return jnp.concatenate(kinds, axis=2)


def columns_by_collectives(in_weight, inner):
    count = lax.axis_size("seq")
    depth = in_weight.shape[1]
    rows = in_weight[0]
    kinds = []
    for kind in range(2):
        part = rows[:, kind * count * inner : (kind + 1) * count * inner]
        part = part.reshape(depth, count, inner).transpose(1, 0, 2)
        part = lax.all_to_all(part, "seq", split_axis=0, concat_axis=0, tiled=True)
        kinds.append(both_layers(part.reshape(count * depth, inner)))
    step_weight = step_columns(rows, count * inner)
    kinds.append(both_layers(lax.all_gather(step_weight, "seq", axis=0, tiled=True)))
    return [[(kind[layer], whole(kind[layer])) for kind in kinds] for layer in range(2)]


class Flow:
    def __init__(self, sizes, ranks, left_in, right_in, left_out, right_out, final, out_final, scratch, sems):
        self.left_in, self.right_in, self.left_out, self.right_out = (
            left_in,
            right_in,
            left_out,
            right_out,
        )
        self.final, self.out_final = final, out_final
        self.give, self.got, self.parts, self.sums = scratch
        (
            self.core_send,
            self.core_recv,
            self.part_send,
            self.part_recv,
            self.z_send,
            self.z_recv,
            self.give_send,
            self.give_recv,
        ) = sems
        self.count, self.copies = sizes["seq"], sizes["dp"]
        self.core, self.rank, self.stream = ranks["section"], ranks["seq"], ranks["dp"]
        self.units, half, self.depth = self.got.shape
        self.halves = (half, left_out.shape[1])

    def multiply(self, unit, kind, core, keep):
        depth = self.depth
        if kind == 0:
            strip = self.halves[0] // 2
            base = core * (self.right_in.shape[1] - self.halves[0])
            source, right = self.right_in, self.left_in
            block = unit
        else:
            strip = self.halves[1] // 2
            base = 0
            source, right = self.left_out, self.right_out
            block = 2 * (unit - self.count) + core
        right = right[:, pl.ds(pl.multiple_of(block * depth, depth), depth)]

        def body(index, _):
            low = pl.multiple_of(base + index * strip, 128)
            keep(pl.ds(pl.multiple_of(index * strip, strip), strip), mm_tn(source[:, pl.ds(low, strip)], right))
            return 0

        lax.fori_loop(0, 2, body, 0)

    def core_copy(self, unit, kind):
        rows = pl.ds(0, self.halves[kind])
        return push(
            "section",
            1 - self.core,
            self.give.at[unit, rows],
            self.got.at[unit, rows],
            self.core_send.at[unit],
            self.core_recv.at[unit],
        )

    def part_rows(self, member, kind):
        share = self.halves[kind] // self.copies
        return pl.ds(pl.multiple_of(member * share, share), share)

    def bits(self, unit):
        first = 1 + lax.rem(unit, 2)
        return first, 3 - first

    def flip(self, bit):
        low = lax.rem(lax.div(self.stream, bit), 2)
        return self.stream + bit - 2 * bit * low

    def step_copy(self, unit, step, kind):
        first, second = self.bits(unit)
        partner, opposite = self.flip(first), self.flip(second)
        member = (partner, partner + opposite - self.stream, opposite)[step]
        return push(
            "dp",
            opposite if step == 2 else partner,
            self.got.at[unit, self.part_rows(member, kind)],
            self.parts.at[unit, step, pl.ds(0, self.halves[kind] // self.copies)],
            self.part_send.at[unit, step],
            self.part_recv.at[unit, step],
        )

    def z_copy(self, unit):
        return push(
            "seq",
            unit,
            self.sums.at[unit],
            self.final.at[self.core, self.rank],
            self.z_send.at[unit],
            self.z_recv.at[self.rank],
        )

    def first(self, unit, kind):
        def keep(rows, value):
            self.give[unit, rows, :] = value.astype(BF16)

        self.multiply(unit, kind, 1 - self.core, keep)
        self.core_copy(unit, kind).start()

    def second(self, unit, kind):
        self.core_copy(unit, kind).wait_recv()

        def keep(rows, value):
            self.got[unit, rows, :] = (value + self.got[unit, rows, :].astype(F32)).astype(BF16)

        self.multiply(unit, kind, self.core, keep)
        self.step_copy(unit, 0, kind).start()
        self.step_copy(unit, 1, kind).start()

    def add_part(self, unit, step, member, kind):
        self.step_copy(unit, step, kind).wait_recv()
        total = self.got[unit, self.part_rows(member, kind), :].astype(F32)
        part = self.parts[unit, step, : self.halves[kind] // self.copies, :]
        return (total + part.astype(F32)).astype(BF16)

    def third(self, unit, kind):
        opposite = self.flip(self.bits(unit)[1])
        self.got[unit, self.part_rows(opposite, kind), :] = self.add_part(unit, 1, opposite, kind)
        self.step_copy(unit, 2, kind).start()
        self.got[unit, self.part_rows(self.stream, kind), :] = self.add_part(
            unit, 0, self.stream, kind
        )

    def fourth(self, unit, kind):
        total = self.add_part(unit, 2, self.stream, kind)
        if kind:
            self.out_final[self.core, unit - self.count] = total
        else:

            @pl.when(unit == self.rank)
            def _():
                self.final[self.core, self.rank] = total

            @pl.when(unit != self.rank)
            def _():
                self.sums[unit] = total
                self.z_copy(unit).start()

    LAGS = (0, 1, 5, 9)

    def turn(self, turn, pace):
        for stage, lag in zip((self.first, self.second, self.third, self.fourth), self.LAGS):
            at = turn - lag

            for kind, (low, high) in enumerate(((0, self.count), (self.count, self.units))):

                @pl.when((at >= low * pace) & (at < high * pace) & (lax.rem(at, pace) == 0))
                def _():
                    stage(lax.div(at, pace), kind)

    def turns(self, pace):
        return (self.units - 1) * pace + self.LAGS[3] + 1

    def ready(self, pace):
        last = self.LAGS[3]
        return (self.count - 1) * pace + last + 2, (self.units - 1) * pace + last + 1

    def finals_here(self, kind, layer):
        if kind == 0:
            for step in range(1, self.count):
                origin = lax.rem(self.rank + step, self.count)
                place = self.final.at[self.core, origin]
                push(
                    "seq", origin, place, place, self.z_send.at[origin], self.z_recv.at[origin]
                ).wait_recv()

        @pl.when(self.core != layer)
        def _():
            self.give_copy(kind).start()

    def give_copy(self, kind):
        final = (self.final, self.out_final)[kind]
        place = final.at[self.core]
        return push(
            "section", 1 - self.core, place, place, self.give_send.at[kind], self.give_recv.at[kind]
        )

    def finals_given(self, kind, layer):
        final = (self.final, self.out_final)[kind]

        @pl.when(self.core == layer)
        def _():
            place = final.at[1 - self.core]
            push(
                "section", 1 - self.core, place, place, self.give_send.at[kind], self.give_recv.at[kind]
            ).wait_recv()

        @pl.when(self.core != layer)
        def _():
            self.give_copy(kind).wait_send()

    def settle(self):
        for kind, (low, high) in enumerate(((0, self.count), (self.count, self.units))):

            def body(unit, _):
                self.core_copy(unit, kind).wait_send()
                for step in range(3):
                    self.step_copy(unit, step, kind).wait_send()
                if kind == 0:

                    @pl.when(unit != self.rank)
                    def _():
                        self.z_copy(unit).wait_send()

                return 0

            lax.fori_loop(low, high, body, 0)


class Square:
    def __init__(self, member, sources, slots, sems):
        self.member, self.sources, self.slots = member, sources, slots
        self.own_sem, self.send, self.recv = sems

    def flip(self, bit):
        return self.member + bit - 2 * bit * lax.rem(lax.div(self.member, bit), 2)

    def own_copy(self, kind):
        return pltpu.make_async_copy(
            self.sources[kind], self.slots[kind].at[self.member], self.own_sem.at[kind]
        )

    def near_copy(self, kind, way):
        return push(
            "dp",
            self.flip(1 + way),
            self.sources[kind],
            self.slots[kind].at[self.member],
            self.send.at[kind, way],
            self.recv.at[kind, way],
        )

    def far_copy(self, kind, way):
        place = self.slots[kind].at[self.flip(1 + way), way]
        return push(
            "dp", self.flip(2 - way), place, place, self.send.at[kind, 2 + way], self.recv.at[kind, 2 + way]
        )

    def begin(self, kind):
        self.own_copy(kind).start()
        for way in range(2):
            self.near_copy(kind, way).start()

    def middle(self, kind):
        for way in range(2):
            self.near_copy(kind, way).wait_recv()
            self.far_copy(kind, way).start()

    def end(self, kind):
        for way in range(2):
            self.far_copy(kind, way).wait_recv()
        for way in range(2):
            self.near_copy(kind, way).wait_send()
            self.far_copy(kind, way).wait_send()
        self.own_copy(kind).wait()


def square_sems():
    dma = pltpu.SemaphoreType.DMA
    return [dma((2,)), dma((2, 4)), dma((2, 4))]


def flow_shapes(sizes, depth, inner, width, wide):
    count, copies = sizes["seq"], sizes["dp"]
    units = count + width // depth // 2
    half = -(-wide // 1024) * 512
    dma = pltpu.SemaphoreType.DMA
    scratch = [
        pltpu.VMEM((units, half, depth), BF16),
        pltpu.VMEM((units, half, depth), BF16),
        pltpu.VMEM((units, 3, half // copies, depth), BF16),
        pltpu.VMEM((count, half // copies, depth), BF16),
    ]
    sems = [
        dma((units,)),
        dma((units,)),
        dma((units, 3)),
        dma((units, 3)),
        dma((sizes["seq"],)),
        dma((sizes["seq"],)),
        dma((2,)),
        dma((2,)),
    ]
    finals = [
        jax.ShapeDtypeStruct((2, count, half // copies, depth), BF16),
        jax.ShapeDtypeStruct((2, units - count, inner // copies, depth), BF16),
    ]
    return scratch, sems, finals


def sum_backward_kernel(
    sizes,
    with_flow,
    whole_inner,
    part,
    stream,
    gain,
    outer,
    product,
    *rest,
):
    ranks = {axis: lax.axis_index(axis) for axis in sizes}
    rank, count = ranks["seq"], sizes["seq"]
    if with_flow:
        factors, rest = rest[:4], rest[4:]
        finals, rest = rest[4:6], rest[:4] + rest[6:]
    spread, means, grad, gain_grad, inbox, columns, *rest = rest
    if with_flow:
        scratch, rest = rest[:4], rest[4:]
    row_send, row_recv, *sems = rest
    greet_all(sizes if with_flow else {"seq": count}, ranks)
    line = Line(count, rank, part, inbox, spread, sems[:5])
    flow = None
    if with_flow:
        flow = Flow(sizes, ranks, *factors, *finals, scratch, sems[5:])
    gain_grad[...] = jnp.zeros_like(gain_grad)
    share = (count, rank, means.at[rank], means, row_send, row_recv)

    def own_piece(piece, total):
        rows = pl.ds(pl.multiple_of(piece * PIECE, PIECE), PIECE)
        back, gain_part = norm_back(stream[rows, :].astype(F32), gain[0:1, :], total)
        gain_grad[0:1, :] += gain_part
        whole = outer[rows, :].astype(F32) + back
        grad[rows, :] = whole
        low = whole.astype(BF16)
        spread[rank, rows, :] = low
        along_rows = jnp.sum(low.astype(F32) * product[rows, :], axis=1, keepdims=True)
        columns[rows, :] = jnp.broadcast_to(along_rows / whole_inner, (PIECE, 128))

    def after_own():
        means[rank] = jnp.transpose(columns[...])[0:8, :]
        share_with_all(*share)

    line.run(own_piece, None, after_own, flow)
    if with_flow:
        flow.finals_here(1)
    share_wait_recv(*share)
    share_wait_send(*share)
    if with_flow:
        flow.finals_given(1)
        flow.settle()


def sum_backward(part, stream, gain, outer, product, whole_inner, grads_of):
    sizes = axis_sizes()
    count = sizes["seq"]
    length, width = part.shape
    pieces = SPAN // PIECE
    factors, scratch, sems, finals = [], [], [], []
    if grads_of is not None:
        factors = list(grads_of)
        scratch, sems, finals = flow_shapes(
            sizes, width // count, factors[2].shape[1], width, factors[1].shape[1]
        )
    return line_call(
        functools.partial(sum_backward_kernel, sizes, grads_of is not None, whole_inner),
        "sum_backward",
        7,
        [part, stream, gain, outer, product] + factors,
        [
            jax.ShapeDtypeStruct((count, SPAN, width), BF16),
            jax.ShapeDtypeStruct((count, 8, SPAN), F32),
            jax.ShapeDtypeStruct((SPAN, width), F32),
            jax.ShapeDtypeStruct((8, width), F32),
        ]
        + finals,
        [
            pltpu.VMEM((count + 1, SPAN, width), BF16),
            pltpu.VMEM((SPAN, 128), F32),
        ]
        + scratch
        + [pltpu.SemaphoreType.DMA((count,)), pltpu.SemaphoreType.DMA((count,))]
        + line_sems(count, pieces)
        + sems,
    )


SMALL_COLUMNS = 1280


def unpack_kernel(inner, halves, result, held, rest, sems):
    origin = pl.program_id(0)
    count = pl.num_programs(0)
    copies, _, _, share, depth = halves.shape
    bounds = ((0, inner), (inner, 2 * inner), (2 * inner, 2 * inner + 3 * STATE))

    @pl.when(origin == 0)
    def _():
        rest[...] = jnp.zeros_like(rest)

    for core in range(2):
        for member in range(copies):
            rows = halves[member, core, 0].astype(F32)
            half = copies * share
            start = core * (bounds[2][1] - half) + member * share
            for kind, (low, high) in enumerate(bounds):
                top, end = max(start, low, core * half), min(start + share, high)
                if top < end:
                    piece = rows[top - start : end - start]
                    if kind < 2:
                        held[origin, kind, top - low : end - low, :] = piece
                    else:
                        rest[top - low : end - low, :] += piece

    def copy(at, kind):
        low = pl.multiple_of((kind * count + at) * inner, 8)
        return pltpu.make_async_copy(
            held.at[at, kind], result.at[pl.ds(low, inner)], sems.at[at, kind]
        )

    for kind in range(2):
        copy(origin, kind).start()

    @pl.when(origin == count - 1)
    def _():
        low = 2 * held.shape[0] * inner
        left = result.shape[0] - low
        tail = pltpu.make_async_copy(
            rest.at[pl.ds(0, left)], result.at[pl.ds(low, left)], sems.at[held.shape[0], 0]
        )
        tail.start()
        for at in range(held.shape[0]):
            for kind in range(2):
                copy(at, kind).wait()
        tail.wait()


def unpack(halves, inner, width):
    copies, _, count, share, depth = halves.shape
    block = pl.BlockSpec((copies, 2, 1, share, depth), lambda origin: (0, 0, origin, 0, 0))
    return pl.pallas_call(
        functools.partial(unpack_kernel, inner),
        grid=(count,),
        in_specs=[block],
        out_specs=IN_HBM,
        out_shape=jax.ShapeDtypeStruct((width, depth), F32),
        scratch_shapes=[
            pltpu.VMEM((count, 2, inner, depth), F32),
            pltpu.VMEM((3 * STATE, depth), F32),
            pltpu.SemaphoreType.DMA((count + 1, 2)),
        ],
        compiler_params=pltpu.CompilerParams(vmem_limit_bytes=VMEM_LIMIT),
        name="unpack",
    )(halves).T


def unpack_rows_kernel(halves, result):
    _, cores, blocks, _, depth = halves.shape
    for core in range(cores):
        for block in range(blocks):
            low = (block * cores + core) * depth
            result[:, low : low + depth] = halves[0, core, block].astype(F32)


def unpack_rows(halves):
    copies, cores, blocks, share, depth = halves.shape
    piece = pl.BlockSpec((1,) + halves.shape[1:], lambda member: (member, 0, 0, 0, 0))
    width = cores * blocks * depth
    return pl.pallas_call(
        unpack_rows_kernel,
        grid=(copies,),
        in_specs=[piece],
        out_specs=pl.BlockSpec((share, width), lambda member: (member, 0)),
        out_shape=jax.ShapeDtypeStruct((copies * share, width), F32),
        compiler_params=pltpu.CompilerParams(vmem_limit_bytes=VMEM_LIMIT),
        name="unpack_rows",
    )(halves)


def grads_by_collectives(in_parts, out_part, inner):
    core = lax.axis_index("section")
    count = lax.axis_size("seq")

    def to_core(pair):
        theirs = other_core(jnp.where(core == 0, pair[1], pair[0]).astype(BF16))
        return (jnp.where(core == 0, pair[0], pair[1]) + theirs.astype(F32)).astype(BF16)

    gate, x, rest = (to_core(pair) for pair in in_parts)
    out = to_core(out_part)
    depth = gate.shape[0] // count

    def rows_of(part):
        part = part.reshape(count, depth, -1)
        part = lax.all_to_all(part, "seq", split_axis=0, concat_axis=0, tiled=True)
        return lax.psum(part, "dp").astype(F32)

    gate, x, rest = rows_of(gate), rows_of(x), rows_of(rest)
    columns = [part.transpose(1, 0, 2).reshape(depth, -1) for part in (gate, x)]
    return jnp.concatenate(columns + [jnp.sum(rest, axis=0)], axis=1), lax.psum(out, "dp").astype(F32)


def local(
    hidden_in,
    doc_starts,
    cotangent,
    norm_gain,
    in_weight,
    conv_weight,
    conv_bias,
    step_bias,
    decay_log,
    skip_gain,
    gate_gain,
    out_weight,
):
    sizes = axis_sizes()
    core = lax.axis_index("section")
    rank = lax.axis_index("seq")
    count, copies = sizes["seq"], sizes["dp"]
    inner = out_weight.shape[1]
    heads = step_bias.shape[1]
    whole_inner = inner * count
    depth = in_weight.shape[1]
    part = conv_bias.shape[1]
    tokens = hidden_in.shape[1]
    regular = inner % depth == 0 and depth % 128 == 0 and copies == 4 and count % 2 == 0

    gather = lambda array: lax.all_gather(array, "seq", axis=0, tiled=True)
    stream = lax.dynamic_index_in_dim(hidden_in, core, 0, keepdims=False)
    outer = lax.dynamic_index_in_dim(cotangent, core, 0, keepdims=False)
    starts = lax.dynamic_index_in_dim(doc_starts, core, 0, keepdims=False)
    small = small_rows(conv_weight, conv_bias, norm_gain)
    if regular:
        normed_0, columns, out_rows, smalls = start(
            small, hidden_in, column_bundle(in_weight, inner), out_weight
        )
        normed_0 = normed_0.reshape(count * tokens, -1)
        both_columns = columns
        columns = [[(columns, of_layer(columns, layer))] for layer in range(2)]
        out_rows = [(out_rows, of_layer(out_rows, layer)) for layer in range(2)]
    else:
        smalls = lax.all_gather(lax.all_gather(small, "seq", axis=0), "section", axis=0)
        columns = columns_by_collectives(in_weight, inner)
        out_rows = [(array, whole(array)) for array in both_layers(out_weight[0])]
    facts = layer_facts(smalls, step_bias, decay_log, skip_gain, gate_gain, part, depth)
    gains = [fact[4] for fact in facts]
    if not regular:
        normed_0 = gather(norm_rows(stream.astype(F32), gains[0][0:1]).astype(BF16))
    layers = [(columns[layer],) + facts[layer][:4] + (out_rows[layer],) for layer in range(2)]
    if regular:
        fused_layers = [(both_columns,) + layers[layer][1:] for layer in range(2)]

    outer_after, normed_0 = lax.optimization_barrier((outer, normed_0))
    dh_whole = gather(outer_after)
    fwd_0 = run_forward(starts, normed_0, layers[0])
    normed_1, scales_0, hidden_1, product_0 = sum_forward(
        fwd_0[6], fwd_0[7], stream, gains[1], whole_inner
    )
    normed_1 = normed_1.reshape(normed_0.shape)
    fwd_1 = run_forward(starts, normed_1, layers[1], dh_whole)
    scales_1, means_1 = sum_stats(fwd_1[7], whole_inner)

    if regular:
        inputs = (hidden_1, gains[1], outer, product_0)
        fused_1 = (1, whole_inner, normed_1, inputs, ())
        input_grad_1, gain_grad_1, *sums_1 = run_backward(
            starts, dh_whole, scales_1, means_1, fused_layers[1], fwd_1[:6], fused_1
        )
        *sums_1, means_0, dh_0, final_1, out_final_1 = sums_1
    else:
        back_1 = run_backward(starts, dh_whole, scales_1, means_1, layers[1], fwd_1[:6])
        kinds = len(columns[0])
        gated_1, dnormed_1 = back_1[kinds : kinds + 2]
        dh_0, means_0, input_grad_1, gain_grad_1 = sum_backward(
            dnormed_1, hidden_1, gains[1], outer, product_0, whole_inner, None
        )
    part_1, dh_0 = lax.optimization_barrier((fwd_1[6], dh_0))
    product_1 = lax.psum_scatter(part_1, "seq", scatter_dimension=0, tiled=True)
    own_scale = lax.dynamic_index_in_dim(scales_1, rank, 0, keepdims=False)[0]
    hidden_2 = (hidden_1.astype(F32) + product_1.astype(F32) * own_scale[:, None]).astype(BF16)
    dh_0 = dh_0.reshape(dh_whole.shape)
    if regular:
        inputs = (stream, gains[0], *sums_1, gain_grad_1)
        input_grad_0, smalls, halves, halves_out = run_backward(
            starts, dh_0, scales_0, means_0, fused_layers[0], fwd_0[:6],
            (0, whole_inner, normed_0, inputs, (final_1, out_final_1)),
        )
        grad_in = unpack(halves, inner, in_weight.shape[2])
        grad_out = unpack_rows(halves_out)
    else:
        back_0 = run_backward(starts, dh_0, scales_0, means_0, layers[0], fwd_0[:6])
        gated_0, dnormed_0 = back_0[kinds : kinds + 2]
        own_dh_0 = lax.dynamic_slice_in_dim(dh_0, rank * tokens, tokens, 0)
        input_grad_0, gain_grad_0 = sum_plain(dnormed_0, stream, gains[0], own_dh_0)

        def packed(back):
            gx, gbc, gheads = back[kinds + 2 : kinds + 5]
            rest = jnp.pad(gheads[:2], ((0, 0), (0, 128)))
            rest = jnp.concatenate([gbc[:5], rest, gbc[7:]], axis=0)
            return jnp.concatenate([gx, rest, jnp.zeros((8, 256), F32)], axis=1)

        small_grads = jnp.stack([packed(back_0), packed(back_1)])
        pairs = [
            (mm_tn(normed_0, back_0[kind]), mm_tn(normed_1, back_1[kind])) for kind in range(kinds)
        ]
        grad_in, grad_out = grads_by_collectives(
            pairs, (mm_tn(gated_0, dh_0), mm_tn(gated_1, dh_whole)), inner
        )
        gain_rows = jnp.stack([gain_grad_0[0], gain_grad_1[0]]).reshape(2, -1, 256)
        small_grads = small_grads.at[:, : gain_rows.shape[1], inner + 256 :].set(gain_rows)
        smalls = lax.all_gather(lax.psum(small_grads, ("section", "dp")), "seq", axis=0)
    grad_in = grad_in[:, : in_weight.shape[2]]

    mine = lax.dynamic_index_in_dim(smalls, core, 1, keepdims=False)
    x_part = mine[:, :5, :inner].transpose(1, 0, 2).reshape(5, whole_inner)
    bc_part = jnp.sum(mine[:, :5, inner : inner + 256], axis=0)
    channels = lax.dynamic_slice_in_dim(
        jnp.concatenate([x_part, bc_part], axis=1), rank * part, part, 1
    )
    gain_rows = norm_gain.shape[1] * count // 256
    norm_grad = jnp.sum(mine[:, :gain_rows, inner + 256 :], axis=0).reshape(-1)
    norm_grad = lax.dynamic_slice_in_dim(norm_grad, rank * norm_gain.shape[1], norm_gain.shape[1], 0)
    own = lax.dynamic_index_in_dim(mine, rank, 0, keepdims=False)

    def by_layer(first, second):
        kept = jnp.where(core == 0, first, second)
        theirs = other_core(jnp.where(core == 0, second, first))
        return jnp.stack([jnp.where(core == 0, kept, theirs), jnp.where(core == 0, theirs, kept)])

    return (
        by_layer(hidden_1, hidden_2)[None],
        by_layer(input_grad_0, input_grad_1)[None],
        norm_grad[None],
        grad_in[None],
        channels[None, :TAPS],
        channels[TAPS:],
        own[5:6, inner : inner + heads],
        own[6:7, inner : inner + heads],
        jnp.sum(own[5, :inner].reshape(1, heads, HEAD), axis=2),
        own[6:7, :inner],
        grad_out[None],
    )


def solution(mesh):
    return jax.shard_map(
        local,
        mesh=mesh,
        in_specs=(
            P("dp", "seq", None),
            P("dp", None),
            P("dp", "seq", None),
            P("section", "seq"),
            P("section", "seq", None),
            P("section", None, "seq"),
            P("section", "seq"),
            P("section", "seq"),
            P("section", "seq"),
            P("section", "seq"),
            P("section", "seq"),
            P("section", "seq", None),
        ),
        out_specs=(
            P("section", "dp", "seq", None),
            P("section", "dp", "seq", None),
            P("section", "seq"),
            P("section", "seq", None),
            P("section", None, "seq"),
            P("section", "seq"),
            P("section", "seq"),
            P("section", "seq"),
            P("section", "seq"),
            P("section", "seq"),
            P("section", "seq", None),
        ),
        check_vma=False,
    )
```
